32 devices in a mesh: seq: 8 (over z, y), head: 4 (over x, core).
Axes of the slice: x: 2, y: 2, z: 4, core: 2. Of those that a mesh axis runs over, the one named last changes fastest.
Arguments:
- tokens: bfloat16 [1024, 2048], P('seq', 'head'), as said below
- w_query: bfloat16 [2048, 1024], P(None, 'head'), may hold values from -0.125 to 0.125
- w_key: bfloat16 [2048, 1024], P(None, 'head')
- w_value: bfloat16 [2048, 1024], P(None, 'head'), may hold values from -0.125 to 0.125
- gate_codes: int32 [1024, 8], P('seq', 'head'), may hold values from 455 to 1572854, as said below
- beta_codes: int32 [1024, 8], P('seq', 'head'), may hold values from 32 to 256
- norm_gain: float32 [128], replicated, may hold values from 0.25 to 1.75
- w_out: bfloat16 [1024, 2048], P('head'), may hold values from -0.1875 to 0.1875
Outputs:
- mixed: bfloat16 [1024, 2048], P('seq', 'head')
The draws below stay inside these ranges and needn't reach their ends.
Inputs may be any that keep to these rules, and one draw needn't show every extreme that they name: `gate_codes`: codes are positive; the sweep's gates are those of one recording, identical law in every draw. `tokens`: activations of order one to ten.
All inputs are finite; a program needn't handle non-finite values.
Results may differ from the reference program's by a relative error of at most 0.0049.
Values may be sent and summed in bfloat16 or wider, within the bound.
No kernel may reach another device: no remote copies, remote signals or barrier semaphores. Data moves between devices by JAX's collectives and lax.ppermute only.
A program may use at most 128 MiB of HBM per device.

```python
import math
import jax
import jax.numpy as jnp
from jax import lax

D = 2048
H = 8
HEAD_DIM = 128
SPAN = 64
TOK_DEV = 128
TOKENS = 1024


def draw_tokens(key, part):
    first, second = jax.random.split(key, 2)
    scales = jnp.exp(jax.random.uniform(second, (TOKENS, 1), jnp.float32, 0.0, math.log(10.0))) / 3.0
    starting_quantity = jax.random.normal(first, (TOKENS, D), jnp.float32)
    return (starting_quantity * scales).astype(jnp.bfloat16)


def draw_w_key(key, part):
    first, second = jax.random.split(key, 2)
    exponents = jax.random.uniform(second, (1, H * HEAD_DIM), jnp.float32, 0.0, 0.3)
    column_scales = jnp.exp(-exponents * math.log(10.0))
    starting_quantity = jax.random.normal(first, (D, H * HEAD_DIM), jnp.float32)
    return (starting_quantity * column_scales / math.sqrt(D)).astype(jnp.bfloat16)


def draw_gate_codes(key, part):
    keys = jax.random.split(key, 6)
    order = jax.random.permutation(keys[0], H)
    fast = order < max(1, H // 4)
    starting_quantity = jnp.where(fast, 2 ** 21 // 200, max(1, 2 ** 22 // (9 * TOKENS))).astype(jnp.int32)
    segment_scaling_factor = jax.random.randint(keys[1], (TOKENS // SPAN, 1, H), 1, 4, dtype=jnp.int32)
    segment_scaling_factor = jnp.broadcast_to(segment_scaling_factor, (TOKENS // SPAN, SPAN, H)).reshape(TOKENS, H)
    processor_scaling_factor = jax.random.randint(keys[2], (TOKENS // TOK_DEV, 1, H), 1, 3, dtype=jnp.int32)
    processor_scaling_factor = jnp.broadcast_to(processor_scaling_factor, (TOKENS // TOK_DEV, TOK_DEV, H)).reshape(TOKENS, H)
    frame_scaling_factor = jax.random.randint(keys[3], (TOKENS, H), 1, 3, dtype=jnp.int32)
    location_indices = jax.random.randint(keys[4], (3, 1, H), 0, TOKENS, dtype=jnp.int32)
    portion_counts = jax.random.randint(keys[5], (3, 1, H), 461373, 1447035, dtype=jnp.int32)
    assigned_locations = jnp.arange(TOKENS, dtype=jnp.int32)[None, :, None]
    segment_lengths = jnp.max(jnp.where(assigned_locations == location_indices, portion_counts, 0), axis=0)
    return starting_quantity[None, :] * segment_scaling_factor * processor_scaling_factor * frame_scaling_factor + segment_lengths


def touch_ends(drawn, own_key, least, largest):
    spot = [jax.random.randint(jax.random.fold_in(own_key, axis), (), 0, length) for axis, length in enumerate(drawn.shape)]
    main_axis = drawn.shape.index(max(drawn.shape))
    next_to = spot[:main_axis] + [(spot[main_axis] + 1) % drawn.shape[main_axis]] + spot[main_axis + 1:]
    return drawn.at[tuple(spot)].set(least).at[tuple(next_to)].set(largest)


def steps_of(stream_key, dims, pieces, least, high):
    def one(dim, parts):
        draws = jax.random.uniform(jax.random.fold_in(jax.random.fold_in(stream_key, 6), dim), (parts,), jnp.float32, least / len(pieces), high / len(pieces))
        return jnp.repeat(jnp.exp(draws), dims[dim] // parts).reshape((-1,) + (1,) * (len(dims) - dim - 1))

    level = one(*pieces[0])
    for cut in pieces[1:]:
        level = level * one(*cut)
    return level


def normal_values(own_key, shape, width, most, cuts=(), held_as=jnp.bfloat16):
    result = jax.random.normal(own_key, shape, jnp.float32) * width
    if len(cuts) > 0:
        result = steps_of(own_key, shape, cuts, -0.22, 0.18) * result
    return jnp.clip(result, min=-most, max=most).astype(held_as)


def setup_inputs(seed: int = 0) -> dict:
    arg_keys = jax.random.split(jax.random.key(seed), 9)
    return {
        "tokens": draw_tokens(jax.random.fold_in(arg_keys[8], 71), 0),
        "w_query": normal_values(arg_keys[1], (D, H * HEAD_DIM), D ** -0.5, 0.125, ((1, 4),)),
        "w_key": draw_w_key(jax.random.fold_in(arg_keys[8], 71), 0),
        "w_value": normal_values(arg_keys[3], (D, H * HEAD_DIM), D ** -0.5, 0.125, ((1, 4),)),
        "gate_codes": draw_gate_codes(jax.random.fold_in(arg_keys[8], 71), 0),
        "beta_codes": touch_ends(jax.random.randint(arg_keys[5], (TOKENS, H), 32, 257), jax.random.fold_in(arg_keys[5], 1), 32, 256).astype(jnp.int32),
        "norm_gain": jnp.clip(1.0 + 0.15 * jax.random.normal(arg_keys[6], (HEAD_DIM,), jnp.float32), 0.25, 1.75),
        "w_out": normal_values(arg_keys[7], (H * HEAD_DIM, D), (H * HEAD_DIM) ** -0.5, 0.1875, ((0, 4),)),
    }


def reference(tokens, w_query, w_key, w_value, gate_codes, beta_codes, norm_gain, w_out):
    highest = lax.Precision.HIGHEST
    query = jnp.dot(tokens.astype(jnp.float32), w_query.astype(jnp.float32), preferred_element_type=jnp.float32)
    key_rows = jnp.dot(tokens.astype(jnp.float32), w_key.astype(jnp.float32), preferred_element_type=jnp.float32)
    value = jnp.dot(tokens.astype(jnp.float32), w_value.astype(jnp.float32), preferred_element_type=jnp.float32)
    n_spans = TOKENS // SPAN

    def split_heads(array):
        return array.reshape(n_spans, SPAN, H, HEAD_DIM).transpose(0, 2, 1, 3)
    queries = split_heads(query)
    unit_keys = split_heads(key_rows)
    unit_keys = unit_keys * lax.rsqrt(lax.optimization_barrier(jnp.sum(unit_keys * unit_keys, -1, keepdims=True)) + 1e-06)
    values = split_heads(value)
    decay_log = (-gate_codes.astype(jnp.float32) / 2097152.0).reshape(n_spans, SPAN, H).transpose(0, 2, 1)
    log_decay = jnp.cumsum(decay_log, axis=-1)
    betas = (beta_codes.astype(jnp.float32) / 256.0).reshape(n_spans, SPAN, H).transpose(0, 2, 1)
    positions = jnp.arange(SPAN)
    lower_incl = positions[:, None] >= positions[None, :]
    lower_strict = positions[:, None] > positions[None, :]
    identity_mat = jnp.eye(SPAN, dtype=jnp.float32)

    def span_step(state, inputs):
        span_query, span_key, span_value, span_log, span_beta = inputs
        gaps = span_log[:, :, None] - span_log[:, None, :]
        inclusive = jnp.where(lower_incl, jnp.exp(jnp.where(lower_incl, gaps, 0.0)), 0.0)
        strict = jnp.where(lower_strict, inclusive, 0.0)
        key_dots = jnp.einsum('htd,hid->hti', span_key, span_key, precision=highest)
        system = identity_mat + span_beta[:, :, None] * key_dots * strict
        right = jnp.concatenate([span_beta[:, :, None] * span_key * jnp.exp(span_log)[:, :, None], span_beta[:, :, None] * span_value], axis=-1)
        solved = jax.scipy.linalg.solve_triangular(system, right, lower=True, unit_diagonal=True)
        wy_keys = solved[..., :HEAD_DIM]
        wy_values = solved[..., HEAD_DIM:]
        pseudo = wy_values - jnp.einsum('htk,hvk->htv', wy_keys, state, precision=highest)
        query_dots = jnp.einsum('htd,hid->hti', span_query, span_key, precision=highest) * inclusive
        span_out = jnp.einsum('htk,hvk->htv', span_query * jnp.exp(span_log)[:, :, None], state, precision=highest)
        span_out = span_out + jnp.einsum('hti,hiv->htv', query_dots, pseudo, precision=highest)
        last_log = span_log[:, -1]
        key_tail = span_key * jnp.exp(last_log[:, None] - span_log)[:, :, None]
        new_state = jnp.exp(last_log)[:, None, None] * state + jnp.einsum('htv,htk->hvk', pseudo, key_tail, precision=highest)
        return (new_state, span_out)
    start_state = jnp.zeros((H, HEAD_DIM, HEAD_DIM), jnp.float32)
    _, outputs = lax.scan(span_step, start_state, (queries, unit_keys, values, log_decay, betas))
    normed = outputs * lax.rsqrt(lax.optimization_barrier(jnp.mean(outputs * outputs, -1, keepdims=True)) + 1e-06) * norm_gain
    normed = normed.astype(jnp.bfloat16).transpose(0, 2, 1, 3).reshape(TOKENS, H * HEAD_DIM)
    return jnp.dot(normed.astype(jnp.float32), w_out.astype(jnp.float32), preferred_element_type=jnp.float32).astype(jnp.bfloat16)
```

```python
import functools
import jax
import jax.numpy as jnp
from jax import lax
from jax.experimental import pallas as pl
from jax.experimental.pallas import tpu as pltpu
from jax.sharding import PartitionSpec as P

BASE = 16
F32 = jnp.float32
BF16 = jnp.bfloat16


def split(x):
    high = x.astype(BF16)
    return high, (x - high.astype(F32)).astype(BF16)


def contract(a, b, dims):
    return lax.dot_general(a, b, (dims, ((), ())), preferred_element_type=F32)


NN = ((1,), (0,))
NT = ((1,), (1,))


def dot3(a, b, dims=NN):
    return contract(a[0], b[0], dims) + (contract(a[0], b[1], dims) + contract(a[1], b[0], dims))


def dot1(a, b, dims=NN):
    return contract(a.astype(BF16), b.astype(BF16), dims)


def gates_kernel(gate_ref, beta_ref, decay_ref, strict_ref, cols_ref):
    rows, heads = gate_ref.shape
    tok = lax.broadcasted_iota(jnp.int32, (rows, rows), 0)
    other = lax.broadcasted_iota(jnp.int32, (rows, rows), 1)
    ones = jnp.where(tok >= other, 1.0, 0.0).astype(BF16)
    codes = gate_ref[...]
    pieces = [codes >> 14, (codes >> 7) & 127, codes & 127]
    pieces = [p.astype(F32).astype(BF16) for p in pieces]
    sums = [contract(ones, p, NN) for p in pieces]
    logs = -(sums[0] * 16384.0 + sums[1] * 128.0 + sums[2]) / 2097152.0
    beta = beta_ref[...].astype(F32) / 256.0
    logs_t = jnp.transpose(logs)
    beta_t = jnp.transpose(beta)
    for h in range(heads):
        col = jnp.broadcast_to(logs[:, h : h + 1], (rows, rows))
        row = logs_t[h : h + 1, :]
        gap = col - row
        decay_ref[h] = jnp.where(tok >= other, jnp.exp(jnp.where(tok >= other, gap, 0.0)), 0.0)
        strict_ref[h] = jnp.where(
            other > tok, jnp.exp(jnp.where(other > tok, -gap, 0.0)) * beta_t[h : h + 1, :], 0.0
        )
        grown = jnp.exp(col)
        beta_col = jnp.broadcast_to(beta[:, h : h + 1], (rows, rows))
        cols_ref[h, 0] = grown
        cols_ref[h, 1] = beta_col * grown
        cols_ref[h, 2] = beta_col
        cols_ref[h, 3] = jnp.exp(row[:, rows - 1 :] - col)


def invert_upper(uppers):
    rows = uppers[0].shape[0]
    blocks = rows // BASE
    tok = lax.broadcasted_iota(jnp.int32, (rows, rows), 0)
    other = lax.broadcasted_iota(jnp.int32, (rows, rows), 1)
    lane = lax.broadcasted_iota(jnp.int32, (BASE, rows), 1)
    sub = lax.broadcasted_iota(jnp.int32, (BASE, rows), 0)
    inverses = []
    for upper in uppers:
        compact = jnp.zeros((BASE, rows), F32)
        for b in range(blocks):
            compact = compact + jnp.where(
                lane // BASE == b, upper[b * BASE : (b + 1) * BASE, :], 0.0
            )
        solved = jnp.where(sub == lane % BASE, 1.0, 0.0)
        for j in range(BASE - 1, 0, -1):
            column = jnp.take_along_axis(compact, (lane // BASE) * BASE + j, axis=1)
            solved = solved - column * solved[j : j + 1, :]
        inverses.append(
            jnp.where(tok // BASE == other // BASE, jnp.concatenate([solved] * blocks, 0), 0.0)
        )
    size = BASE
    while size < rows:
        link = (tok // size + 1 == other // size) & ((tok // size) % 2 == 0)
        links = [split(jnp.where(link, upper, 0.0)) for upper in uppers]
        halves = [split(inverse) for inverse in inverses]
        first = [dot3(halves[h], links[h]) for h in range(len(uppers))]
        first = [split(x) for x in first]
        inverses = [inverses[h] - dot3(first[h], halves[h]) for h in range(len(uppers))]
        size *= 2
    return inverses


def project(pieces, weight_ref, place):
    depth = pieces[0].shape[1]
    total = None
    for d, piece in enumerate(pieces):
        start = pl.multiple_of((place ^ d) * depth, depth)
        term = contract(piece[...], weight_ref[pl.ds(start, depth), :], NN)
        total = term if total is None else total + term
    return total


def summary_kernel(n_pieces, size, place_ref, *refs):
    pieces = refs[:n_pieces]
    wk_ref, wv_ref, strict_ref, cols_ref = refs[n_pieces : n_pieces + 4]
    map_ref, send_ref, keys_ref, inv_ref, right_ref = refs[n_pieces + 4 :]
    heads = strict_ref.shape[0]
    rows = pieces[0].shape[0]
    place = place_ref[0]
    keys = project(pieces, wk_ref, place)
    values = project(pieces, wv_ref, place)
    uppers, tails, lefts = [], [], []
    for h in range(heads):
        key = keys[:, h * size : (h + 1) * size]
        key = key * lax.rsqrt(jnp.sum(key * key, -1, keepdims=True) + 1e-06)
        halves = split(key)
        keys_ref[h] = key
        uppers.append(dot3(halves, halves, NT) * strict_ref[h])
        tails.append(split(key * cols_ref[h, 3]))
        right_key = key * cols_ref[h, 1]
        right_value = values[:, h * size : (h + 1) * size] * cols_ref[h, 2]
        right_ref[h, 0] = right_value
        right_ref[h, 1] = right_key
        lefts.append(split(jnp.concatenate([jnp.transpose(right_key), jnp.transpose(right_value)], 0)))
    inverses = invert_upper(uppers)
    eye = lax.broadcasted_iota(jnp.int32, (size, size), 0) == lax.broadcasted_iota(
        jnp.int32, (size, size), 1
    )
    for h in range(heads):
        inv_ref[h] = inverses[h]
        z = split(dot3(split(inverses[h]), tails[h]))
        both = dot3(lefts[h], z)
        step = jnp.where(eye, cols_ref[h, 0][rows - 1 :, :], 0.0) - both[:size]
        add = both[size:]
        map_ref[h, 0] = step
        map_ref[h, 1] = add
        send_ref[h, 0] = step.astype(BF16)
        send_ref[h, 1] = add.astype(BF16)


def local_kernel(n_pieces, size, place_ref, *refs):
    pieces = refs[:n_pieces]
    wq_ref, decay_ref, cols_ref, keys_ref, inv_ref, right_ref = refs[n_pieces : n_pieces + 6]
    out_ref = refs[-1]
    heads = decay_ref.shape[0]
    queries = project(pieces, wq_ref, place_ref[0])
    for h in range(heads):
        query = queries[:, h * size : (h + 1) * size]
        dots = dot3(split(query), split(keys_ref[h]), NT) * decay_ref[h]
        mixed = split(dot3(split(dots), split(inv_ref[h]), NT))
        out_ref[h, 0] = dot3(mixed, split(right_ref[h, 0]))
        out_ref[h, 1] = query * cols_ref[h, 0] - dot3(mixed, split(right_ref[h, 1]))


def merge_kernel(first, upper_ref, got_ref, own_ref, *refs):
    if first:
        prefix_ref = None
        total_ref, send_ref, new_ref = refs
    else:
        prefix_ref, total_ref, send_ref, new_ref = refs
    heads, _, size, _ = own_ref.shape
    is_upper = upper_ref[0] > 0
    eye = lax.broadcasted_iota(jnp.int32, (size, size), 0) == lax.broadcasted_iota(
        jnp.int32, (size, size), 1
    )
    for h in range(heads):
        own = own_ref[h].reshape(2 * size, size)
        got = got_ref[h].astype(F32).reshape(2 * size, size)
        early = jnp.where(is_upper, got, own)
        late = jnp.where(is_upper, own, got)
        both = dot1(early, late[:size])
        step = both[:size]
        add = both[size:] + late[size:]
        total_ref[h, 0] = step
        total_ref[h, 1] = add
        send_ref[h, 0] = step.astype(BF16)
        send_ref[h, 1] = add.astype(BF16)
        if first:
            new_ref[h, 0] = jnp.where(is_upper, got[:size], jnp.where(eye, 1.0, 0.0))
            new_ref[h, 1] = jnp.where(is_upper, got[size:], 0.0)
        else:
            prefix = prefix_ref[h].reshape(2 * size, size)
            joined = dot1(got, prefix[:size])
            new_ref[h, 0] = jnp.where(is_upper, joined[:size], prefix[:size])
            new_ref[h, 1] = jnp.where(is_upper, joined[size:] + prefix[size:], prefix[size:])


def output_kernel(upper_ref, got_ref, prefix_ref, local_ref, gain_ref, normed_ref):
    heads, _, size, _ = prefix_ref.shape
    is_upper = upper_ref[0] > 0
    for h in range(heads):
        state = prefix_ref[h, 1] + jnp.where(
            is_upper, dot1(got_ref[h], prefix_ref[h, 0]), 0.0
        )
        out = local_ref[h, 0] + dot3(split(local_ref[h, 1]), split(state), NT)
        scale = lax.rsqrt(jnp.mean(out * out, -1, keepdims=True) + 1e-06)
        normed_ref[:, h * size : (h + 1) * size] = (out * scale * gain_ref[...]).astype(BF16)


def mix_kernel(n_pieces, *refs):
    total = None
    for d in range(n_pieces):
        term = contract(refs[d][...], refs[n_pieces + d][...], NN)
        total = term if total is None else total + term
    refs[-1][...] = total.astype(BF16)


def call(kernel, outs, args, scalars=0):
    specs = [pl.BlockSpec(memory_space=pltpu.SMEM)] * scalars
    specs += [pl.BlockSpec(memory_space=pltpu.VMEM)] * (len(args) - scalars)
    many = isinstance(outs, (list, tuple))
    return pl.pallas_call(
        kernel,
        out_shape=outs,
        in_specs=specs,
        out_specs=jax.tree.map(lambda _: pl.BlockSpec(memory_space=pltpu.VMEM), outs),
        compiler_params=pltpu.CompilerParams(vmem_limit_bytes=24 * 1024 * 1024),
    )(*args)


def like(*shape, dtype=F32):
    return jax.ShapeDtypeStruct(shape, dtype)


def shards(n_seq, n_head, tokens, w_query, w_key, w_value, gate_codes, beta_codes, norm_gain, w_out):
    rows, depth = tokens.shape
    heads = gate_codes.shape[1]
    size = norm_gain.shape[0]
    width = w_out.shape[1] // n_head
    place = lax.axis_index("head")
    turn = lax.axis_index("seq")

    def swap(x, axis, count, d):
        return lax.ppermute(x, axis, [(i, i ^ d) for i in range(count)])

    def spread(x):
        have = {0: x}
        d = n_head // 2
        while d:
            have.update({e ^ d: swap(have[e], "head", n_head, d) for e in list(have)})
            d //= 2
        return [have[d] for d in range(n_head)]

    pieces = spread(tokens)
    out_weights = []
    for d in range(n_head):
        part = lax.dynamic_slice(w_out, (0, (place ^ d) * width), (w_out.shape[0], width))
        out_weights.append(swap(part, "head", n_head, d) if d else part)
    decay, strict, cols = call(
        gates_kernel,
        [like(heads, rows, rows), like(heads, rows, rows), like(heads, 4, rows, size)],
        [gate_codes, beta_codes],
    )
    here = place.astype(jnp.int32).reshape(1)
    pair = like(heads, 2, size, size)
    pair_sent = like(heads, 2, size, size, dtype=BF16)
    total, send, keys, inverse, right = call(
        functools.partial(summary_kernel, n_head, size),
        [pair, pair_sent, like(heads, rows, size), like(heads, rows, rows), like(heads, 2, rows, size)],
        [here, *pieces, w_key, w_value, strict, cols],
        1,
    )
    local = call(
        functools.partial(local_kernel, n_head, size),
        like(heads, 2, rows, size),
        [here, *pieces, w_query, decay, cols, keys, inverse, right],
        1,
    )
    prefix = None
    d = 1
    while d < n_seq // 2:
        got = swap(send, "seq", n_seq, d)
        upper = ((turn // d) % 2).astype(jnp.int32).reshape(1)
        args = [upper, got, total] + ([] if prefix is None else [prefix])
        total, send, prefix = call(
            functools.partial(merge_kernel, prefix is None), [pair, pair_sent, pair], args, 1
        )
        d *= 2
    got = swap(send[:, 1], "seq", n_seq, d)
    upper = ((turn // d) % 2).astype(jnp.int32).reshape(1)
    normed = call(
        output_kernel,
        like(rows, heads * size, dtype=BF16),
        [upper, got, prefix, local, norm_gain.reshape(1, size)],
        1,
    )
    return call(
        functools.partial(mix_kernel, n_head),
        like(rows, width, dtype=BF16),
        spread(normed) + out_weights,
    )


def solution(mesh):
    n_seq, n_head = mesh.shape["seq"], mesh.shape["head"]
    return jax.shard_map(
        functools.partial(shards, n_seq, n_head),
        mesh=mesh,
        in_specs=(
            P("seq", "head"),
            P(None, "head"),
            P(None, "head"),
            P(None, "head"),
            P("seq", "head"),
            P("seq", "head"),
            P(),
            P("head", None),
        ),
        out_specs=P("seq", "head"),
        check_vma=False,
    )
```

```python
import functools
import jax
import jax.numpy as jnp
from jax import lax
from jax.experimental import pallas as pl
from jax.experimental.pallas import tpu as pltpu
from jax.sharding import PartitionSpec as P

BASE = 16
F32 = jnp.float32
BF16 = jnp.bfloat16


def split(x):
    high = x.astype(BF16)
    return high, (x - high.astype(F32)).astype(BF16)


def contract(a, b, dims):
    return lax.dot_general(a, b, (dims, ((), ())), preferred_element_type=F32)


NN = ((1,), (0,))
NT = ((1,), (1,))


def dot3(a, b, dims=NN):
    return contract(a[0], b[0], dims) + (contract(a[0], b[1], dims) + contract(a[1], b[0], dims))


def dot1(a, b, dims=NN):
    return contract(a.astype(BF16), b.astype(BF16), dims)


def gate_tables(codes, beta, decay_ref, strict_ref, cols_ref, grown_ref):
    heads, rows = codes.shape
    tok = lax.broadcasted_iota(jnp.int32, (rows, rows), 0)
    other = lax.broadcasted_iota(jnp.int32, (rows, rows), 1)
    ones = jnp.where(tok <= other, 1.0, 0.0).astype(BF16)
    sums = [
        contract(p.astype(F32).astype(BF16), ones, NN)
        for p in (codes >> 14, (codes >> 7) & 127, codes & 127)
    ]
    logs = -(sums[0] * 16384.0 + sums[1] * 128.0 + sums[2]) / 2097152.0
    beta = beta.astype(F32) / 256.0
    logs_t = jnp.transpose(logs)
    beta_t = jnp.transpose(beta)
    for h in range(heads):
        row = logs[h : h + 1, :]
        col = jnp.broadcast_to(logs_t[:, h : h + 1], (rows, rows))
        gap = col - row
        decay_ref[h] = jnp.where(tok >= other, jnp.exp(jnp.where(tok >= other, gap, 0.0)), 0.0)
        strict_ref[h] = jnp.where(
            other > tok, jnp.exp(jnp.where(other > tok, -gap, 0.0)) * beta[h : h + 1, :], 0.0
        )
        grown = jnp.exp(col)
        beta_col = jnp.broadcast_to(beta_t[:, h : h + 1], (rows, rows))
        grown_ref[h] = grown
        cols_ref[h, 0] = beta_col * grown
        cols_ref[h, 1] = beta_col
        cols_ref[h, 2] = jnp.exp(row[:, rows - 1 :] - col)


def copy_all(moves, sems):
    copies = [pltpu.make_async_copy(a, b, sems.at[i]) for i, (a, b) in enumerate(moves)]
    for copy in copies:
        copy.start()
    return copies


def block_of(place, d, depth):
    return pl.ds(pl.multiple_of((place ^ d) * depth, depth), depth)


def out_slices(place, wo_hbm, out_refs, first):
    width = out_refs[0].shape[1]
    return [
        (wo_hbm.at[:, block_of(place, first + i, width)], ref) for i, ref in enumerate(out_refs)
    ]


def prepare_kernel(n_head, place_ref, tok_hbm, wk_hbm, wv_hbm, wo_hbm, gate_hbm, beta_hbm, gain_hbm, *refs):
    acc_ref, rest_ref, decay_ref, strict_ref, cols_ref, grown_ref, gain_ref = refs[:7]
    out_refs = refs[7:-5]
    tok_ref, own_ref, gate_ref, beta_ref, sems = refs[-5:]
    place = place_ref[0]
    depth = tok_ref.shape[1]
    weights = (wk_hbm, wv_hbm)
    moves = [(gate_hbm, gate_ref), (beta_hbm, beta_ref), (gain_hbm, gain_ref), (tok_hbm, tok_ref)]
    moves += [(w.at[block_of(place, 0, depth), :], own_ref.at[i]) for i, w in enumerate(weights)]
    moves += [
        (w.at[block_of(place, d, depth), :], rest_ref.at[d - 1, i])
        for d in range(1, n_head)
        for i, w in enumerate(weights)
    ]
    moves += out_slices(place, wo_hbm, out_refs, n_head - len(out_refs))
    copies = copy_all(moves, sems)
    copies[0].wait()
    copies[1].wait()
    gate_tables(gate_ref[...], beta_ref[...], decay_ref, strict_ref, cols_ref, grown_ref)
    for copy in copies[2:6]:
        copy.wait()
    for i in range(len(weights)):
        acc_ref[i] = contract(tok_ref[...], own_ref[i], NN)
    for copy in copies[6:]:
        copy.wait()


def more_kernel(n_pieces, acc_ref, rest_ref, *refs):
    out_ref = refs[-1]
    for i in range(acc_ref.shape[0]):
        total = acc_ref[i]
        for d in range(n_pieces):
            total = total + contract(refs[d][...], rest_ref[d, i], NN)
        out_ref[i] = total


def invert_upper(uppers):
    rows = uppers[0].shape[0]
    blocks = rows // BASE
    tok = lax.broadcasted_iota(jnp.int32, (rows, rows), 0)
    other = lax.broadcasted_iota(jnp.int32, (rows, rows), 1)
    lane = lax.broadcasted_iota(jnp.int32, (BASE, rows), 1)
    sub = lax.broadcasted_iota(jnp.int32, (BASE, rows), 0)
    inverses = []
    for upper in uppers:
        compact = jnp.zeros((BASE, rows), F32)
        for b in range(blocks):
            compact = compact + jnp.where(
                lane // BASE == b, upper[b * BASE : (b + 1) * BASE, :], 0.0
            )
        solved = jnp.where(sub == lane % BASE, 1.0, 0.0)
        for j in range(BASE - 1, 0, -1):
            column = jnp.take_along_axis(compact, (lane // BASE) * BASE + j, axis=1)
            solved = solved - column * solved[j : j + 1, :]
        inverses.append(
            jnp.where(tok // BASE == other // BASE, jnp.concatenate([solved] * blocks, 0), 0.0)
        )
    size = BASE
    while size < rows:
        link = (tok // size + 1 == other // size) & ((tok // size) % 2 == 0)
        links = [split(jnp.where(link, upper, 0.0)) for upper in uppers]
        halves = [split(inverse) for inverse in inverses]
        first = [dot3(halves[h], links[h]) for h in range(len(uppers))]
        first = [split(x) for x in first]
        inverses = [inverses[h] - dot3(first[h], halves[h]) for h in range(len(uppers))]
        size *= 2
    return inverses


def summary_kernel(size, acc_ref, rest_ref, piece_ref, strict_ref, cols_ref, grown_ref, add_ref, send_ref, keys_ref, inv_ref, right_ref):
    heads, rows, _ = strict_ref.shape
    last = rest_ref.shape[0] - 1
    keys = acc_ref[0] + contract(piece_ref[...], rest_ref[last, 0], NN)
    values = acc_ref[1] + contract(piece_ref[...], rest_ref[last, 1], NN)
    uppers, tails, lefts = [], [], []
    for h in range(heads):
        key = keys[:, h * size : (h + 1) * size]
        key = key * lax.rsqrt(jnp.sum(key * key, -1, keepdims=True) + 1e-06)
        halves = split(key)
        keys_ref[h] = key
        uppers.append(dot3(halves, halves, NT) * strict_ref[h])
        tails.append(split(key * cols_ref[h, 2]))
        right_key = key * cols_ref[h, 0]
        right_value = values[:, h * size : (h + 1) * size] * cols_ref[h, 1]
        right_ref[h, 0] = right_value
        right_ref[h, 1] = right_key
        lefts.append(split(jnp.concatenate([jnp.transpose(right_key), jnp.transpose(right_value)], 0)))
    inverses = invert_upper(uppers)
    eye = lax.broadcasted_iota(jnp.int32, (size, size), 0) == lax.broadcasted_iota(
        jnp.int32, (size, size), 1
    )
    for h in range(heads):
        inv_ref[h] = inverses[h]
        z = split(dot3(split(inverses[h]), tails[h]))
        both = dot3(lefts[h], z)
        step = jnp.where(eye, grown_ref[h, rows - 1 :, :], 0.0) - both[:size]
        add = both[size:]
        add_ref[h] = add
        send_ref[h, 0] = step.astype(BF16)
        send_ref[h, 1] = add.astype(BF16)


def local_kernel(n_head, size, place_ref, wq_hbm, tok_hbm, *refs):
    pieces = refs[: n_head - 1]
    decay_ref, grown_ref, keys_ref, inv_ref, right_ref, out_ref, wq_ref, tok_ref, sems = refs[n_head - 1 :]
    heads = decay_ref.shape[0]
    depth = tok_ref.shape[1]
    moves = [(tok_hbm, tok_ref)]
    moves += [
        (wq_hbm.at[block_of(place_ref[0], d, depth), :], wq_ref.at[d]) for d in range(n_head)
    ]
    for copy in copy_all(moves, sems):
        copy.wait()
    queries = contract(tok_ref[...], wq_ref[0], NN)
    for d in range(1, n_head):
        queries = queries + contract(pieces[d - 1][...], wq_ref[d], NN)
    for h in range(heads):
        query = queries[:, h * size : (h + 1) * size]
        dots = dot3(split(query), split(keys_ref[h]), NT) * decay_ref[h]
        mixed = split(dot3(split(dots), split(inv_ref[h]), NT))
        out_ref[h, 0] = dot3(mixed, split(right_ref[h, 0]))
        out_ref[h, 1] = query * grown_ref[h] - dot3(mixed, split(right_ref[h, 1]))


def merge_kernel(first, last, upper_ref, got_ref, own_ref, add_ref, *refs):
    if not first:
        pmap_ref, padd_ref, *refs = refs
    new_map_ref, new_add_ref, send_ref, *total_ref = refs
    heads, _, size, _ = own_ref.shape
    is_upper = upper_ref[0] > 0
    eye = lax.broadcasted_iota(jnp.int32, (size, size), 0) == lax.broadcasted_iota(
        jnp.int32, (size, size), 1
    )
    for h in range(heads):
        own = own_ref[h].reshape(2 * size, size)
        got = got_ref[h].reshape(2 * size, size)
        early = jnp.where(is_upper, got, own)
        late = jnp.where(is_upper, own[:size], got[:size])
        late_add = jnp.where(is_upper, add_ref[h], got[size:].astype(F32))
        if last:
            send_ref[h] = (contract(early[size:], late, NN) + late_add).astype(BF16)
        else:
            both = contract(early, late, NN)
            add = both[size:] + late_add
            total_ref[0][h] = add
            send_ref[h, 0] = both[:size].astype(BF16)
            send_ref[h, 1] = add.astype(BF16)
        if first:
            new_map_ref[h] = jnp.where(is_upper, got[:size], jnp.where(eye, 1.0, 0.0).astype(BF16))
            new_add_ref[h] = jnp.where(is_upper, got[size:].astype(F32), 0.0)
        else:
            joined = contract(got, pmap_ref[h], NN)
            new_map_ref[h] = jnp.where(is_upper, joined[:size].astype(BF16), pmap_ref[h])
            new_add_ref[h] = jnp.where(is_upper, joined[size:], 0.0) + padd_ref[h]


def output_kernel(upper_ref, got_ref, pmap_ref, padd_ref, local_ref, gain_ref, normed_ref):
    heads, size, _ = padd_ref.shape
    is_upper = upper_ref[0] > 0
    for h in range(heads):
        state = padd_ref[h] + jnp.where(is_upper, contract(got_ref[h], pmap_ref[h], NN), 0.0)
        out = local_ref[h, 0] + dot3(split(local_ref[h, 1]), split(state), NT)
        scale = lax.rsqrt(jnp.mean(out * out, -1, keepdims=True) + 1e-06)
        normed_ref[:, h * size : (h + 1) * size] = (out * scale * gain_ref[...]).astype(BF16)


def mix_own_kernel(place_ref, wo_hbm, part_ref, out_ref, weight_ref, sem):
    width = weight_ref.shape[1]
    copy = pltpu.make_async_copy(wo_hbm.at[:, block_of(place_ref[0], 0, width)], weight_ref, sem)
    copy.start()
    copy.wait()
    out_ref[...] = contract(part_ref[...], weight_ref[...], NN)


def mix_kernel(n_pieces, base_ref, *refs):
    total = base_ref[...]
    for part, weight in zip(refs[:n_pieces], refs[n_pieces : 2 * n_pieces]):
        total = total + contract(part[...], weight[...], NN)
    refs[-1][...] = total.astype(refs[-1].dtype)


def call(kernel, outs, args, scalars=0, hbm=0, scratch=()):
    vmem = pl.BlockSpec(memory_space=pltpu.VMEM)
    far = pl.BlockSpec(memory_space=pltpu.HBM)
    specs = [pl.BlockSpec(memory_space=pltpu.SMEM)] * scalars + [far] * hbm
    specs += [vmem] * (len(args) - scalars - hbm)
    args = [
        pltpu.with_memory_space_constraint(a, pltpu.HBM) if scalars <= i < scalars + hbm else a
        for i, a in enumerate(args)
    ]
    return pl.pallas_call(
        kernel,
        out_shape=outs,
        in_specs=specs,
        out_specs=[vmem] * len(outs),
        scratch_shapes=scratch,
        compiler_params=pltpu.CompilerParams(vmem_limit_bytes=16 * 1024 * 1024),
    )(*args)


def like(*shape, dtype=F32):
    return jax.ShapeDtypeStruct(shape, dtype)


def shards(n_seq, n_head, tokens, w_query, w_key, w_value, gate_codes, beta_codes, norm_gain, w_out):
    rows, depth = tokens.shape
    heads = gate_codes.shape[1]
    size = norm_gain.shape[0]
    width = w_out.shape[1] // n_head
    place = lax.axis_index("head")
    turn = lax.axis_index("seq")

    def swap(x, axis, count, d):
        return lax.ppermute(x, axis, [(i, i ^ d) for i in range(count)])

    def tie(*x):
        return lax.optimization_barrier(x)

    def spread(x, during):
        d = n_head // 2
        have = {d: swap(x, "head", n_head, d)}
        have[d], extra = tie(have[d], during)
        while d > 1:
            d //= 2
            have.update({e ^ d: swap(have[e], "head", n_head, d) for e in list(have)})
            have[d] = swap(x, "head", n_head, d)
        return [have[d] for d in range(1, n_head)], extra

    here = place.astype(jnp.int32).reshape(1)
    slice_out = like(heads * size, width, dtype=BF16)
    acc, rest, decay, strict, cols, grown, gain, *slices = call(
        functools.partial(prepare_kernel, n_head),
        [
            like(2, rows, heads * size),
            like(n_head - 1, 2, depth, heads * size, dtype=BF16),
            like(heads, rows, rows),
            like(heads, rows, rows),
            like(heads, 3, rows, size),
            like(heads, rows, size),
            like(1, size),
        ]
        + [slice_out] * (n_head - 1),
        [here, tokens, w_key, w_value, w_out, gate_codes.T, beta_codes.T, norm_gain.reshape(1, size)],
        1,
        7,
        [
            pltpu.VMEM((rows, depth), BF16),
            pltpu.VMEM((2, depth, heads * size), BF16),
            pltpu.VMEM((heads, rows), jnp.int32),
            pltpu.VMEM((heads, rows), jnp.int32),
            pltpu.SemaphoreType.DMA((3 + 3 * n_head,)),
        ],
    )
    pieces, (acc, rest) = spread(tokens, (acc, rest))
    (acc,) = call(
        functools.partial(more_kernel, n_head - 2),
        [like(2, rows, heads * size)],
        [acc, rest, *pieces[:-1]],
    )
    state = like(heads, size, size)
    state_sent = like(heads, size, size, dtype=BF16)
    pair_sent = like(heads, 2, size, size, dtype=BF16)
    total, send, keys, inverse, right = call(
        functools.partial(summary_kernel, size),
        [state, pair_sent, like(heads, rows, size), like(heads, rows, rows), like(heads, 2, rows, size)],
        [acc, rest, pieces[-1], strict, cols, grown],
    )
    send, *slices = tie(send, *slices)
    (local,) = call(
        functools.partial(local_kernel, n_head, size),
        [like(heads, 2, rows, size)],
        [here, w_query, tokens, *pieces, decay, grown, keys, inverse, right],
        1,
        2,
        [
            pltpu.VMEM((n_head, depth, heads * size), BF16),
            pltpu.VMEM((rows, depth), BF16),
            pltpu.SemaphoreType.DMA((n_head + 1,)),
        ],
    )
    out_weights = [swap(slices[d - 1], "head", n_head, d) for d in range(1, n_head)]
    prefix = []
    d = 1
    while d < n_seq // 2:
        got = swap(send, "seq", n_seq, d)
        upper = ((turn // d) % 2).astype(jnp.int32).reshape(1)
        last = 2 * d >= n_seq // 2
        if last:
            got, local = tie(got, local)
        outs = [state_sent, state] + ([state_sent] if last else [pair_sent, state])
        *prefix, send, total = [
            *call(
                functools.partial(merge_kernel, d == 1, last),
                outs,
                [upper, got, send, total, *prefix],
                1,
            ),
            None,
        ][:4]
        d *= 2
    got = swap(send, "seq", n_seq, d)
    got, *out_weights = tie(got, *out_weights)
    upper = ((turn // d) % 2).astype(jnp.int32).reshape(1)
    (normed,) = call(
        output_kernel,
        [like(rows, heads * size, dtype=BF16)],
        [upper, got, *prefix, local, gain],
        1,
    )
    (mixed,) = call(
        mix_own_kernel,
        [like(rows, width)],
        [here, w_out, normed],
        1,
        1,
        [pltpu.VMEM((heads * size, width), BF16), pltpu.SemaphoreType.DMA(())],
    )
    parts, mixed = spread(normed, mixed)
    (mixed,) = call(
        functools.partial(mix_kernel, n_head - 2),
        [like(rows, width)],
        [mixed, *parts[:-1], *out_weights[:-1]],
    )
    return call(
        functools.partial(mix_kernel, 1),
        [like(rows, width, dtype=BF16)],
        [mixed, parts[-1], out_weights[-1]],
    )[0]


def solution(mesh):
    n_seq, n_head = mesh.shape["seq"], mesh.shape["head"]
    return jax.shard_map(
        functools.partial(shards, n_seq, n_head),
        mesh=mesh,
        in_specs=(
            P("seq", "head"),
            P(None, "head"),
            P(None, "head"),
            P(None, "head"),
            P("seq", "head"),
            P("seq", "head"),
            P(),
            P("head", None),
        ),
        out_specs=P("seq", "head"),
        check_vma=False,
    )
```

```python
import functools
import jax
import jax.numpy as jnp
from jax import lax
from jax.experimental import pallas as pl
from jax.experimental.pallas import tpu as pltpu
from jax.sharding import PartitionSpec as P

BASE = 16
F32 = jnp.float32
BF16 = jnp.bfloat16


def split(x):
    high = x.astype(BF16)
    return high, (x - high.astype(F32)).astype(BF16)


def contract(a, b, dims):
    return lax.dot_general(a, b, (dims, ((), ())), preferred_element_type=F32)


NN = ((1,), (0,))
NT = ((1,), (1,))


def dot3(a, b, dims=NN):
    left = jnp.concatenate([a[0], a[1], a[0]], dims[0][0])
    right = jnp.concatenate([b[0], b[0], b[1]], dims[1][0])
    return contract(left, right, dims)


def dot2(a, b, dims=NN):
    return contract(
        jnp.concatenate(a, dims[0][0]), jnp.concatenate([b, b], dims[1][0]), dims
    )


def gate_tables(codes, beta, decay_ref, strict_ref, cols_ref, grown_ref):
    heads, rows = codes.shape
    tok = lax.broadcasted_iota(jnp.int32, (rows, rows), 0)
    other = lax.broadcasted_iota(jnp.int32, (rows, rows), 1)
    ones = jnp.where(tok <= other, 1.0, 0.0).astype(BF16)
    sums = [
        contract(p.astype(F32).astype(BF16), ones, NN)
        for p in (codes >> 14, (codes >> 7) & 127, codes & 127)
    ]
    logs = -(sums[0] * 16384.0 + sums[1] * 128.0 + sums[2]) / 2097152.0
    beta = beta.astype(F32) / 256.0
    logs_t = jnp.transpose(logs)
    beta_t = jnp.transpose(beta)
    for h in range(heads):
        row = logs[h : h + 1, :]
        col = jnp.broadcast_to(logs_t[:, h : h + 1], (rows, rows))
        gap = col - row
        decay_ref[h] = jnp.where(tok >= other, jnp.exp(jnp.where(tok >= other, gap, 0.0)), 0.0)
        strict_ref[h] = jnp.where(
            other > tok, jnp.exp(jnp.where(other > tok, -gap, 0.0)) * beta[h : h + 1, :], 0.0
        )
        grown = jnp.exp(col)
        beta_col = jnp.broadcast_to(beta_t[:, h : h + 1], (rows, rows))
        grown_ref[h] = grown
        cols_ref[h, 0] = beta_col * grown
        cols_ref[h, 1] = beta_col
        cols_ref[h, 2] = jnp.exp(row[:, rows - 1 :] - col)


def copy_all(moves, sems):
    copies = [pltpu.make_async_copy(a, b, sems.at[i]) for i, (a, b) in enumerate(moves)]
    for copy in copies:
        copy.start()
    return copies


def block_of(place, d, depth):
    return pl.ds(pl.multiple_of((place ^ d) * depth, depth), depth)


def out_slices(place, wo_hbm, out_refs, first):
    width = out_refs[0].shape[1]
    return [
        (wo_hbm.at[:, block_of(place, first + i, width)], ref) for i, ref in enumerate(out_refs)
    ]


def prepare_kernel(n_head, place_ref, tok_hbm, wk_hbm, wv_hbm, wo_hbm, gate_hbm, beta_hbm, gain_hbm, *refs):
    acc_ref, rest_ref, decay_ref, strict_ref, cols_ref, grown_ref, gain_ref = refs[:7]
    out_refs = refs[7:-5]
    tok_ref, own_ref, gate_ref, beta_ref, sems = refs[-5:]
    place = place_ref[0]
    depth = tok_ref.shape[1]
    weights = (wk_hbm, wv_hbm)
    moves = [(gate_hbm, gate_ref), (beta_hbm, beta_ref), (gain_hbm, gain_ref), (tok_hbm, tok_ref)]
    moves += [(w.at[block_of(place, 0, depth), :], own_ref.at[i]) for i, w in enumerate(weights)]
    moves += [
        (w.at[block_of(place, d, depth), :], rest_ref.at[d - 1, i])
        for d in range(1, n_head)
        for i, w in enumerate(weights)
    ]
    moves += out_slices(place, wo_hbm, out_refs, n_head - len(out_refs))
    copies = copy_all(moves, sems)
    copies[0].wait()
    copies[1].wait()
    gate_tables(gate_ref[...], beta_ref[...], decay_ref, strict_ref, cols_ref, grown_ref)
    for copy in copies[2:6]:
        copy.wait()
    for i in range(len(weights)):
        acc_ref[i] = contract(tok_ref[...], own_ref[i], NN)
    for copy in copies[6:]:
        copy.wait()


def more_kernel(n_pieces, acc_ref, rest_ref, *refs):
    out_ref = refs[-1]
    for i in range(acc_ref.shape[0]):
        total = acc_ref[i]
        for d in range(n_pieces):
            total = total + contract(refs[d][...], rest_ref[d, i], NN)
        out_ref[i] = total


def invert_upper(uppers):
    rows = uppers[0].shape[0]
    blocks = rows // BASE
    tok = lax.broadcasted_iota(jnp.int32, (rows, rows), 0)
    other = lax.broadcasted_iota(jnp.int32, (rows, rows), 1)
    lane = lax.broadcasted_iota(jnp.int32, (BASE, rows), 1)
    sub = lax.broadcasted_iota(jnp.int32, (BASE, rows), 0)
    inverses = []
    for upper in uppers:
        compact = jnp.zeros((BASE, rows), F32)
        for b in range(blocks):
            compact = compact + jnp.where(
                lane // BASE == b, upper[b * BASE : (b + 1) * BASE, :], 0.0
            )
        solved = jnp.where(sub == lane % BASE, 1.0, 0.0)
        for j in range(BASE - 1, 0, -1):
            column = jnp.take_along_axis(compact, (lane // BASE) * BASE + j, axis=1)
            solved = solved - column * solved[j : j + 1, :]
        inverses.append(
            jnp.where(tok // BASE == other // BASE, jnp.concatenate([solved] * blocks, 0), 0.0)
        )
    if blocks == 1:
        return inverses
    between = tok // BASE != other // BASE
    diagonal = [split(x) for x in inverses]
    step = [dot3(d, split(jnp.where(between, u, 0.0))) for d, u in zip(diagonal, uppers)]
    step = [split(x) for x in step]
    inverses = [x - dot3(v, d) for x, v, d in zip(inverses, step, diagonal)]
    covered = 2
    while covered < blocks:
        step = [split(dot3(v, v)) for v in step]
        inverses = [x + dot3(v, split(x)) for x, v in zip(inverses, step)]
        covered *= 2
    return inverses


def summary_kernel(size, acc_ref, rest_ref, piece_ref, strict_ref, cols_ref, grown_ref, send_ref, keys_ref, inv_ref, right_ref):
    heads, rows, _ = strict_ref.shape
    last = rest_ref.shape[0] - 1
    keys = acc_ref[0] + contract(piece_ref[...], rest_ref[last, 0], NN)
    values = acc_ref[1] + contract(piece_ref[...], rest_ref[last, 1], NN)
    every = range(heads)
    each = [keys[:, h * size : (h + 1) * size] for h in every]
    scales = [lax.rsqrt(jnp.sum(key * key, -1, keepdims=True) + 1e-06) for key in each]
    each = [key * scale for key, scale in zip(each, scales)]
    halves = [split(key) for key in each]
    uppers = [dot3(halves[h], halves[h], NT) * strict_ref[h] for h in every]
    tails = [split(each[h] * cols_ref[h, 2]) for h in every]
    right_keys = [each[h] * cols_ref[h, 0] for h in every]
    right_values = [values[:, h * size : (h + 1) * size] * cols_ref[h, 1] for h in every]
    lefts = [
        split(jnp.concatenate([jnp.transpose(right_keys[h]), jnp.transpose(right_values[h])], 0))
        for h in every
    ]
    inverses = invert_upper(uppers)
    eye = lax.broadcasted_iota(jnp.int32, (size, size), 0) == lax.broadcasted_iota(
        jnp.int32, (size, size), 1
    )
    reached = [split(dot3(split(inverses[h]), tails[h])) for h in every]
    both = [dot3(lefts[h], reached[h]) for h in every]
    for h in every:
        step = jnp.where(eye, grown_ref[h, rows - 1 :, :], 0.0) - both[h][:size]
        send_ref[h, 0] = step.astype(BF16)
        send_ref[h, 1] = both[h][size:].astype(BF16)
        keys_ref[h] = each[h]
        inv_ref[h] = inverses[h]
        right_ref[h, 0] = right_values[h]
        right_ref[h, 1] = right_keys[h]


def local_kernel(n_head, size, place_ref, upper_ref, wq_hbm, tok_hbm, *refs):
    pieces = refs[: n_head - 1]
    decay_ref, grown_ref, keys_ref, inv_ref, right_ref, pmap_ref, padd_ref = refs[n_head - 1 : n_head + 6]
    out_ref, reach_ref, wq_ref, tok_ref, sems = refs[n_head + 6 :]
    heads = decay_ref.shape[0]
    depth = tok_ref.shape[1]
    moves = [(tok_hbm, tok_ref)]
    moves += [
        (wq_hbm.at[block_of(place_ref[0], d, depth), :], wq_ref.at[d]) for d in range(n_head)
    ]
    for copy in copy_all(moves, sems):
        copy.wait()
    queries = contract(tok_ref[...], wq_ref[0], NN)
    for d in range(1, n_head):
        queries = queries + contract(pieces[d - 1][...], wq_ref[d], NN)
    is_upper = upper_ref[0] > 0
    for h in range(heads):
        query = queries[:, h * size : (h + 1) * size]
        dots = dot3(split(query), split(keys_ref[h]), NT) * decay_ref[h]
        mixed = split(dot3(split(dots), split(inv_ref[h]), NT))
        reach = split(query * grown_ref[h] - dot3(mixed, split(right_ref[h, 1])))
        out_ref[h] = dot3(mixed, split(right_ref[h, 0])) + dot3(reach, split(padd_ref[h]), NT)
        later = jnp.where(is_upper, dot2(reach, pmap_ref[h], NT), 0.0)
        reach_ref[h] = jnp.concatenate(split(later), 1)


def merge_kernel(radix, first, last, place_ref, *refs):
    got_refs, refs = refs[: radix - 1], refs[radix - 1 :]
    own_ref, *refs = refs
    if not first:
        pmap_ref, padd_ref, *refs = refs
    new_map_ref, new_add_ref, send_ref = refs
    heads, _, size, _ = own_ref.shape
    every = range(heads)
    eye = lax.broadcasted_iota(jnp.int32, (size, size), 0) == lax.broadcasted_iota(
        jnp.int32, (size, size), 1
    )

    def join(early, late):
        both = [contract(early[h], late[h][:size], NN) for h in every]
        add = [both[h][size:] + late[h][size:].astype(F32) for h in every]
        return [jnp.concatenate([both[h][:size], add[h]], 0).astype(BF16) for h in every]

    def merge(place):
        refs_in = (own_ref, *got_refs)
        parts = [[refs_in[i ^ place][h].reshape(2 * size, size) for h in every] for i in range(radix)]
        start = jnp.concatenate([jnp.where(eye, 1.0, 0.0), jnp.zeros((size, size), F32)], 0)
        before = [[start.astype(BF16)] * heads, parts[0]]
        if radix == 2:
            total = join(*parts)
        else:
            before.append(join(parts[0], parts[1]))
            total = join(before[2], join(parts[2], parts[3]))
            if place == 3:
                before.append(join(before[2], parts[2]))
        pair = before[place]
        for h in every:
            if first:
                new_map_ref[h] = pair[h][:size]
                new_add_ref[h] = pair[h][size:].astype(F32)
            else:
                both = contract(pair[h], pmap_ref[h], NN)
                new_map_ref[h] = both[:size].astype(BF16)
                new_add_ref[h] = both[size:] + padd_ref[h]
            if last:
                send_ref[h] = total[h][size:]
            else:
                send_ref[h] = total[h].reshape(2, size, size)

    for place in range(radix):
        pl.when(place_ref[0] == place)(functools.partial(merge, place))


def output_kernel(got_ref, local_ref, reach_ref, gain_ref, normed_ref):
    heads, size, _ = got_ref.shape
    for h in range(heads):
        got = jnp.concatenate([got_ref[h]] * 2, 1)
        out = local_ref[h] + contract(reach_ref[h], got, NT)
        scale = lax.rsqrt(jnp.mean(out * out, -1, keepdims=True) + 1e-06)
        normed_ref[:, h * size : (h + 1) * size] = (out * scale * gain_ref[...]).astype(BF16)


def mix_own_kernel(place_ref, wo_hbm, part_ref, out_ref, weight_ref, sem):
    width = weight_ref.shape[1]
    copy = pltpu.make_async_copy(wo_hbm.at[:, block_of(place_ref[0], 0, width)], weight_ref, sem)
    copy.start()
    copy.wait()
    out_ref[...] = contract(part_ref[...], weight_ref[...], NN)


def mix_kernel(n_pieces, base_ref, *refs):
    total = base_ref[...]
    for part, weight in zip(refs[:n_pieces], refs[n_pieces : 2 * n_pieces]):
        total = total + contract(part[...], weight[...], NN)
    refs[-1][...] = total.astype(refs[-1].dtype)


def call(kernel, outs, args, scalars=0, hbm=0, scratch=()):
    vmem = pl.BlockSpec(memory_space=pltpu.VMEM)
    far = pl.BlockSpec(memory_space=pltpu.HBM)
    specs = [pl.BlockSpec(memory_space=pltpu.SMEM)] * scalars + [far] * hbm
    specs += [vmem] * (len(args) - scalars - hbm)
    args = [
        pltpu.with_memory_space_constraint(a, pltpu.HBM) if scalars <= i < scalars + hbm else a
        for i, a in enumerate(args)
    ]
    return pl.pallas_call(
        kernel,
        out_shape=outs,
        in_specs=specs,
        out_specs=[vmem] * len(outs),
        scratch_shapes=scratch,
        compiler_params=pltpu.CompilerParams(vmem_limit_bytes=16 * 1024 * 1024),
    )(*args)


def like(*shape, dtype=F32):
    return jax.ShapeDtypeStruct(shape, dtype)


def shards(n_seq, n_head, tokens, w_query, w_key, w_value, gate_codes, beta_codes, norm_gain, w_out):
    rows, depth = tokens.shape
    heads = gate_codes.shape[1]
    size = norm_gain.shape[0]
    width = w_out.shape[1] // n_head
    place = lax.axis_index("head")
    turn = lax.axis_index("seq")

    def swap(x, axis, count, d):
        return lax.ppermute(x, axis, [(i, i ^ d) for i in range(count)])

    def tie(*x):
        return lax.optimization_barrier(x)

    def spread(x, during):
        d = n_head // 2
        have = {d: swap(x, "head", n_head, d)}
        have[d], extra = tie(have[d], during)
        while d > 1:
            d //= 2
            have.update({e ^ d: swap(have[e], "head", n_head, d) for e in list(have)})
            have[d] = swap(x, "head", n_head, d)
        return [have[d] for d in range(1, n_head)], extra

    here = place.astype(jnp.int32).reshape(1)
    slice_out = like(heads * size, width, dtype=BF16)
    acc, rest, decay, strict, cols, grown, gain, *slices = call(
        functools.partial(prepare_kernel, n_head),
        [
            like(2, rows, heads * size),
            like(n_head - 1, 2, depth, heads * size, dtype=BF16),
            like(heads, rows, rows),
            like(heads, rows, rows),
            like(heads, 3, rows, size),
            like(heads, rows, size),
            like(1, size),
        ]
        + [slice_out] * (n_head - 1),
        [here, tokens, w_key, w_value, w_out, gate_codes.T, beta_codes.T, norm_gain.reshape(1, size)],
        1,
        7,
        [
            pltpu.VMEM((rows, depth), BF16),
            pltpu.VMEM((2, depth, heads * size), BF16),
            pltpu.VMEM((heads, rows), jnp.int32),
            pltpu.VMEM((heads, rows), jnp.int32),
            pltpu.SemaphoreType.DMA((3 + 3 * n_head,)),
        ],
    )
    pieces, (acc, rest) = spread(tokens, (acc, rest))
    (acc,) = call(
        functools.partial(more_kernel, n_head - 2),
        [like(2, rows, heads * size)],
        [acc, rest, *pieces[:-1]],
    )
    state = like(heads, size, size)
    state_sent = like(heads, size, size, dtype=BF16)
    pair_sent = like(heads, 2, size, size, dtype=BF16)
    send, keys, inverse, right = call(
        functools.partial(summary_kernel, size),
        [pair_sent, like(heads, rows, size), like(heads, rows, rows), like(heads, 2, rows, size)],
        [acc, rest, pieces[-1], strict, cols, grown],
    )
    send, *slices = tie(send, *slices)
    out_weights = [swap(slices[d - 1], "head", n_head, d) for d in range(1, n_head)]
    prefix = []
    d = 1
    while 2 * d < n_seq:
        radix = 4 if 4 * d < n_seq else 2
        last = 2 * radix * d >= n_seq
        got = [swap(send, "seq", n_seq, i * d) for i in reversed(range(1, radix))][::-1]
        place_in = ((turn // d) % radix).astype(jnp.int32).reshape(1)
        outs = [state_sent, state, state_sent if last else pair_sent]
        *prefix, send = call(
            functools.partial(merge_kernel, radix, d == 1, last),
            outs,
            [place_in, *got, send, *prefix],
            1,
        )
        d *= radix
    got = swap(send, "seq", n_seq, d)
    upper = ((turn // d) % 2).astype(jnp.int32).reshape(1)
    local, reach = call(
        functools.partial(local_kernel, n_head, size),
        [like(heads, rows, size), like(heads, rows, 2 * size, dtype=BF16)],
        [here, upper, w_query, tokens, *pieces, decay, grown, keys, inverse, right, *prefix],
        2,
        2,
        [
            pltpu.VMEM((n_head, depth, heads * size), BF16),
            pltpu.VMEM((rows, depth), BF16),
            pltpu.SemaphoreType.DMA((n_head + 1,)),
        ],
    )
    got, local, reach = tie(got, local, reach)
    (normed,) = call(
        output_kernel,
        [like(rows, heads * size, dtype=BF16)],
        [got, local, reach, gain],
    )
    (mixed,) = call(
        mix_own_kernel,
        [like(rows, width)],
        [here, w_out, normed],
        1,
        1,
        [pltpu.VMEM((heads * size, width), BF16), pltpu.SemaphoreType.DMA(())],
    )
    parts, mixed = spread(normed, mixed)
    (mixed,) = call(
        functools.partial(mix_kernel, n_head - 2),
        [like(rows, width)],
        [mixed, *parts[:-1], *out_weights[:-1]],
    )
    return call(
        functools.partial(mix_kernel, 1),
        [like(rows, width, dtype=BF16)],
        [mixed, parts[-1], out_weights[-1]],
    )[0]


def solution(mesh):
    n_seq, n_head = mesh.shape["seq"], mesh.shape["head"]
    return jax.shard_map(
        functools.partial(shards, n_seq, n_head),
        mesh=mesh,
        in_specs=(
            P("seq", "head"),
            P(None, "head"),
            P(None, "head"),
            P(None, "head"),
            P("seq", "head"),
            P("seq", "head"),
            P(),
            P("head", None),
        ),
        out_specs=P("seq", "head"),
        check_vma=False,
    )
```

```python
import functools
import jax
import jax.numpy as jnp
from jax import lax
from jax.experimental import pallas as pl
from jax.experimental.pallas import tpu as pltpu
from jax.sharding import PartitionSpec as P

BASE = 16
F32 = jnp.float32
BF16 = jnp.bfloat16


def split(x):
    high = x.astype(BF16)
    return high, (x - high.astype(F32)).astype(BF16)


def contract(a, b, dims):
    return lax.dot_general(a, b, (dims, ((), ())), preferred_element_type=F32)


NN = ((1,), (0,))
NT = ((1,), (1,))


def dot3(a, b, dims=NN):
    left = jnp.concatenate([a[0], a[1], a[0]], dims[0][0])
    right = jnp.concatenate([b[0], b[0], b[1]], dims[1][0])
    return contract(left, right, dims)


def dot2(a, b, dims=NN):
    return contract(
        jnp.concatenate(a, dims[0][0]), jnp.concatenate([b, b], dims[1][0]), dims
    )


def gate_tables(codes, beta, decay_ref, strict_ref, cols_ref, grown_ref):
    heads, rows = codes.shape
    tok = lax.broadcasted_iota(jnp.int32, (rows, rows), 0)
    other = lax.broadcasted_iota(jnp.int32, (rows, rows), 1)
    ones = jnp.where(tok <= other, 1.0, 0.0).astype(BF16)
    sums = [
        contract(p.astype(F32).astype(BF16), ones, NN)
        for p in (codes >> 14, (codes >> 7) & 127, codes & 127)
    ]
    logs = -(sums[0] * 16384.0 + sums[1] * 128.0 + sums[2]) / 2097152.0
    beta = beta.astype(F32) / 256.0
    logs_t = jnp.transpose(logs)
    beta_t = jnp.transpose(beta)
    for h in range(heads):
        row = logs[h : h + 1, :]
        col = jnp.broadcast_to(logs_t[:, h : h + 1], (rows, rows))
        gap = col - row
        decay_ref[h] = jnp.where(tok >= other, jnp.exp(jnp.where(tok >= other, gap, 0.0)), 0.0)
        grown = jnp.exp(col)
        beta_col = jnp.broadcast_to(beta_t[:, h : h + 1], (rows, rows))
        strict_ref[h] = jnp.where(tok > other, decay_ref[h] * beta_col, 0.0)
        grown_ref[h] = grown
        cols_ref[h, 0] = beta_col * grown
        cols_ref[h, 1] = beta_col
        cols_ref[h, 2] = jnp.exp(row[:, rows - 1 :] - col)


def copy_all(moves, sems):
    copies = [pltpu.make_async_copy(a, b, sems.at[i]) for i, (a, b) in enumerate(moves)]
    for copy in copies:
        copy.start()
    return copies


def block_of(place, d, depth):
    return pl.ds(pl.multiple_of((place ^ d) * depth, depth), depth)


def out_slices(place, wo_hbm, out_refs, first):
    width = out_refs[0].shape[1]
    return [
        (wo_hbm.at[:, block_of(place, first + i, width)], ref) for i, ref in enumerate(out_refs)
    ]


def prepare_kernel(n_head, place_ref, tok_hbm, wk_hbm, wv_hbm, wo_hbm, gate_hbm, beta_hbm, gain_hbm, *refs):
    acc_ref, rest_ref, decay_ref, strict_ref, cols_ref, grown_ref, gain_ref = refs[:7]
    out_refs = refs[7:-5]
    tok_ref, own_ref, gate_ref, beta_ref, sems = refs[-5:]
    place = place_ref[0]
    depth = tok_ref.shape[1]
    weights = (wk_hbm, wv_hbm)
    moves = [(gate_hbm, gate_ref), (beta_hbm, beta_ref), (gain_hbm, gain_ref), (tok_hbm, tok_ref)]
    moves += [(w.at[block_of(place, 0, depth), :], own_ref.at[i]) for i, w in enumerate(weights)]
    moves += [
        (w.at[block_of(place, d, depth), :], rest_ref.at[d - 1, i])
        for d in range(1, n_head)
        for i, w in enumerate(weights)
    ]
    moves += out_slices(place, wo_hbm, out_refs, n_head - len(out_refs))
    copies = copy_all(moves, sems)
    copies[0].wait()
    copies[1].wait()
    gate_tables(gate_ref[...], beta_ref[...], decay_ref, strict_ref, cols_ref, grown_ref)
    for copy in copies[2:6]:
        copy.wait()
    for i in range(len(weights)):
        acc_ref[i] = contract(tok_ref[...], own_ref[i], NN)
    for copy in copies[6:]:
        copy.wait()


def more_kernel(n_pieces, acc_ref, rest_ref, *refs):
    out_ref = refs[-1]
    for i in range(acc_ref.shape[0]):
        total = acc_ref[i]
        for d in range(n_pieces):
            total = total + contract(refs[d][...], rest_ref[d, i], NN)
        out_ref[i] = total


def solve_lower(lowers, rights):
    rows = lowers[0].shape[0]
    blocks = rows // BASE
    tok = lax.broadcasted_iota(jnp.int32, (rows, rows), 0)
    other = lax.broadcasted_iota(jnp.int32, (rows, rows), 1)
    lane = lax.broadcasted_iota(jnp.int32, (BASE, rows), 1)
    sub = lax.broadcasted_iota(jnp.int32, (BASE, rows), 0)
    diagonal = []
    for lower in lowers:
        compact = jnp.zeros((BASE, rows), F32)
        for b in range(blocks):
            compact = compact + jnp.where(
                lane // BASE == b, lower[b * BASE : (b + 1) * BASE, :], 0.0
            )
        solved = jnp.where(sub == lane % BASE, 1.0, 0.0)
        for j in range(BASE - 1):
            column = jnp.take_along_axis(compact, (lane // BASE) * BASE + j, axis=1)
            solved = solved - column * solved[j : j + 1, :]
        inside = tok // BASE == other // BASE
        diagonal.append(split(jnp.where(inside, jnp.concatenate([solved] * blocks, 0), 0.0)))
    results = [dot3(d, r) for d, r in zip(diagonal, rights)]
    if blocks == 1:
        return results
    step = [
        dot3(d, split(jnp.where(tok // BASE == other // BASE, 0.0, lower)))
        for d, lower in zip(diagonal, lowers)
    ]
    step = [split(x) for x in step]
    covered = 1
    while True:
        top = covered * BASE
        lowest = [tuple(part[top:] for part in v) for v in step]
        sign = -1.0 if covered == 1 else 1.0
        changes = [dot3(v, split(x)) for v, x in zip(lowest, results)]
        results = [
            jnp.concatenate([x[:top], x[top:] + sign * change], 0)
            for x, change in zip(results, changes)
        ]
        covered *= 2
        if covered >= blocks:
            return results
        powers = [dot3(tuple(part[covered * BASE :] for part in v), v) for v in step]
        empty = jnp.zeros((covered * BASE, rows), F32)
        step = [split(jnp.concatenate([empty, power], 0)) for power in powers]


def summary_kernel(size, acc_ref, rest_ref, piece_ref, strict_ref, cols_ref, grown_ref, send_ref, keys_ref, wy_ref):
    heads, rows, _ = strict_ref.shape
    last = rest_ref.shape[0] - 1
    keys = acc_ref[0] + contract(piece_ref[...], rest_ref[last, 0], NN)
    values = acc_ref[1] + contract(piece_ref[...], rest_ref[last, 1], NN)
    every = range(heads)
    each = [keys[:, h * size : (h + 1) * size] for h in every]
    scales = [lax.rsqrt(jnp.sum(key * key, -1, keepdims=True) + 1e-06) for key in each]
    each = [key * scale for key, scale in zip(each, scales)]
    halves = [split(key) for key in each]
    lowers = [dot3(halves[h], halves[h], NT) * strict_ref[h] for h in every]
    tails = [split(jnp.transpose(each[h] * cols_ref[h, 2])) for h in every]
    rights = [
        jnp.concatenate(
            [each[h] * cols_ref[h, 0], values[:, h * size : (h + 1) * size] * cols_ref[h, 1]], 1
        )
        for h in every
    ]
    solved = solve_lower(lowers, [split(right) for right in rights])
    eye = lax.broadcasted_iota(jnp.int32, (size, size), 0) == lax.broadcasted_iota(
        jnp.int32, (size, size), 1
    )
    both = [dot3(tails[h], split(solved[h])) for h in every]
    for h in every:
        step = jnp.where(eye, grown_ref[h, rows - 1 :, :], 0.0) - both[h][:, :size]
        send_ref[h, :, :size] = step.astype(BF16)
        send_ref[h, :, size:] = both[h][:, size:].astype(BF16)
        keys_ref[h] = each[h]
        wy_ref[h] = solved[h]


def local_kernel(n_head, size, place_ref, upper_ref, wq_hbm, tok_hbm, *refs):
    pieces = refs[: n_head - 1]
    decay_ref, grown_ref, keys_ref, wy_ref, pmap_ref, padd_ref = refs[n_head - 1 : n_head + 5]
    out_ref, reach_ref, wq_ref, tok_ref, sems = refs[n_head + 5 :]
    heads = decay_ref.shape[0]
    depth = tok_ref.shape[1]
    moves = [(tok_hbm, tok_ref)]
    moves += [
        (wq_hbm.at[block_of(place_ref[0], d, depth), :], wq_ref.at[d]) for d in range(n_head)
    ]
    for copy in copy_all(moves, sems):
        copy.wait()
    queries = contract(tok_ref[...], wq_ref[0], NN)
    for d in range(1, n_head):
        queries = queries + contract(pieces[d - 1][...], wq_ref[d], NN)
    is_upper = upper_ref[0] > 0
    for h in range(heads):
        query = queries[:, h * size : (h + 1) * size]
        dots = dot3(split(query), split(keys_ref[h]), NT) * decay_ref[h]
        both = dot3(split(dots), split(wy_ref[h]))
        reach = split(query * grown_ref[h] - both[:, :size])
        out_ref[h] = both[:, size:] + dot3(reach, split(padd_ref[h]))
        later = jnp.where(is_upper, dot2(reach, pmap_ref[h]), 0.0)
        reach_ref[h] = jnp.concatenate(split(later), 1)


def merge_kernel(radix, first, last, place_ref, *refs):
    got_refs, refs = refs[: radix - 1], refs[radix - 1 :]
    own_ref, *refs = refs
    if not first:
        pmap_ref, padd_ref, *refs = refs
    new_map_ref, new_add_ref, send_ref = refs
    heads, size, _ = own_ref.shape
    every = range(heads)
    eye = lax.broadcasted_iota(jnp.int32, (size, size), 0) == lax.broadcasted_iota(
        jnp.int32, (size, size), 1
    )

    def join(early, late):
        both = [contract(late[h][:, :size], early[h], NN) for h in every]
        add = [both[h][:, size:] + late[h][:, size:].astype(F32) for h in every]
        return [jnp.concatenate([both[h][:, :size], add[h]], 1).astype(BF16) for h in every]

    def merge(place):
        refs_in = (own_ref, *got_refs)
        parts = [[refs_in[i ^ place][h] for h in every] for i in range(radix)]
        start = jnp.concatenate([jnp.where(eye, 1.0, 0.0), jnp.zeros((size, size), F32)], 1)
        before = [[start.astype(BF16)] * heads, parts[0]]
        if radix == 2:
            total = join(*parts)
        else:
            before.append(join(parts[0], parts[1]))
            total = join(before[2], join(parts[2], parts[3]))
            if place == 3:
                before.append(join(before[2], parts[2]))
        pair = before[place]
        for h in every:
            if first:
                new_map_ref[h] = pair[h][:, :size]
                new_add_ref[h] = pair[h][:, size:].astype(F32)
            else:
                both = contract(pmap_ref[h], pair[h], NN)
                new_map_ref[h] = both[:, :size].astype(BF16)
                new_add_ref[h] = both[:, size:] + padd_ref[h]
            send_ref[h] = total[h][:, size:] if last else total[h]

    for place in range(radix):
        pl.when(place_ref[0] == place)(functools.partial(merge, place))


def output_kernel(got_ref, local_ref, reach_ref, gain_ref, normed_ref):
    heads, size, _ = got_ref.shape
    for h in range(heads):
        got = jnp.concatenate([got_ref[h]] * 2, 0)
        out = local_ref[h] + contract(reach_ref[h], got, NN)
        scale = lax.rsqrt(jnp.mean(out * out, -1, keepdims=True) + 1e-06)
        normed_ref[:, h * size : (h + 1) * size] = (out * scale * gain_ref[...]).astype(BF16)


def mix_own_kernel(place_ref, wo_hbm, part_ref, out_ref, weight_ref, sem):
    width = weight_ref.shape[1]
    copy = pltpu.make_async_copy(wo_hbm.at[:, block_of(place_ref[0], 0, width)], weight_ref, sem)
    copy.start()
    copy.wait()
    out_ref[...] = contract(part_ref[...], weight_ref[...], NN)


def mix_kernel(n_pieces, base_ref, *refs):
    total = base_ref[...]
    for part, weight in zip(refs[:n_pieces], refs[n_pieces : 2 * n_pieces]):
        total = total + contract(part[...], weight[...], NN)
    refs[-1][...] = total.astype(refs[-1].dtype)


def call(kernel, outs, args, scalars=0, hbm=0, scratch=()):
    vmem = pl.BlockSpec(memory_space=pltpu.VMEM)
    far = pl.BlockSpec(memory_space=pltpu.HBM)
    specs = [pl.BlockSpec(memory_space=pltpu.SMEM)] * scalars + [far] * hbm
    specs += [vmem] * (len(args) - scalars - hbm)
    args = [
        pltpu.with_memory_space_constraint(a, pltpu.HBM) if scalars <= i < scalars + hbm else a
        for i, a in enumerate(args)
    ]
    return pl.pallas_call(
        kernel,
        out_shape=outs,
        in_specs=specs,
        out_specs=[vmem] * len(outs),
        scratch_shapes=scratch,
        compiler_params=pltpu.CompilerParams(vmem_limit_bytes=16 * 1024 * 1024),
    )(*args)


def like(*shape, dtype=F32):
    return jax.ShapeDtypeStruct(shape, dtype)


def shards(n_seq, n_head, tokens, w_query, w_key, w_value, gate_codes, beta_codes, norm_gain, w_out):
    rows, depth = tokens.shape
    heads = gate_codes.shape[1]
    size = norm_gain.shape[0]
    width = w_out.shape[1] // n_head
    place = lax.axis_index("head")
    turn = lax.axis_index("seq")

    def swap(x, axis, count, d):
        return lax.ppermute(x, axis, [(i, i ^ d) for i in range(count)])

    def tie(*x):
        return lax.optimization_barrier(x)

    def spread(x, during):
        d = n_head // 2
        have = {d: swap(x, "head", n_head, d)}
        have[d], extra = tie(have[d], during)
        while d > 1:
            d //= 2
            have.update({e ^ d: swap(have[e], "head", n_head, d) for e in list(have)})
            have[d] = swap(x, "head", n_head, d)
        return [have[d] for d in range(1, n_head)], extra

    here = place.astype(jnp.int32).reshape(1)
    slice_out = like(heads * size, width, dtype=BF16)
    acc, rest, decay, strict, cols, grown, gain, *slices = call(
        functools.partial(prepare_kernel, n_head),
        [
            like(2, rows, heads * size),
            like(n_head - 1, 2, depth, heads * size, dtype=BF16),
            like(heads, rows, rows),
            like(heads, rows, rows),
            like(heads, 3, rows, size),
            like(heads, rows, size),
            like(1, size),
        ]
        + [slice_out] * (n_head - 1),
        [here, tokens, w_key, w_value, w_out, gate_codes.T, beta_codes.T, norm_gain.reshape(1, size)],
        1,
        7,
        [
            pltpu.VMEM((rows, depth), BF16),
            pltpu.VMEM((2, depth, heads * size), BF16),
            pltpu.VMEM((heads, rows), jnp.int32),
            pltpu.VMEM((heads, rows), jnp.int32),
            pltpu.SemaphoreType.DMA((3 + 3 * n_head,)),
        ],
    )
    pieces, (acc, rest) = spread(tokens, (acc, rest))
    (acc,) = call(
        functools.partial(more_kernel, n_head - 2),
        [like(2, rows, heads * size)],
        [acc, rest, *pieces[:-1]],
    )
    state = like(heads, size, size)
    state_sent = like(heads, size, size, dtype=BF16)
    pair_sent = like(heads, size, 2 * size, dtype=BF16)
    send, keys, solved = call(
        functools.partial(summary_kernel, size),
        [pair_sent, like(heads, rows, size), like(heads, rows, 2 * size)],
        [acc, rest, pieces[-1], strict, cols, grown],
    )
    send, *slices = tie(send, *slices)
    out_weights = [swap(slices[d - 1], "head", n_head, d) for d in range(1, n_head)]
    prefix = []
    d = 1
    while 2 * d < n_seq:
        radix = 4 if 4 * d < n_seq else 2
        last = 2 * radix * d >= n_seq
        got = [swap(send, "seq", n_seq, i * d) for i in reversed(range(1, radix))][::-1]
        place_in = ((turn // d) % radix).astype(jnp.int32).reshape(1)
        outs = [state_sent, state, state_sent if last else pair_sent]
        *prefix, send = call(
            functools.partial(merge_kernel, radix, d == 1, last),
            outs,
            [place_in, *got, send, *prefix],
            1,
        )
        d *= radix
    got = swap(send, "seq", n_seq, d)
    upper = ((turn // d) % 2).astype(jnp.int32).reshape(1)
    local, reach = call(
        functools.partial(local_kernel, n_head, size),
        [like(heads, rows, size), like(heads, rows, 2 * size, dtype=BF16)],
        [here, upper, w_query, tokens, *pieces, decay, grown, keys, solved, *prefix],
        2,
        2,
        [
            pltpu.VMEM((n_head, depth, heads * size), BF16),
            pltpu.VMEM((rows, depth), BF16),
            pltpu.SemaphoreType.DMA((n_head + 1,)),
        ],
    )
    got, local, reach = tie(got, local, reach)
    (normed,) = call(
        output_kernel,
        [like(rows, heads * size, dtype=BF16)],
        [got, local, reach, gain],
    )
    (mixed,) = call(
        mix_own_kernel,
        [like(rows, width)],
        [here, w_out, normed],
        1,
        1,
        [pltpu.VMEM((heads * size, width), BF16), pltpu.SemaphoreType.DMA(())],
    )
    parts, mixed = spread(normed, mixed)
    (mixed,) = call(
        functools.partial(mix_kernel, n_head - 2),
        [like(rows, width)],
        [mixed, *parts[:-1], *out_weights[:-1]],
    )
    return call(
        functools.partial(mix_kernel, 1),
        [like(rows, width, dtype=BF16)],
        [mixed, parts[-1], out_weights[-1]],
    )[0]


def solution(mesh):
    n_seq, n_head = mesh.shape["seq"], mesh.shape["head"]
    return jax.shard_map(
        functools.partial(shards, n_seq, n_head),
        mesh=mesh,
        in_specs=(
            P("seq", "head"),
            P(None, "head"),
            P(None, "head"),
            P(None, "head"),
            P("seq", "head"),
            P("seq", "head"),
            P(),
            P("head", None),
        ),
        out_specs=P("seq", "head"),
        check_vma=False,
    )
```

```python
import functools
import jax
import jax.numpy as jnp
from jax import lax
from jax.experimental import pallas as pl
from jax.experimental.pallas import tpu as pltpu
from jax.sharding import PartitionSpec as P

BASE = 16
F32 = jnp.float32
BF16 = jnp.bfloat16


def split(x):
    high = x.astype(BF16)
    return high, (x - high.astype(F32)).astype(BF16)


def contract(a, b, dims):
    return lax.dot_general(a, b, (dims, ((), ())), preferred_element_type=F32)


NN = ((1,), (0,))
NT = ((1,), (1,))


def dot3(a, b, dims=NN):
    left = jnp.concatenate([a[0], a[1], a[0]], dims[0][0])
    right = jnp.concatenate([b[0], b[0], b[1]], dims[1][0])
    return contract(left, right, dims)


def dot2(a, b, dims=NN):
    return contract(
        jnp.concatenate(a, dims[0][0]), jnp.concatenate([b, b], dims[1][0]), dims
    )


def gate_tables(codes, beta, decay_ref, strict_ref, cols_ref, grown_ref):
    heads, rows = codes.shape
    tok = lax.broadcasted_iota(jnp.int32, (rows, rows), 0)
    other = lax.broadcasted_iota(jnp.int32, (rows, rows), 1)
    ones = jnp.where(tok <= other, 1.0, 0.0).astype(BF16)
    sums = [
        contract(p.astype(F32).astype(BF16), ones, NN)
        for p in (codes >> 14, (codes >> 7) & 127, codes & 127)
    ]
    logs = -(sums[0] * 16384.0 + sums[1] * 128.0 + sums[2]) / 2097152.0
    beta = beta.astype(F32) / 256.0
    logs_t = jnp.transpose(logs)
    beta_t = jnp.transpose(beta)
    for h in range(heads):
        row = logs[h : h + 1, :]
        col = jnp.broadcast_to(logs_t[:, h : h + 1], (rows, rows))
        gap = col - row
        decay_ref[h] = jnp.where(tok >= other, jnp.exp(jnp.where(tok >= other, gap, 0.0)), 0.0)
        grown = jnp.exp(col)
        beta_col = jnp.broadcast_to(beta_t[:, h : h + 1], (rows, rows))
        strict_ref[h] = jnp.where(tok > other, decay_ref[h] * beta_col, 0.0)
        grown_ref[h] = grown
        cols_ref[h, 0] = beta_col * grown
        cols_ref[h, 1] = beta_col
        cols_ref[h, 2] = jnp.exp(row[:, rows - 1 :] - col)


def copy_all(moves, sems):
    copies = [pltpu.make_async_copy(a, b, sems.at[i]) for i, (a, b) in enumerate(moves)]
    for copy in copies:
        copy.start()
    return copies


def block_of(place, d, depth):
    return pl.ds(pl.multiple_of((place ^ d) * depth, depth), depth)


def out_slices(place, wo_hbm, out_refs, first):
    width = out_refs[0].shape[1]
    return [
        (wo_hbm.at[:, block_of(place, first + i, width)], ref) for i, ref in enumerate(out_refs)
    ]


def prepare_kernel(n_head, place_ref, tok_hbm, wk_hbm, wv_hbm, wo_hbm, gate_hbm, beta_hbm, gain_hbm, *refs):
    acc_ref, rest_ref, decay_ref, strict_ref, cols_ref, grown_ref, gain_ref = refs[:7]
    out_refs = refs[7:-5]
    tok_ref, own_ref, gate_ref, beta_ref, sems = refs[-5:]
    place = place_ref[0]
    depth = tok_ref.shape[1]
    weights = (wk_hbm, wv_hbm)
    moves = [(gate_hbm, gate_ref), (beta_hbm, beta_ref), (gain_hbm, gain_ref), (tok_hbm, tok_ref)]
    moves += [(w.at[block_of(place, 0, depth), :], own_ref.at[i]) for i, w in enumerate(weights)]
    moves += [
        (w.at[block_of(place, d, depth), :], rest_ref.at[d - 1, i])
        for d in range(1, n_head)
        for i, w in enumerate(weights)
    ]
    moves += out_slices(place, wo_hbm, out_refs, n_head - len(out_refs))
    copies = copy_all(moves, sems)
    copies[0].wait()
    copies[1].wait()
    gate_tables(gate_ref[...], beta_ref[...], decay_ref, strict_ref, cols_ref, grown_ref)
    for copy in copies[2:6]:
        copy.wait()
    for i in range(len(weights)):
        acc_ref[i] = contract(tok_ref[...], own_ref[i], NN)
    for copy in copies[6:]:
        copy.wait()


def more_kernel(n_pieces, acc_ref, rest_ref, *refs):
    out_ref = refs[-1]
    for i in range(acc_ref.shape[0]):
        total = acc_ref[i]
        for d in range(n_pieces):
            total = total + contract(refs[d][...], rest_ref[d, i], NN)
        out_ref[i] = total


def solve_lower(lowers, rights):
    rows = lowers[0].shape[0]
    blocks = rows // BASE
    tok = lax.broadcasted_iota(jnp.int32, (rows, rows), 0)
    other = lax.broadcasted_iota(jnp.int32, (rows, rows), 1)
    lane = lax.broadcasted_iota(jnp.int32, (BASE, rows), 1)
    sub = lax.broadcasted_iota(jnp.int32, (BASE, rows), 0)
    diagonal = []
    for lower in lowers:
        compact = jnp.zeros((BASE, rows), F32)
        for b in range(blocks):
            compact = compact + jnp.where(
                lane // BASE == b, lower[b * BASE : (b + 1) * BASE, :], 0.0
            )
        solved = jnp.where(sub == lane % BASE, 1.0, 0.0)
        for j in range(BASE - 1):
            column = jnp.take_along_axis(compact, (lane // BASE) * BASE + j, axis=1)
            solved = solved - column * solved[j : j + 1, :]
        inside = tok // BASE == other // BASE
        diagonal.append(split(jnp.where(inside, jnp.concatenate([solved] * blocks, 0), 0.0)))
    results = [dot3(d, r) for d, r in zip(diagonal, rights)]
    if blocks == 1:
        return results
    step = [
        dot3(d, split(jnp.where(tok // BASE == other // BASE, 0.0, lower)))
        for d, lower in zip(diagonal, lowers)
    ]
    step = [split(x) for x in step]
    covered = 1
    while True:
        top = covered * BASE
        lowest = [tuple(part[top:] for part in v) for v in step]
        sign = -1.0 if covered == 1 else 1.0
        changes = [dot3(v, split(x)) for v, x in zip(lowest, results)]
        results = [
            jnp.concatenate([x[:top], x[top:] + sign * change], 0)
            for x, change in zip(results, changes)
        ]
        covered *= 2
        if covered >= blocks:
            return results
        powers = [dot3(tuple(part[covered * BASE :] for part in v), v) for v in step]
        empty = jnp.zeros((covered * BASE, rows), F32)
        step = [split(jnp.concatenate([empty, power], 0)) for power in powers]


def summary_kernel(size, acc_ref, rest_ref, piece_ref, strict_ref, cols_ref, grown_ref, send_ref, keys_ref, wy_ref):
    heads, rows, _ = strict_ref.shape
    last = rest_ref.shape[0] - 1
    keys = acc_ref[0] + contract(piece_ref[...], rest_ref[last, 0], NN)
    values = acc_ref[1] + contract(piece_ref[...], rest_ref[last, 1], NN)
    every = range(heads)
    each = [keys[:, h * size : (h + 1) * size] for h in every]
    scales = [lax.rsqrt(jnp.sum(key * key, -1, keepdims=True) + 1e-06) for key in each]
    each = [key * scale for key, scale in zip(each, scales)]
    halves = [split(key) for key in each]
    lowers = [dot3(halves[h], halves[h], NT) * strict_ref[h] for h in every]
    tails = [split(jnp.transpose(each[h] * cols_ref[h, 2])) for h in every]
    rights = [
        jnp.concatenate(
            [each[h] * cols_ref[h, 0], values[:, h * size : (h + 1) * size] * cols_ref[h, 1]], 1
        )
        for h in every
    ]
    solved = solve_lower(lowers, [split(right) for right in rights])
    eye = lax.broadcasted_iota(jnp.int32, (size, size), 0) == lax.broadcasted_iota(
        jnp.int32, (size, size), 1
    )
    both = [dot3(tails[h], split(solved[h])) for h in every]
    for h in every:
        step = jnp.where(eye, grown_ref[h, rows - 1 :, :], 0.0) - both[h][:, :size]
        send_ref[h, :, :size] = step.astype(BF16)
        send_ref[h, :, size:] = both[h][:, size:].astype(BF16)
        keys_ref[h] = each[h]
        wy_ref[h] = solved[h]


def join(early, late):
    every = range(len(early))
    size = early[0].shape[0]
    both = [contract(late[h][:, :size], early[h], NN) for h in every]
    add = [both[h][:, size:] + late[h][:, size:].astype(F32) for h in every]
    return [jnp.concatenate([both[h][:, :size], add[h]], 1).astype(BF16) for h in every]


def parts_of(place, odd, own_ref, got_refs):
    refs = [own_ref, *got_refs]
    if odd:
        refs[1], refs[2] = refs[2], refs[1]
    return [[refs[i ^ place][h] for h in range(own_ref.shape[0])] for i in range(len(refs))]


def total_of(parts):
    if len(parts) == 2:
        return join(*parts)
    return join(join(parts[0], parts[1]), join(parts[2], parts[3]))


def before(place, parts):
    if place:
        pair = parts[0]
        for part in parts[1:place]:
            pair = join(pair, part)
        return pair
    size = parts[0][0].shape[0]
    row = lax.broadcasted_iota(jnp.int32, (size, 2 * size), 0)
    column = lax.broadcasted_iota(jnp.int32, (size, 2 * size), 1)
    return [jnp.where(row == column, 1.0, 0.0).astype(BF16)] * len(parts[0])


def at_place(radix, place_ref, run):
    for place in range(radix):
        for odd in range(2 if radix > 2 else 1):
            pl.when(place_ref[0] == place + radix * odd)(functools.partial(run, place, odd))


def enter(pair, new_map_ref, new_add_ref, pmap_ref=None, padd_ref=None):
    size = new_map_ref.shape[1]
    for h in range(len(pair)):
        if pmap_ref is None:
            new_map_ref[h] = pair[h][:, :size]
            new_add_ref[h] = pair[h][:, size:].astype(F32)
        else:
            both = contract(pmap_ref[h], pair[h], NN)
            new_map_ref[h] = both[:, :size].astype(BF16)
            new_add_ref[h] = both[:, size:] + padd_ref[h]


def merge_kernel(radix, place_ref, *refs):
    got_refs, own_ref, prefix_refs = refs[: radix - 1], refs[radix - 1], refs[radix:-3]
    new_map_ref, new_add_ref, send_ref = refs[-3:]

    def run(place, odd):
        parts = parts_of(place, odd, own_ref, got_refs)
        total = total_of(parts)
        enter(before(place, parts), new_map_ref, new_add_ref, *prefix_refs)
        for h in range(len(total)):
            send_ref[h] = total[h]

    at_place(radix, place_ref, run)


def total_kernel(radix, place_ref, *refs):
    got_refs, own_ref, send_ref = refs[: radix - 1], refs[radix - 1], refs[-1]
    heads, size, _ = own_ref.shape

    def follow(early, late):
        return [
            (contract(late[h][:, :size], early[h], NN) + late[h][:, size:].astype(F32)).astype(BF16)
            for h in range(heads)
        ]

    def run(place, odd):
        parts = parts_of(place, odd, own_ref, got_refs)
        add = follow([part[:, size:] for part in parts[0]], parts[1])
        if radix > 2:
            add = follow(add, join(parts[2], parts[3]))
        for h in range(heads):
            send_ref[h] = add[h]

    at_place(radix, place_ref, run)


def local_kernel(n_head, radix, place_ref, upper_ref, turn_ref, wq_hbm, tok_hbm, *refs):
    pieces, refs = refs[: n_head - 1], refs[n_head - 1 :]
    decay_ref, grown_ref, keys_ref, wy_ref, *refs = refs
    got_refs, own_ref, prefix_refs = refs[: radix - 1], refs[radix - 1], refs[radix:-7]
    out_ref, reach_ref, wq_ref, tok_ref, pmap_ref, padd_ref, sems = refs[-7:]
    heads, size, _ = padd_ref.shape
    every = range(heads)
    depth = tok_ref.shape[1]
    moves = [(tok_hbm, tok_ref)]
    moves += [
        (wq_hbm.at[block_of(place_ref[0], d, depth), :], wq_ref.at[d]) for d in range(n_head)
    ]
    copies = copy_all(moves, sems)

    def run(place, odd):
        parts = parts_of(place, odd, own_ref, got_refs)
        enter(before(place, parts), pmap_ref, padd_ref, *prefix_refs)

    at_place(radix, turn_ref, run)
    for copy in copies:
        copy.wait()
    queries = contract(tok_ref[...], wq_ref[0], NN)
    for d in range(1, n_head):
        queries = queries + contract(pieces[d - 1][...], wq_ref[d], NN)
    is_upper = upper_ref[0] > 0
    queries = [queries[:, h * size : (h + 1) * size] for h in every]
    dots = [dot3(split(queries[h]), split(keys_ref[h]), NT) * decay_ref[h] for h in every]
    both = [dot3(split(dots[h]), split(wy_ref[h])) for h in every]
    reach = [split(queries[h] * grown_ref[h] - both[h][:, :size]) for h in every]
    out = [both[h][:, size:] + dot3(reach[h], split(padd_ref[h])) for h in every]
    later = [jnp.where(is_upper, dot2(reach[h], pmap_ref[h]), 0.0) for h in every]
    for h in every:
        out_ref[h] = out[h]
        reach_ref[h] = jnp.concatenate(split(later[h]), 1)


def output_kernel(got_ref, local_ref, reach_ref, gain_ref, normed_ref):
    heads, size, _ = got_ref.shape
    for h in range(heads):
        got = jnp.concatenate([got_ref[h]] * 2, 0)
        out = local_ref[h] + contract(reach_ref[h], got, NN)
        scale = lax.rsqrt(jnp.mean(out * out, -1, keepdims=True) + 1e-06)
        normed_ref[:, h * size : (h + 1) * size] = (out * scale * gain_ref[...]).astype(BF16)


def mix_own_kernel(place_ref, wo_hbm, part_ref, out_ref, weight_ref, sem):
    width = weight_ref.shape[1]
    copy = pltpu.make_async_copy(wo_hbm.at[:, block_of(place_ref[0], 0, width)], weight_ref, sem)
    copy.start()
    copy.wait()
    out_ref[...] = contract(part_ref[...], weight_ref[...], NN)


def mix_kernel(n_pieces, base_ref, *refs):
    total = base_ref[...]
    for part, weight in zip(refs[:n_pieces], refs[n_pieces : 2 * n_pieces]):
        total = total + contract(part[...], weight[...], NN)
    refs[-1][...] = total.astype(refs[-1].dtype)


def call(kernel, outs, args, scalars=0, hbm=0, scratch=()):
    vmem = pl.BlockSpec(memory_space=pltpu.VMEM)
    far = pl.BlockSpec(memory_space=pltpu.HBM)
    specs = [pl.BlockSpec(memory_space=pltpu.SMEM)] * scalars + [far] * hbm
    specs += [vmem] * (len(args) - scalars - hbm)
    args = [
        pltpu.with_memory_space_constraint(a, pltpu.HBM) if scalars <= i < scalars + hbm else a
        for i, a in enumerate(args)
    ]
    return pl.pallas_call(
        kernel,
        out_shape=outs,
        in_specs=specs,
        out_specs=[vmem] * len(outs),
        scratch_shapes=scratch,
        compiler_params=pltpu.CompilerParams(vmem_limit_bytes=16 * 1024 * 1024),
    )(*args)


def like(*shape, dtype=F32):
    return jax.ShapeDtypeStruct(shape, dtype)


def shards(n_seq, n_head, tokens, w_query, w_key, w_value, gate_codes, beta_codes, norm_gain, w_out):
    rows, depth = tokens.shape
    heads = gate_codes.shape[1]
    size = norm_gain.shape[0]
    width = w_out.shape[1] // n_head
    place = lax.axis_index("head")
    turn = lax.axis_index("seq")

    def swap(x, axis, count, d):
        return lax.ppermute(x, axis, [(i, i ^ d) for i in range(count)])

    def swap_two(x, even, odd):
        pairs = [
            (i * n_head + j, (i ^ (odd if j % 2 else even)) * n_head + j)
            for i in range(n_seq)
            for j in range(n_head)
        ]
        return lax.ppermute(x, ("seq", "head"), pairs)

    def tie(*x):
        return lax.optimization_barrier(x)

    def spread(x, during):
        d = n_head // 2
        have = {d: swap(x, "head", n_head, d)}
        have[d], extra = tie(have[d], during)
        while d > 1:
            d //= 2
            have.update({e ^ d: swap(have[e], "head", n_head, d) for e in list(have)})
            have[d] = swap(x, "head", n_head, d)
        return [have[d] for d in range(1, n_head)], extra

    here = place.astype(jnp.int32).reshape(1)
    slice_out = like(heads * size, width, dtype=BF16)
    acc, rest, decay, strict, cols, grown, gain, *slices = call(
        functools.partial(prepare_kernel, n_head),
        [
            like(2, rows, heads * size),
            like(n_head - 1, 2, depth, heads * size, dtype=BF16),
            like(heads, rows, rows),
            like(heads, rows, rows),
            like(heads, 3, rows, size),
            like(heads, rows, size),
            like(1, size),
        ]
        + [slice_out] * (n_head - 1),
        [here, tokens, w_key, w_value, w_out, gate_codes.T, beta_codes.T, norm_gain.reshape(1, size)],
        1,
        7,
        [
            pltpu.VMEM((rows, depth), BF16),
            pltpu.VMEM((2, depth, heads * size), BF16),
            pltpu.VMEM((heads, rows), jnp.int32),
            pltpu.VMEM((heads, rows), jnp.int32),
            pltpu.SemaphoreType.DMA((3 + 3 * n_head,)),
        ],
    )
    pieces, (acc, rest) = spread(tokens, (acc, rest))
    (acc,) = call(
        functools.partial(more_kernel, n_head - 2),
        [like(2, rows, heads * size)],
        [acc, rest, *pieces[:-1]],
    )
    state = like(heads, size, size)
    state_sent = like(heads, size, size, dtype=BF16)
    pair_sent = like(heads, size, 2 * size, dtype=BF16)
    send, keys, solved = call(
        functools.partial(summary_kernel, size),
        [pair_sent, like(heads, rows, size), like(heads, rows, 2 * size)],
        [acc, rest, pieces[-1], strict, cols, grown],
    )
    send, *slices = tie(send, *slices)
    out_weights = [swap(slices[d - 1], "head", n_head, d) for d in range(1, n_head)]
    prefix = []
    d = 1
    while 2 * d < n_seq:
        radix = 4 if 4 * d < n_seq else 2
        last = 2 * radix * d >= n_seq
        if radix == 4:
            got = [swap_two(send, d, 2 * d), swap_two(send, 2 * d, d), swap_two(send, 3 * d, 3 * d)]
        else:
            got = [swap(send, "seq", n_seq, d)]
        place_in = (turn // d) % radix
        if radix == 4:
            place_in = place_in + radix * (place % 2)
        place_in = place_in.astype(jnp.int32).reshape(1)
        merged = [place_in, *got, send, *prefix]
        d *= radix
        if last:
            (send,) = call(
                functools.partial(total_kernel, radix), [state_sent], merged[: radix + 1], 1
            )
        else:
            *prefix, send = call(
                functools.partial(merge_kernel, radix), [state_sent, state, pair_sent], merged, 1
            )
    got = swap(send, "seq", n_seq, d)
    upper = ((turn // d) % 2).astype(jnp.int32).reshape(1)
    local, reach = call(
        functools.partial(local_kernel, n_head, radix),
        [like(heads, rows, size), like(heads, rows, 2 * size, dtype=BF16)],
        [here, upper, merged[0], w_query, tokens, *pieces, decay, grown, keys, solved, *merged[1:]],
        3,
        2,
        [
            pltpu.VMEM((n_head, depth, heads * size), BF16),
            pltpu.VMEM((rows, depth), BF16),
            pltpu.VMEM((heads, size, size), BF16),
            pltpu.VMEM((heads, size, size), F32),
            pltpu.SemaphoreType.DMA((n_head + 1,)),
        ],
    )
    got, local, reach = tie(got, local, reach)
    (normed,) = call(
        output_kernel,
        [like(rows, heads * size, dtype=BF16)],
        [got, local, reach, gain],
    )
    (mixed,) = call(
        mix_own_kernel,
        [like(rows, width)],
        [here, w_out, normed],
        1,
        1,
        [pltpu.VMEM((heads * size, width), BF16), pltpu.SemaphoreType.DMA(())],
    )
    parts, mixed = spread(normed, mixed)
    (mixed,) = call(
        functools.partial(mix_kernel, n_head - 2),
        [like(rows, width)],
        [mixed, *parts[:-1], *out_weights[:-1]],
    )
    return call(
        functools.partial(mix_kernel, 1),
        [like(rows, width, dtype=BF16)],
        [mixed, parts[-1], out_weights[-1]],
    )[0]


def solution(mesh):
    n_seq, n_head = mesh.shape["seq"], mesh.shape["head"]
    return jax.shard_map(
        functools.partial(shards, n_seq, n_head),
        mesh=mesh,
        in_specs=(
            P("seq", "head"),
            P(None, "head"),
            P(None, "head"),
            P(None, "head"),
            P("seq", "head"),
            P("seq", "head"),
            P(),
            P("head", None),
        ),
        out_specs=P("seq", "head"),
        check_vma=False,
    )
```

```python
import functools
import jax
import jax.numpy as jnp
from jax import lax
from jax.experimental import pallas as pl
from jax.experimental.pallas import tpu as pltpu
from jax.sharding import PartitionSpec as P

BASE = 16
F32 = jnp.float32
BF16 = jnp.bfloat16


def split(x):
    high = x.astype(BF16)
    return high, (x - high.astype(F32)).astype(BF16)


def contract(a, b, dims):
    return lax.dot_general(a, b, (dims, ((), ())), preferred_element_type=F32)


NN = ((1,), (0,))
NT = ((1,), (1,))


def dot3(a, b, dims=NN):
    left = jnp.concatenate([a[0], a[1], a[0]], dims[0][0])
    right = jnp.concatenate([b[0], b[0], b[1]], dims[1][0])
    return contract(left, right, dims)


def gate_tables(codes, beta, decay_ref, strict_ref, cols_ref, grown_ref):
    heads, rows = codes.shape
    tok = lax.broadcasted_iota(jnp.int32, (rows, rows), 0)
    other = lax.broadcasted_iota(jnp.int32, (rows, rows), 1)
    ones = jnp.where(tok <= other, 1.0, 0.0).astype(BF16)
    sums = [
        contract(p.astype(F32).astype(BF16), ones, NN)
        for p in (codes >> 14, (codes >> 7) & 127, codes & 127)
    ]
    logs = -(sums[0] * 16384.0 + sums[1] * 128.0 + sums[2]) / 2097152.0
    beta = beta.astype(F32) / 256.0
    logs_t = jnp.transpose(logs)
    beta_t = jnp.transpose(beta)
    for h in range(heads):
        row = logs[h : h + 1, :]
        col = jnp.broadcast_to(logs_t[:, h : h + 1], (rows, rows))
        gap = col - row
        decay_ref[h] = jnp.where(tok >= other, jnp.exp(jnp.where(tok >= other, gap, 0.0)), 0.0)
        grown = jnp.exp(col)
        beta_col = jnp.broadcast_to(beta_t[:, h : h + 1], (rows, rows))
        strict_ref[h] = jnp.where(tok > other, decay_ref[h] * beta_col, 0.0)
        grown_ref[h] = grown
        cols_ref[h, 0] = beta_col * grown
        cols_ref[h, 1] = beta_col
        cols_ref[h, 2] = jnp.exp(row[:, rows - 1 :] - col)


def copy_all(moves, sems):
    copies = [pltpu.make_async_copy(a, b, sems.at[i]) for i, (a, b) in enumerate(moves)]
    for copy in copies:
        copy.start()
    return copies


def block_of(place, d, depth):
    return pl.ds(pl.multiple_of((place ^ d) * depth, depth), depth)


def out_slices(place, wo_hbm, out_refs, first):
    width = out_refs[0].shape[1]
    return [
        (wo_hbm.at[:, block_of(place, first + i, width)], ref) for i, ref in enumerate(out_refs)
    ]


def prepare_kernel(n_head, place_ref, tok_hbm, wk_hbm, wv_hbm, wo_hbm, gate_hbm, beta_hbm, gain_hbm, *refs):
    acc_ref, rest_ref, decay_ref, strict_ref, cols_ref, grown_ref, gain_ref = refs[:7]
    out_refs = refs[7:-5]
    tok_ref, own_ref, gate_ref, beta_ref, sems = refs[-5:]
    place = place_ref[0]
    depth = tok_ref.shape[1]
    weights = (wk_hbm, wv_hbm)
    moves = [(gate_hbm, gate_ref), (beta_hbm, beta_ref), (gain_hbm, gain_ref), (tok_hbm, tok_ref)]
    moves += [(w.at[block_of(place, 0, depth), :], own_ref.at[i]) for i, w in enumerate(weights)]
    moves += [
        (w.at[block_of(place, d, depth), :], rest_ref.at[d - 1, i])
        for d in range(1, n_head)
        for i, w in enumerate(weights)
    ]
    moves += out_slices(place, wo_hbm, out_refs, n_head - len(out_refs))
    copies = copy_all(moves, sems)
    copies[0].wait()
    copies[1].wait()
    gate_tables(gate_ref[...], beta_ref[...], decay_ref, strict_ref, cols_ref, grown_ref)
    for copy in copies[2:6]:
        copy.wait()
    for i in range(len(weights)):
        acc_ref[i] = contract(tok_ref[...], own_ref[i], NN)
    for copy in copies[6:]:
        copy.wait()


def more_kernel(n_pieces, acc_ref, rest_ref, *refs):
    out_ref = refs[-1]
    for i in range(acc_ref.shape[0]):
        total = acc_ref[i]
        for d in range(n_pieces):
            total = total + contract(refs[d][...], rest_ref[d, i], NN)
        out_ref[i] = total


def solve_lower(lowers, rights):
    rows = lowers[0].shape[0]
    blocks = rows // BASE
    tok = lax.broadcasted_iota(jnp.int32, (rows, rows), 0)
    other = lax.broadcasted_iota(jnp.int32, (rows, rows), 1)
    lane = lax.broadcasted_iota(jnp.int32, (BASE, rows), 1)
    sub = lax.broadcasted_iota(jnp.int32, (BASE, rows), 0)
    diagonal = []
    for lower in lowers:
        compact = jnp.zeros((BASE, rows), F32)
        for b in range(blocks):
            compact = compact + jnp.where(
                lane // BASE == b, lower[b * BASE : (b + 1) * BASE, :], 0.0
            )
        solved = jnp.where(sub == lane % BASE, 1.0, 0.0)
        for j in range(BASE - 1):
            column = jnp.take_along_axis(compact, (lane // BASE) * BASE + j, axis=1)
            solved = solved - column * solved[j : j + 1, :]
        inside = tok // BASE == other // BASE
        diagonal.append(split(jnp.where(inside, jnp.concatenate([solved] * blocks, 0), 0.0)))
    results = [dot3(d, r) for d, r in zip(diagonal, rights)]
    if blocks == 1:
        return results
    step = [
        dot3(d, split(jnp.where(tok // BASE == other // BASE, 0.0, lower)))
        for d, lower in zip(diagonal, lowers)
    ]
    step = [split(x) for x in step]
    covered = 1
    while True:
        top = covered * BASE
        lowest = [tuple(part[top:] for part in v) for v in step]
        sign = -1.0 if covered == 1 else 1.0
        changes = [dot3(v, split(x)) for v, x in zip(lowest, results)]
        results = [
            jnp.concatenate([x[:top], x[top:] + sign * change], 0)
            for x, change in zip(results, changes)
        ]
        covered *= 2
        if covered >= blocks:
            return results
        powers = [dot3(tuple(part[covered * BASE :] for part in v), v) for v in step]
        empty = jnp.zeros((covered * BASE, rows), F32)
        step = [split(jnp.concatenate([empty, power], 0)) for power in powers]


def summary_kernel(size, acc_ref, rest_ref, piece_ref, strict_ref, cols_ref, grown_ref, send_ref, keys_ref, wy_ref):
    heads, rows, _ = strict_ref.shape
    last = rest_ref.shape[0] - 1
    keys = acc_ref[0] + contract(piece_ref[...], rest_ref[last, 0], NN)
    values = acc_ref[1] + contract(piece_ref[...], rest_ref[last, 1], NN)
    every = range(heads)
    each = [keys[:, h * size : (h + 1) * size] for h in every]
    scales = [lax.rsqrt(jnp.sum(key * key, -1, keepdims=True) + 1e-06) for key in each]
    each = [key * scale for key, scale in zip(each, scales)]
    halves = [split(key) for key in each]
    lowers = [dot3(halves[h], halves[h], NT) * strict_ref[h] for h in every]
    tails = [split(jnp.transpose(each[h] * cols_ref[h, 2])) for h in every]
    rights = [
        jnp.concatenate(
            [each[h] * cols_ref[h, 0], values[:, h * size : (h + 1) * size] * cols_ref[h, 1]], 1
        )
        for h in every
    ]
    solved = solve_lower(lowers, [split(right) for right in rights])
    eye = lax.broadcasted_iota(jnp.int32, (size, size), 0) == lax.broadcasted_iota(
        jnp.int32, (size, size), 1
    )
    both = [dot3(tails[h], split(solved[h])) for h in every]
    for h in every:
        step = jnp.where(eye, grown_ref[h, rows - 1 :, :], 0.0) - both[h][:, :size]
        send_ref[h, :, :size] = step.astype(BF16)
        send_ref[h, :, size:] = both[h][:, size:].astype(BF16)
        keys_ref[h] = each[h]
        wy_ref[h] = solved[h]


def apply(step, early):
    if step.dtype == BF16 and early.dtype == BF16:
        return contract(step, early, NN)
    if step.dtype == BF16:
        high, low = split(early)
        return contract(
            jnp.concatenate([step, step], 1), jnp.concatenate([high, low], 0), NN
        )
    early = split(early) if early.dtype == F32 else (early, jnp.zeros_like(early))
    return dot3(split(step), early)


def follow(early, late):
    size = early[0].shape[0]
    moved = [apply(late[h][:, :size], early[h]) for h in range(len(early))]
    return [moved[h] + late[h][:, size:].astype(F32) for h in range(len(early))]


def join(early, late):
    every = range(len(early))
    size = early[0].shape[0]
    both = [apply(late[h][:, :size], early[h]) for h in every]
    add = [both[h][:, size:] + late[h][:, size:].astype(F32) for h in every]
    return [jnp.concatenate([both[h][:, :size], add[h]], 1) for h in every]


def parts_of(place, odd, own_ref, got_refs):
    refs = [own_ref, *got_refs]
    if odd:
        refs[1], refs[2] = refs[2], refs[1]
    return [[refs[i ^ place][h] for h in range(own_ref.shape[0])] for i in range(len(refs))]


def total_of(parts):
    if len(parts) == 2:
        return join(*parts)
    return join(join(parts[0], parts[1]), join(parts[2], parts[3]))


def before(place, parts):
    if place:
        pair = parts[0]
        for part in parts[1:place]:
            pair = join(pair, part)
        return pair
    size = parts[0][0].shape[0]
    row = lax.broadcasted_iota(jnp.int32, (size, 2 * size), 0)
    column = lax.broadcasted_iota(jnp.int32, (size, 2 * size), 1)
    return [jnp.where(row == column, 1.0, 0.0).astype(BF16)] * len(parts[0])


def at_place(radix, place_ref, run):
    for place in range(radix):
        for odd in range(2 if radix > 2 else 1):
            pl.when(place_ref[0] == place + radix * odd)(functools.partial(run, place, odd))


def enter(pair, new_map_ref, new_add_ref, pmap_ref=None, padd_ref=None):
    size = new_map_ref.shape[1]
    for h in range(len(pair)):
        if pmap_ref is None:
            new_map_ref[h] = pair[h][:, :size].astype(F32)
            new_add_ref[h] = pair[h][:, size:].astype(F32)
        else:
            both = apply(pmap_ref[h], pair[h])
            new_map_ref[h] = both[:, :size]
            new_add_ref[h] = both[:, size:] + padd_ref[h]


def merge_kernel(radix, place_ref, *refs):
    got_refs, own_ref, prefix_refs = refs[: radix - 1], refs[radix - 1], refs[radix:-3]
    new_map_ref, new_add_ref, send_ref = refs[-3:]

    def run(place, odd):
        parts = parts_of(place, odd, own_ref, got_refs)
        total = total_of(parts)
        enter(before(place, parts), new_map_ref, new_add_ref, *prefix_refs)
        for h in range(len(total)):
            send_ref[h] = total[h].astype(BF16)

    at_place(radix, place_ref, run)


def total_kernel(radix, place_ref, *refs):
    got_refs, own_ref, send_ref = refs[: radix - 1], refs[radix - 1], refs[-1]
    heads, size, _ = own_ref.shape

    def run(place, odd):
        parts = parts_of(place, odd, own_ref, got_refs)
        add = follow([part[:, size:] for part in parts[0]], parts[1])
        if radix > 2:
            add = follow(add, join(parts[2], parts[3]))
        for h in range(heads):
            send_ref[h] = add[h].astype(BF16)

    at_place(radix, place_ref, run)


def local_kernel(n_head, radix, place_ref, upper_ref, turn_ref, wq_hbm, tok_hbm, *refs):
    pieces, refs = refs[: n_head - 1], refs[n_head - 1 :]
    decay_ref, grown_ref, keys_ref, wy_ref, *refs = refs
    got_refs, own_ref, prefix_refs = refs[: radix - 1], refs[radix - 1], refs[radix:-7]
    out_ref, reach_ref, wq_ref, tok_ref, pmap_ref, padd_ref, sems = refs[-7:]
    heads, size, _ = padd_ref.shape
    every = range(heads)
    depth = tok_ref.shape[1]
    moves = [(tok_hbm, tok_ref)]
    moves += [
        (wq_hbm.at[block_of(place_ref[0], d, depth), :], wq_ref.at[d]) for d in range(n_head)
    ]
    copies = copy_all(moves, sems)

    def run(place, odd):
        parts = parts_of(place, odd, own_ref, got_refs)
        enter(before(place, parts), pmap_ref, padd_ref, *prefix_refs)

    at_place(radix, turn_ref, run)
    for copy in copies:
        copy.wait()
    queries = contract(tok_ref[...], wq_ref[0], NN)
    for d in range(1, n_head):
        queries = queries + contract(pieces[d - 1][...], wq_ref[d], NN)
    is_upper = upper_ref[0] > 0
    queries = [queries[:, h * size : (h + 1) * size] for h in every]
    dots = [dot3(split(queries[h]), split(keys_ref[h]), NT) * decay_ref[h] for h in every]
    both = [dot3(split(dots[h]), split(wy_ref[h])) for h in every]
    reach = [split(queries[h] * grown_ref[h] - both[h][:, :size]) for h in every]
    out = [both[h][:, size:] + dot3(reach[h], split(padd_ref[h])) for h in every]
    later = [jnp.where(is_upper, dot3(reach[h], split(pmap_ref[h])), 0.0) for h in every]
    for h in every:
        out_ref[h] = out[h]
        reach_ref[h] = jnp.concatenate(split(later[h]), 1)


def output_kernel(got_ref, local_ref, reach_ref, gain_ref, normed_ref):
    heads, size, _ = got_ref.shape
    for h in range(heads):
        got = jnp.concatenate([got_ref[h]] * 2, 0)
        out = local_ref[h] + contract(reach_ref[h], got, NN)
        scale = lax.rsqrt(jnp.mean(out * out, -1, keepdims=True) + 1e-06)
        normed_ref[:, h * size : (h + 1) * size] = (out * scale * gain_ref[...]).astype(BF16)


def mix_own_kernel(place_ref, wo_hbm, part_ref, out_ref, weight_ref, sem):
    width = weight_ref.shape[1]
    copy = pltpu.make_async_copy(wo_hbm.at[:, block_of(place_ref[0], 0, width)], weight_ref, sem)
    copy.start()
    copy.wait()
    out_ref[...] = contract(part_ref[...], weight_ref[...], NN)


def mix_kernel(n_pieces, base_ref, *refs):
    total = base_ref[...]
    for part, weight in zip(refs[:n_pieces], refs[n_pieces : 2 * n_pieces]):
        total = total + contract(part[...], weight[...], NN)
    refs[-1][...] = total.astype(refs[-1].dtype)


def call(kernel, outs, args, scalars=0, hbm=0, scratch=()):
    vmem = pl.BlockSpec(memory_space=pltpu.VMEM)
    far = pl.BlockSpec(memory_space=pltpu.HBM)
    specs = [pl.BlockSpec(memory_space=pltpu.SMEM)] * scalars + [far] * hbm
    specs += [vmem] * (len(args) - scalars - hbm)
    args = [
        pltpu.with_memory_space_constraint(a, pltpu.HBM) if scalars <= i < scalars + hbm else a
        for i, a in enumerate(args)
    ]
    return pl.pallas_call(
        kernel,
        out_shape=outs,
        in_specs=specs,
        out_specs=[vmem] * len(outs),
        scratch_shapes=scratch,
        compiler_params=pltpu.CompilerParams(vmem_limit_bytes=16 * 1024 * 1024),
    )(*args)


def like(*shape, dtype=F32):
    return jax.ShapeDtypeStruct(shape, dtype)


def shards(n_seq, n_head, tokens, w_query, w_key, w_value, gate_codes, beta_codes, norm_gain, w_out):
    rows, depth = tokens.shape
    heads = gate_codes.shape[1]
    size = norm_gain.shape[0]
    width = w_out.shape[1] // n_head
    place = lax.axis_index("head")
    turn = lax.axis_index("seq")

    def swap(x, axis, count, d):
        return lax.ppermute(x, axis, [(i, i ^ d) for i in range(count)])

    def swap_two(x, even, odd):
        pairs = [
            (i * n_head + j, (i ^ (odd if j % 2 else even)) * n_head + j)
            for i in range(n_seq)
            for j in range(n_head)
        ]
        return lax.ppermute(x, ("seq", "head"), pairs)

    def tie(*x):
        return lax.optimization_barrier(x)

    def spread(x, during):
        d = n_head // 2
        have = {d: swap(x, "head", n_head, d)}
        have[d], extra = tie(have[d], during)
        while d > 1:
            d //= 2
            have.update({e ^ d: swap(have[e], "head", n_head, d) for e in list(have)})
            have[d] = swap(x, "head", n_head, d)
        return [have[d] for d in range(1, n_head)], extra

    here = place.astype(jnp.int32).reshape(1)
    slice_out = like(heads * size, width, dtype=BF16)
    acc, rest, decay, strict, cols, grown, gain, *slices = call(
        functools.partial(prepare_kernel, n_head),
        [
            like(2, rows, heads * size),
            like(n_head - 1, 2, depth, heads * size, dtype=BF16),
            like(heads, rows, rows),
            like(heads, rows, rows),
            like(heads, 3, rows, size),
            like(heads, rows, size),
            like(1, size),
        ]
        + [slice_out] * (n_head - 1),
        [here, tokens, w_key, w_value, w_out, gate_codes.T, beta_codes.T, norm_gain.reshape(1, size)],
        1,
        7,
        [
            pltpu.VMEM((rows, depth), BF16),
            pltpu.VMEM((2, depth, heads * size), BF16),
            pltpu.VMEM((heads, rows), jnp.int32),
            pltpu.VMEM((heads, rows), jnp.int32),
            pltpu.SemaphoreType.DMA((3 + 3 * n_head,)),
        ],
    )
    pieces, (acc, rest) = spread(tokens, (acc, rest))
    (acc,) = call(
        functools.partial(more_kernel, n_head - 2),
        [like(2, rows, heads * size)],
        [acc, rest, *pieces[:-1]],
    )
    state = like(heads, size, size)
    state_sent = like(heads, size, size, dtype=BF16)
    pair_sent = like(heads, size, 2 * size, dtype=BF16)
    send, keys, solved = call(
        functools.partial(summary_kernel, size),
        [pair_sent, like(heads, rows, size), like(heads, rows, 2 * size)],
        [acc, rest, pieces[-1], strict, cols, grown],
    )
    send, *slices = tie(send, *slices)
    out_weights = [swap(slices[d - 1], "head", n_head, d) for d in range(1, n_head)]
    prefix = []
    d = 1
    while 2 * d < n_seq:
        radix = 4 if 4 * d < n_seq else 2
        last = 2 * radix * d >= n_seq
        if radix == 4:
            got = [swap_two(send, d, 2 * d), swap_two(send, 2 * d, d), swap_two(send, 3 * d, 3 * d)]
        else:
            got = [swap(send, "seq", n_seq, d)]
        place_in = (turn // d) % radix
        if radix == 4:
            place_in = place_in + radix * (place % 2)
        place_in = place_in.astype(jnp.int32).reshape(1)
        merged = [place_in, *got, send, *prefix]
        d *= radix
        if last:
            (send,) = call(
                functools.partial(total_kernel, radix), [state_sent], merged[: radix + 1], 1
            )
        else:
            *prefix, send = call(
                functools.partial(merge_kernel, radix), [state, state, pair_sent], merged, 1
            )
    got = swap(send, "seq", n_seq, d)
    upper = ((turn // d) % 2).astype(jnp.int32).reshape(1)
    local, reach = call(
        functools.partial(local_kernel, n_head, radix),
        [like(heads, rows, size), like(heads, rows, 2 * size, dtype=BF16)],
        [here, upper, merged[0], w_query, tokens, *pieces, decay, grown, keys, solved, *merged[1:]],
        3,
        2,
        [
            pltpu.VMEM((n_head, depth, heads * size), BF16),
            pltpu.VMEM((rows, depth), BF16),
            pltpu.VMEM((heads, size, size), F32),
            pltpu.VMEM((heads, size, size), F32),
            pltpu.SemaphoreType.DMA((n_head + 1,)),
        ],
    )
    got, local, reach = tie(got, local, reach)
    (normed,) = call(
        output_kernel,
        [like(rows, heads * size, dtype=BF16)],
        [got, local, reach, gain],
    )
    (mixed,) = call(
        mix_own_kernel,
        [like(rows, width)],
        [here, w_out, normed],
        1,
        1,
        [pltpu.VMEM((heads * size, width), BF16), pltpu.SemaphoreType.DMA(())],
    )
    parts, mixed = spread(normed, mixed)
    (mixed,) = call(
        functools.partial(mix_kernel, n_head - 2),
        [like(rows, width)],
        [mixed, *parts[:-1], *out_weights[:-1]],
    )
    return call(
        functools.partial(mix_kernel, 1),
        [like(rows, width, dtype=BF16)],
        [mixed, parts[-1], out_weights[-1]],
    )[0]


def solution(mesh):
    n_seq, n_head = mesh.shape["seq"], mesh.shape["head"]
    return jax.shard_map(
        functools.partial(shards, n_seq, n_head),
        mesh=mesh,
        in_specs=(
            P("seq", "head"),
            P(None, "head"),
            P(None, "head"),
            P(None, "head"),
            P("seq", "head"),
            P("seq", "head"),
            P(),
            P("head", None),
        ),
        out_specs=P("seq", "head"),
        check_vma=False,
    )
```

```python
import functools
import jax
import jax.numpy as jnp
from jax import lax
from jax.experimental import pallas as pl
from jax.experimental.pallas import tpu as pltpu
from jax.sharding import PartitionSpec as P

BASE = 16
F32 = jnp.float32
BF16 = jnp.bfloat16


def split(x):
    high = x.astype(BF16)
    return high, (x - high.astype(F32)).astype(BF16)


def contract(a, b, dims):
    return lax.dot_general(a, b, (dims, ((), ())), preferred_element_type=F32)


NN = ((1,), (0,))
NT = ((1,), (1,))


def dot3(a, b, dims=NN):
    left = jnp.concatenate([a[0], a[1], a[0]], dims[0][0])
    right = jnp.concatenate([b[0], b[0], b[1]], dims[1][0])
    return contract(left, right, dims)


def gate_tables(codes, beta, decay_ref, strict_ref, cols_ref, grown_ref):
    heads, rows = codes.shape
    tok = lax.broadcasted_iota(jnp.int32, (rows, rows), 0)
    other = lax.broadcasted_iota(jnp.int32, (rows, rows), 1)
    ones = jnp.where(tok <= other, 1.0, 0.0).astype(BF16)
    sums = [
        contract(p.astype(F32).astype(BF16), ones, NN)
        for p in (codes >> 14, (codes >> 7) & 127, codes & 127)
    ]
    logs = -(sums[0] * 16384.0 + sums[1] * 128.0 + sums[2]) / 2097152.0
    beta = beta.astype(F32) / 256.0
    logs_t = jnp.transpose(logs)
    beta_t = jnp.transpose(beta)
    for h in range(heads):
        row = logs[h : h + 1, :]
        col = jnp.broadcast_to(logs_t[:, h : h + 1], (rows, rows))
        gap = col - row
        decay_ref[h] = jnp.where(tok >= other, jnp.exp(jnp.where(tok >= other, gap, 0.0)), 0.0)
        grown = jnp.exp(col)
        beta_col = jnp.broadcast_to(beta_t[:, h : h + 1], (rows, rows))
        strict_ref[h] = jnp.where(tok > other, decay_ref[h] * beta_col, 0.0)
        grown_ref[h] = grown
        cols_ref[h, 0] = beta_col * grown
        cols_ref[h, 1] = beta_col
        cols_ref[h, 2] = jnp.exp(row[:, rows - 1 :] - col)


def copy_all(moves, sems):
    copies = [pltpu.make_async_copy(a, b, sems.at[i]) for i, (a, b) in enumerate(moves)]
    for copy in copies:
        copy.start()
    return copies


def block_of(place, d, depth):
    return pl.ds(pl.multiple_of((place ^ d) * depth, depth), depth)


def out_slices(place, wo_hbm, out_refs, first):
    width = out_refs[0].shape[1]
    return [
        (wo_hbm.at[:, block_of(place, first + i, width)], ref) for i, ref in enumerate(out_refs)
    ]


def prepare_kernel(n_head, place_ref, tok_hbm, wk_hbm, wv_hbm, wo_hbm, gate_hbm, beta_hbm, gain_hbm, *refs):
    acc_ref, rest_ref, decay_ref, strict_ref, cols_ref, grown_ref, gain_ref = refs[:7]
    out_refs = refs[7:-5]
    tok_ref, own_ref, gate_ref, beta_ref, sems = refs[-5:]
    place = place_ref[0]
    depth = tok_ref.shape[1]
    weights = (wk_hbm, wv_hbm)
    moves = [(gate_hbm, gate_ref), (beta_hbm, beta_ref), (gain_hbm, gain_ref), (tok_hbm, tok_ref)]
    moves += [(w.at[block_of(place, 0, depth), :], own_ref.at[i]) for i, w in enumerate(weights)]
    moves += [
        (w.at[block_of(place, d, depth), :], rest_ref.at[d - 1, i])
        for d in range(1, n_head)
        for i, w in enumerate(weights)
    ]
    moves += out_slices(place, wo_hbm, out_refs, n_head - len(out_refs))
    copies = copy_all(moves, sems)
    copies[0].wait()
    copies[1].wait()
    gate_tables(gate_ref[...], beta_ref[...], decay_ref, strict_ref, cols_ref, grown_ref)
    for copy in copies[2:6]:
        copy.wait()
    for i in range(len(weights)):
        acc_ref[i] = contract(tok_ref[...], own_ref[i], NN)
    for copy in copies[6:]:
        copy.wait()


def more_kernel(n_pieces, acc_ref, rest_ref, *refs):
    out_ref = refs[-1]
    for i in range(acc_ref.shape[0]):
        total = acc_ref[i]
        for d in range(n_pieces):
            total = total + contract(refs[d][...], rest_ref[d, i], NN)
        out_ref[i] = total


def solve_lower(lowers, rights):
    rows = lowers[0].shape[0]
    blocks = rows // BASE
    tok = lax.broadcasted_iota(jnp.int32, (rows, rows), 0)
    other = lax.broadcasted_iota(jnp.int32, (rows, rows), 1)
    lane = lax.broadcasted_iota(jnp.int32, (BASE, rows), 1)
    sub = lax.broadcasted_iota(jnp.int32, (BASE, rows), 0)
    diagonal = []
    for lower in lowers:
        compact = jnp.zeros((BASE, rows), F32)
        for b in range(blocks):
            compact = compact + jnp.where(
                lane // BASE == b, lower[b * BASE : (b + 1) * BASE, :], 0.0
            )
        solved = jnp.where(sub == lane % BASE, 1.0, 0.0)
        for j in range(BASE - 1):
            column = jnp.take_along_axis(compact, (lane // BASE) * BASE + j, axis=1)
            solved = solved - column * solved[j : j + 1, :]
        inside = tok // BASE == other // BASE
        diagonal.append(split(jnp.where(inside, jnp.concatenate([solved] * blocks, 0), 0.0)))
    results = [dot3(d, r) for d, r in zip(diagonal, rights)]
    if blocks == 1:
        return results
    step = [
        dot3(d, split(jnp.where(tok // BASE == other // BASE, 0.0, lower)))
        for d, lower in zip(diagonal, lowers)
    ]
    step = [split(x) for x in step]
    covered = 1
    while True:
        top = covered * BASE
        lowest = [tuple(part[top:] for part in v) for v in step]
        sign = -1.0 if covered == 1 else 1.0
        changes = [dot3(v, split(x)) for v, x in zip(lowest, results)]
        results = [
            jnp.concatenate([x[:top], x[top:] + sign * change], 0)
            for x, change in zip(results, changes)
        ]
        covered *= 2
        if covered >= blocks:
            return results
        powers = [dot3(tuple(part[covered * BASE :] for part in v), v) for v in step]
        empty = jnp.zeros((covered * BASE, rows), F32)
        step = [split(jnp.concatenate([empty, power], 0)) for power in powers]


def summary_kernel(size, acc_ref, rest_ref, piece_ref, strict_ref, cols_ref, grown_ref, send_ref, keys_ref, wy_ref):
    heads, rows, _ = strict_ref.shape
    last = rest_ref.shape[0] - 1
    keys = acc_ref[0] + contract(piece_ref[...], rest_ref[last, 0], NN)
    values = acc_ref[1] + contract(piece_ref[...], rest_ref[last, 1], NN)
    every = range(heads)
    each = [keys[:, h * size : (h + 1) * size] for h in every]
    scales = [lax.rsqrt(jnp.sum(key * key, -1, keepdims=True) + 1e-06) for key in each]
    each = [key * scale for key, scale in zip(each, scales)]
    halves = [split(key) for key in each]
    lowers = [dot3(halves[h], halves[h], NT) * strict_ref[h] for h in every]
    tails = [split(jnp.transpose(each[h] * cols_ref[h, 2])) for h in every]
    rights = [
        jnp.concatenate(
            [each[h] * cols_ref[h, 0], values[:, h * size : (h + 1) * size] * cols_ref[h, 1]], 1
        )
        for h in every
    ]
    solved = solve_lower(lowers, [split(right) for right in rights])
    eye = lax.broadcasted_iota(jnp.int32, (size, size), 0) == lax.broadcasted_iota(
        jnp.int32, (size, size), 1
    )
    both = [dot3(tails[h], split(solved[h])) for h in every]
    for h in every:
        step = jnp.where(eye, grown_ref[h, rows - 1 :, :], 0.0) - both[h][:, :size]
        send_ref[h, :, :size] = step.astype(BF16)
        send_ref[h, :, size:] = both[h][:, size:].astype(BF16)
        keys_ref[h] = each[h]
        wy_ref[h] = solved[h]


def apply(step, early):
    if step.dtype == BF16 and early.dtype == BF16:
        return contract(step, early, NN)
    if step.dtype == BF16:
        high, low = split(early)
        return contract(
            jnp.concatenate([step, step], 1), jnp.concatenate([high, low], 0), NN
        )
    return apply(step.astype(BF16), early)


def follow(early, late):
    size = early[0].shape[0]
    moved = [apply(late[h][:, :size], early[h]) for h in range(len(early))]
    return [moved[h] + late[h][:, size:].astype(F32) for h in range(len(early))]


def join(early, late):
    every = range(len(early))
    size = early[0].shape[0]
    both = [apply(late[h][:, :size], early[h]) for h in every]
    add = [both[h][:, size:] + late[h][:, size:].astype(F32) for h in every]
    return [jnp.concatenate([both[h][:, :size], add[h]], 1) for h in every]


def parts_of(place, own_ref, got_refs):
    refs = [own_ref, *got_refs]
    return [[refs[i ^ place][h] for h in range(own_ref.shape[0])] for i in range(len(refs))]


def total_of(parts):
    if len(parts) == 2:
        return join(*parts)
    return join(join(parts[0], parts[1]), join(parts[2], parts[3]))


def before(place, parts):
    if place:
        pair = parts[0]
        for part in parts[1:place]:
            pair = join(pair, part)
        return pair
    size = parts[0][0].shape[0]
    row = lax.broadcasted_iota(jnp.int32, (size, 2 * size), 0)
    column = lax.broadcasted_iota(jnp.int32, (size, 2 * size), 1)
    return [jnp.where(row == column, 1.0, 0.0).astype(BF16)] * len(parts[0])


def at_place(radix, place_ref, run):
    for place in range(radix):
        pl.when(place_ref[0] == place)(functools.partial(run, place))


def enter(pair, new_map_ref, new_add_ref, pmap_ref=None, padd_ref=None):
    size = new_map_ref.shape[1]
    for h in range(len(pair)):
        if pmap_ref is None:
            new_map_ref[h] = pair[h][:, :size].astype(F32)
            new_add_ref[h] = pair[h][:, size:].astype(F32)
        else:
            both = apply(pmap_ref[h], pair[h])
            new_map_ref[h] = both[:, :size]
            new_add_ref[h] = both[:, size:] + padd_ref[h]


def merge_kernel(radix, place_ref, *refs):
    got_refs, own_ref, prefix_refs = refs[: radix - 1], refs[radix - 1], refs[radix:-3]
    new_map_ref, new_add_ref, send_ref = refs[-3:]

    def run(place):
        parts = parts_of(place, own_ref, got_refs)
        total = total_of(parts)
        enter(before(place, parts), new_map_ref, new_add_ref, *prefix_refs)
        for h in range(len(total)):
            send_ref[h] = total[h].astype(BF16)

    at_place(radix, place_ref, run)


def total_kernel(radix, place_ref, upper_ref, *refs):
    got_refs, own_ref, send_ref = refs[: radix - 1], refs[radix - 1], refs[-1]
    heads, size, _ = own_ref.shape

    def run(place):
        parts = parts_of(place, own_ref, got_refs)
        add = follow([part[:, size:] for part in parts[0]], parts[1])
        if radix > 2:
            add = follow(add, join(parts[2], parts[3]))
        for h in range(heads):
            send_ref[h] = add[h].astype(BF16)

    @pl.when(upper_ref[0] == 0)
    def _():
        at_place(radix, place_ref, run)

    @pl.when(upper_ref[0] > 0)
    def _():
        send_ref[...] = jnp.zeros_like(send_ref)


def local_kernel(n_head, radix, place_ref, upper_ref, turn_ref, wq_hbm, tok_hbm, *refs):
    pieces, refs = refs[: n_head - 1], refs[n_head - 1 :]
    decay_ref, grown_ref, keys_ref, wy_ref, *refs = refs
    got_refs, own_ref, prefix_refs = refs[: radix - 1], refs[radix - 1], refs[radix:-7]
    out_ref, reach_ref, wq_ref, tok_ref, pmap_ref, padd_ref, sems = refs[-7:]
    heads, size, _ = padd_ref.shape
    every = range(heads)
    depth = tok_ref.shape[1]
    moves = [(tok_hbm, tok_ref)]
    moves += [
        (wq_hbm.at[block_of(place_ref[0], d, depth), :], wq_ref.at[d]) for d in range(n_head)
    ]
    copies = copy_all(moves, sems)

    def run(place):
        parts = parts_of(place, own_ref, got_refs)
        enter(before(place, parts), pmap_ref, padd_ref, *prefix_refs)

    at_place(radix, turn_ref, run)
    for copy in copies:
        copy.wait()
    queries = contract(tok_ref[...], wq_ref[0], NN)
    for d in range(1, n_head):
        queries = queries + contract(pieces[d - 1][...], wq_ref[d], NN)
    is_upper = upper_ref[0] > 0
    queries = [queries[:, h * size : (h + 1) * size] for h in every]
    dots = [dot3(split(queries[h]), split(keys_ref[h]), NT) * decay_ref[h] for h in every]
    both = [dot3(split(dots[h]), split(wy_ref[h])) for h in every]
    reach = [split(queries[h] * grown_ref[h] - both[h][:, :size]) for h in every]
    out = [both[h][:, size:] + dot3(reach[h], split(padd_ref[h])) for h in every]
    later = [jnp.where(is_upper, dot3(reach[h], split(pmap_ref[h])), 0.0) for h in every]
    for h in every:
        out_ref[h] = out[h]
        reach_ref[h] = jnp.concatenate(split(later[h]), 1)


def output_kernel(got_ref, local_ref, reach_ref, gain_ref, normed_ref):
    heads, size, _ = got_ref.shape
    for h in range(heads):
        got = jnp.concatenate([got_ref[h]] * 2, 0)
        out = local_ref[h] + contract(reach_ref[h], got, NN)
        scale = lax.rsqrt(jnp.mean(out * out, -1, keepdims=True) + 1e-06)
        normed_ref[:, h * size : (h + 1) * size] = (out * scale * gain_ref[...]).astype(BF16)


def mix_own_kernel(place_ref, wo_hbm, part_ref, out_ref, weight_ref, sem):
    width = weight_ref.shape[1]
    copy = pltpu.make_async_copy(wo_hbm.at[:, block_of(place_ref[0], 0, width)], weight_ref, sem)
    copy.start()
    copy.wait()
    out_ref[...] = contract(part_ref[...], weight_ref[...], NN)


def mix_kernel(n_pieces, base_ref, *refs):
    total = base_ref[...]
    for part, weight in zip(refs[:n_pieces], refs[n_pieces : 2 * n_pieces]):
        total = total + contract(part[...], weight[...], NN)
    refs[-1][...] = total.astype(refs[-1].dtype)


def call(kernel, outs, args, scalars=0, hbm=0, scratch=()):
    vmem = pl.BlockSpec(memory_space=pltpu.VMEM)
    far = pl.BlockSpec(memory_space=pltpu.HBM)
    specs = [pl.BlockSpec(memory_space=pltpu.SMEM)] * scalars + [far] * hbm
    specs += [vmem] * (len(args) - scalars - hbm)
    args = [
        pltpu.with_memory_space_constraint(a, pltpu.HBM) if scalars <= i < scalars + hbm else a
        for i, a in enumerate(args)
    ]
    return pl.pallas_call(
        kernel,
        out_shape=outs,
        in_specs=specs,
        out_specs=[vmem] * len(outs),
        scratch_shapes=scratch,
        compiler_params=pltpu.CompilerParams(vmem_limit_bytes=16 * 1024 * 1024),
    )(*args)


def like(*shape, dtype=F32):
    return jax.ShapeDtypeStruct(shape, dtype)


def shards(n_seq, n_head, tokens, w_query, w_key, w_value, gate_codes, beta_codes, norm_gain, w_out):
    rows, depth = tokens.shape
    heads = gate_codes.shape[1]
    size = norm_gain.shape[0]
    width = w_out.shape[1] // n_head
    place = lax.axis_index("head")
    turn = lax.axis_index("seq")

    def swap(x, axis, count, d):
        return lax.ppermute(x, axis, [(i, i ^ d) for i in range(count)])

    def tie(*x):
        return lax.optimization_barrier(x)

    def spread(x, during):
        d = n_head // 2
        have = {d: swap(x, "head", n_head, d)}
        have[d], extra = tie(have[d], during)
        while d > 1:
            d //= 2
            have.update({e ^ d: swap(have[e], "head", n_head, d) for e in list(have)})
            have[d] = swap(x, "head", n_head, d)
        return [have[d] for d in range(1, n_head)], extra

    here = place.astype(jnp.int32).reshape(1)
    slice_out = like(heads * size, width, dtype=BF16)
    acc, rest, decay, strict, cols, grown, gain, *slices = call(
        functools.partial(prepare_kernel, n_head),
        [
            like(2, rows, heads * size),
            like(n_head - 1, 2, depth, heads * size, dtype=BF16),
            like(heads, rows, rows),
            like(heads, rows, rows),
            like(heads, 3, rows, size),
            like(heads, rows, size),
            like(1, size),
        ]
        + [slice_out] * (n_head - 1),
        [here, tokens, w_key, w_value, w_out, gate_codes.T, beta_codes.T, norm_gain.reshape(1, size)],
        1,
        7,
        [
            pltpu.VMEM((rows, depth), BF16),
            pltpu.VMEM((2, depth, heads * size), BF16),
            pltpu.VMEM((heads, rows), jnp.int32),
            pltpu.VMEM((heads, rows), jnp.int32),
            pltpu.SemaphoreType.DMA((3 + 3 * n_head,)),
        ],
    )
    pieces, (acc, rest) = spread(tokens, (acc, rest))
    (acc,) = call(
        functools.partial(more_kernel, n_head - 2),
        [like(2, rows, heads * size)],
        [acc, rest, *pieces[:-1]],
    )
    state = like(heads, size, size)
    state_sent = like(heads, size, size, dtype=BF16)
    pair_sent = like(heads, size, 2 * size, dtype=BF16)
    send, keys, solved = call(
        functools.partial(summary_kernel, size),
        [pair_sent, like(heads, rows, size), like(heads, rows, 2 * size)],
        [acc, rest, pieces[-1], strict, cols, grown],
    )
    send, *slices = tie(send, *slices)
    out_weights = [swap(slices[d - 1], "head", n_head, d) for d in range(1, n_head)]
    prefix = []
    d = 1
    while 2 * d < n_seq:
        radix = 4 if 4 * d < n_seq else 2
        last = 2 * radix * d >= n_seq
        if radix == 4:
            got = [swap(send, "seq", n_seq, i * d) for i in (3, 2, 1)][::-1]
        else:
            got = [swap(send, "seq", n_seq, d)]
        place_in = (turn // d) % radix
        place_in = place_in.astype(jnp.int32).reshape(1)
        merged = [place_in, *got, send, *prefix]
        d *= radix
        if last:
            upper = ((turn // d) % 2).astype(jnp.int32).reshape(1)
            (send,) = call(
                functools.partial(total_kernel, radix),
                [state_sent],
                [place_in, upper, *merged[1 : radix + 1]],
                2,
            )
        else:
            *prefix, send = call(
                functools.partial(merge_kernel, radix), [state, state, pair_sent], merged, 1
            )
    got = swap(send, "seq", n_seq, d)
    local, reach = call(
        functools.partial(local_kernel, n_head, radix),
        [like(heads, rows, size), like(heads, rows, 2 * size, dtype=BF16)],
        [here, upper, merged[0], w_query, tokens, *pieces, decay, grown, keys, solved, *merged[1:]],
        3,
        2,
        [
            pltpu.VMEM((n_head, depth, heads * size), BF16),
            pltpu.VMEM((rows, depth), BF16),
            pltpu.VMEM((heads, size, size), F32),
            pltpu.VMEM((heads, size, size), F32),
            pltpu.SemaphoreType.DMA((n_head + 1,)),
        ],
    )
    got, local, reach = tie(got, local, reach)
    (normed,) = call(
        output_kernel,
        [like(rows, heads * size, dtype=BF16)],
        [got, local, reach, gain],
    )
    (mixed,) = call(
        mix_own_kernel,
        [like(rows, width)],
        [here, w_out, normed],
        1,
        1,
        [pltpu.VMEM((heads * size, width), BF16), pltpu.SemaphoreType.DMA(())],
    )
    parts, mixed = spread(normed, mixed)
    (mixed,) = call(
        functools.partial(mix_kernel, n_head - 2),
        [like(rows, width)],
        [mixed, *parts[:-1], *out_weights[:-1]],
    )
    return call(
        functools.partial(mix_kernel, 1),
        [like(rows, width, dtype=BF16)],
        [mixed, parts[-1], out_weights[-1]],
    )[0]


def solution(mesh):
    n_seq, n_head = mesh.shape["seq"], mesh.shape["head"]
    return jax.shard_map(
        functools.partial(shards, n_seq, n_head),
        mesh=mesh,
        in_specs=(
            P("seq", "head"),
            P(None, "head"),
            P(None, "head"),
            P(None, "head"),
            P("seq", "head"),
            P("seq", "head"),
            P(),
            P("head", None),
        ),
        out_specs=P("seq", "head"),
        check_vma=False,
    )
```

```python
import functools
import jax
import jax.numpy as jnp
from jax import lax
from jax.experimental import pallas as pl
from jax.experimental.pallas import tpu as pltpu
from jax.sharding import PartitionSpec as P

BASE = 16
F32 = jnp.float32
BF16 = jnp.bfloat16


def split(x):
    high = x.astype(BF16)
    return high, (x - high.astype(F32)).astype(BF16)


def contract(a, b, dims):
    return lax.dot_general(a, b, (dims, ((), ())), preferred_element_type=F32)


NN = ((1,), (0,))
NT = ((1,), (1,))


def dot3(a, b, dims=NN):
    left = jnp.concatenate([a[0], a[1], a[0]], dims[0][0])
    right = jnp.concatenate([b[0], b[0], b[1]], dims[1][0])
    return contract(left, right, dims)


def gate_tables(codes, beta, decay_ref, strict_ref, cols_ref, grown_ref):
    heads, rows = codes.shape
    tok = lax.broadcasted_iota(jnp.int32, (rows, rows), 0)
    other = lax.broadcasted_iota(jnp.int32, (rows, rows), 1)
    ones = jnp.where(tok <= other, 1.0, 0.0).astype(BF16)
    sums = [
        contract(p.astype(F32).astype(BF16), ones, NN)
        for p in (codes >> 14, (codes >> 7) & 127, codes & 127)
    ]
    logs = -(sums[0] * 16384.0 + sums[1] * 128.0 + sums[2]) / 2097152.0
    beta = beta.astype(F32) / 256.0
    logs_t = jnp.transpose(logs)
    beta_t = jnp.transpose(beta)
    for h in range(heads):
        row = logs[h : h + 1, :]
        col = jnp.broadcast_to(logs_t[:, h : h + 1], (rows, rows))
        gap = col - row
        decay_ref[h] = jnp.where(tok >= other, jnp.exp(jnp.where(tok >= other, gap, 0.0)), 0.0)
        grown = jnp.exp(col)
        beta_col = jnp.broadcast_to(beta_t[:, h : h + 1], (rows, rows))
        strict_ref[h] = jnp.where(tok > other, decay_ref[h] * beta_col, 0.0)
        grown_ref[h] = grown
        cols_ref[h, 0] = beta_col * grown
        cols_ref[h, 1] = beta_col
        cols_ref[h, 2] = jnp.exp(row[:, rows - 1 :] - col)


def copy_all(moves, sems):
    copies = [pltpu.make_async_copy(a, b, sems.at[i]) for i, (a, b) in enumerate(moves)]
    for copy in copies:
        copy.start()
    return copies


def block_of(place, d, depth):
    return pl.ds(pl.multiple_of((place ^ d) * depth, depth), depth)


def out_slices(place, wo_hbm, out_refs, first):
    width = out_refs[0].shape[1]
    return [
        (wo_hbm.at[:, block_of(place, first + i, width)], ref) for i, ref in enumerate(out_refs)
    ]


def prepare_kernel(n_head, place_ref, tok_hbm, wk_hbm, wv_hbm, wo_hbm, gate_hbm, beta_hbm, gain_hbm, *refs):
    acc_ref, rest_ref, decay_ref, strict_ref, cols_ref, grown_ref, gain_ref = refs[:7]
    out_refs = refs[7:-5]
    tok_ref, own_ref, gate_ref, beta_ref, sems = refs[-5:]
    place = place_ref[0]
    depth = tok_ref.shape[1]
    weights = (wk_hbm, wv_hbm)
    moves = [(gate_hbm, gate_ref), (beta_hbm, beta_ref), (gain_hbm, gain_ref), (tok_hbm, tok_ref)]
    moves += [(w.at[block_of(place, 0, depth), :], own_ref.at[i]) for i, w in enumerate(weights)]
    moves += [
        (w.at[block_of(place, d, depth), :], rest_ref.at[d - 1, i])
        for d in range(1, n_head)
        for i, w in enumerate(weights)
    ]
    moves += out_slices(place, wo_hbm, out_refs, n_head - len(out_refs))
    copies = copy_all(moves, sems)
    copies[0].wait()
    copies[1].wait()
    gate_tables(gate_ref[...], beta_ref[...], decay_ref, strict_ref, cols_ref, grown_ref)
    for copy in copies[2:6]:
        copy.wait()
    for i in range(len(weights)):
        acc_ref[i] = contract(tok_ref[...], own_ref[i], NN)
    for copy in copies[6:]:
        copy.wait()


def more_kernel(n_pieces, acc_ref, rest_ref, *refs):
    out_ref = refs[-1]
    for i in range(acc_ref.shape[0]):
        total = acc_ref[i]
        for d in range(n_pieces):
            total = total + contract(refs[d][...], rest_ref[d, i], NN)
        out_ref[i] = total


def solve_lower(lowers, rights):
    rows = lowers[0].shape[0]
    blocks = rows // BASE
    tok = lax.broadcasted_iota(jnp.int32, (rows, rows), 0)
    other = lax.broadcasted_iota(jnp.int32, (rows, rows), 1)
    lane = lax.broadcasted_iota(jnp.int32, (BASE, rows), 1)
    sub = lax.broadcasted_iota(jnp.int32, (BASE, rows), 0)
    diagonal = []
    for lower in lowers:
        compact = jnp.zeros((BASE, rows), F32)
        for b in range(blocks):
            compact = compact + jnp.where(
                lane // BASE == b, lower[b * BASE : (b + 1) * BASE, :], 0.0
            )
        solved = jnp.where(sub == lane % BASE, 1.0, 0.0)
        for j in range(BASE - 1):
            column = jnp.take_along_axis(compact, (lane // BASE) * BASE + j, axis=1)
            solved = solved - column * solved[j : j + 1, :]
        inside = tok // BASE == other // BASE
        diagonal.append(split(jnp.where(inside, jnp.concatenate([solved] * blocks, 0), 0.0)))
    results = [dot3(d, r) for d, r in zip(diagonal, rights)]
    if blocks == 1:
        return results
    step = [
        dot3(d, split(jnp.where(tok // BASE == other // BASE, 0.0, lower)))
        for d, lower in zip(diagonal, lowers)
    ]
    step = [split(x) for x in step]
    covered = 1
    while True:
        top = covered * BASE
        lowest = [tuple(part[top:] for part in v) for v in step]
        sign = -1.0 if covered == 1 else 1.0
        changes = [dot3(v, split(x)) for v, x in zip(lowest, results)]
        results = [
            jnp.concatenate([x[:top], x[top:] + sign * change], 0)
            for x, change in zip(results, changes)
        ]
        covered *= 2
        if covered >= blocks:
            return results
        powers = [dot3(tuple(part[covered * BASE :] for part in v), v) for v in step]
        empty = jnp.zeros((covered * BASE, rows), F32)
        step = [split(jnp.concatenate([empty, power], 0)) for power in powers]


def summary_kernel(size, acc_ref, rest_ref, piece_ref, strict_ref, cols_ref, grown_ref, send_ref, keys_ref, wy_ref):
    heads, rows, _ = strict_ref.shape
    last = rest_ref.shape[0] - 1
    keys = acc_ref[0] + contract(piece_ref[...], rest_ref[last, 0], NN)
    values = acc_ref[1] + contract(piece_ref[...], rest_ref[last, 1], NN)
    every = range(heads)
    each = [keys[:, h * size : (h + 1) * size] for h in every]
    scales = [lax.rsqrt(jnp.sum(key * key, -1, keepdims=True) + 1e-06) for key in each]
    each = [key * scale for key, scale in zip(each, scales)]
    halves = [split(key) for key in each]
    lowers = [dot3(halves[h], halves[h], NT) * strict_ref[h] for h in every]
    tails = [split(jnp.transpose(each[h] * cols_ref[h, 2])) for h in every]
    rights = [
        jnp.concatenate(
            [each[h] * cols_ref[h, 0], values[:, h * size : (h + 1) * size] * cols_ref[h, 1]], 1
        )
        for h in every
    ]
    solved = solve_lower(lowers, [split(right) for right in rights])
    eye = lax.broadcasted_iota(jnp.int32, (size, size), 0) == lax.broadcasted_iota(
        jnp.int32, (size, size), 1
    )
    both = [dot3(tails[h], split(solved[h])) for h in every]
    for h in every:
        step = jnp.where(eye, grown_ref[h, rows - 1 :, :], 0.0) - both[h][:, :size]
        send_ref[h, :, :size] = step.astype(BF16)
        send_ref[h, :, size:] = both[h][:, size:].astype(BF16)
        keys_ref[h] = each[h]
        wy_ref[h] = solved[h]


def apply(step, early):
    if step.dtype == BF16 and early.dtype == BF16:
        return contract(step, early, NN)
    if step.dtype == BF16:
        high, low = split(early)
        return contract(
            jnp.concatenate([step, step], 1), jnp.concatenate([high, low], 0), NN
        )
    return apply(step.astype(BF16), early)


def follow(early, late):
    size = early[0].shape[0]
    moved = [apply(late[h][:, :size], early[h]) for h in range(len(early))]
    return [moved[h] + late[h][:, size:].astype(F32) for h in range(len(early))]


def join(early, late):
    every = range(len(early))
    size = early[0].shape[0]
    both = [apply(late[h][:, :size], early[h]) for h in every]
    add = [both[h][:, size:] + late[h][:, size:].astype(F32) for h in every]
    return [jnp.concatenate([both[h][:, :size], add[h]], 1) for h in every]


def parts_of(place, own_ref, got_refs):
    refs = [own_ref, *got_refs]
    return [[refs[i ^ place][h] for h in range(own_ref.shape[0])] for i in range(len(refs))]


def total_of(parts):
    if len(parts) == 2:
        return join(*parts)
    return join(join(parts[0], parts[1]), join(parts[2], parts[3]))


def before(place, parts):
    if place:
        pair = parts[0]
        for part in parts[1:place]:
            pair = join(pair, part)
        return pair
    size = parts[0][0].shape[0]
    row = lax.broadcasted_iota(jnp.int32, (size, 2 * size), 0)
    column = lax.broadcasted_iota(jnp.int32, (size, 2 * size), 1)
    return [jnp.where(row == column, 1.0, 0.0).astype(BF16)] * len(parts[0])


def at_place(radix, place_ref, run):
    for place in range(radix):
        pl.when(place_ref[0] == place)(functools.partial(run, place))


def enter(pair, new_map_ref, new_add_ref, pmap_ref=None, padd_ref=None):
    size = new_map_ref.shape[1]
    for h in range(len(pair)):
        if pmap_ref is None:
            new_map_ref[h] = pair[h][:, :size].astype(F32)
            new_add_ref[h] = pair[h][:, size:].astype(F32)
        else:
            both = apply(pmap_ref[h], pair[h])
            new_map_ref[h] = both[:, :size]
            new_add_ref[h] = both[:, size:] + padd_ref[h]


def merge_kernel(radix, place_ref, *refs):
    got_refs, own_ref, prefix_refs = refs[: radix - 1], refs[radix - 1], refs[radix:-3]
    new_map_ref, new_add_ref, send_ref = refs[-3:]

    def run(place):
        parts = parts_of(place, own_ref, got_refs)
        total = total_of(parts)
        enter(before(place, parts), new_map_ref, new_add_ref, *prefix_refs)
        for h in range(len(total)):
            send_ref[h] = total[h].astype(BF16)

    at_place(radix, place_ref, run)


def total_kernel(radix, place_ref, upper_ref, *refs):
    got_refs, own_ref, send_ref = refs[: radix - 1], refs[radix - 1], refs[-1]
    heads, size, _ = own_ref.shape

    def run(place):
        parts = parts_of(place, own_ref, got_refs)
        add = follow([part[:, size:] for part in parts[0]], parts[1])
        if radix > 2:
            add = follow(add, join(parts[2], parts[3]))
        for h in range(heads):
            send_ref[h] = add[h].astype(BF16)

    @pl.when(upper_ref[0] == 0)
    def _():
        at_place(radix, place_ref, run)

    @pl.when(upper_ref[0] > 0)
    def _():
        send_ref[...] = jnp.zeros_like(send_ref)


def local_kernel(n_head, radix, place_ref, turn_ref, wq_hbm, tok_hbm, *refs):
    pieces, refs = refs[: n_head - 1], refs[n_head - 1 :]
    decay_ref, grown_ref, keys_ref, wy_ref, *refs = refs
    got_refs, own_ref, prefix_refs = refs[: radix - 1], refs[radix - 1], refs[radix:-7]
    out_ref, reach_ref, wq_ref, tok_ref, pmap_ref, padd_ref, sems = refs[-7:]
    heads, size, _ = padd_ref.shape
    every = range(heads)
    depth = tok_ref.shape[1]
    moves = [(tok_hbm, tok_ref)]
    moves += [
        (wq_hbm.at[block_of(place_ref[0], d, depth), :], wq_ref.at[d]) for d in range(n_head)
    ]
    copies = copy_all(moves, sems)

    def run(place):
        parts = parts_of(place, own_ref, got_refs)
        enter(before(place, parts), pmap_ref, padd_ref, *prefix_refs)

    at_place(radix, turn_ref, run)
    for copy in copies:
        copy.wait()
    queries = contract(tok_ref[...], wq_ref[0], NN)
    for d in range(1, n_head):
        queries = queries + contract(pieces[d - 1][...], wq_ref[d], NN)
    queries = [queries[:, h * size : (h + 1) * size] for h in every]
    dots = [dot3(split(queries[h]), split(keys_ref[h]), NT) * decay_ref[h] for h in every]
    both = [dot3(split(dots[h]), split(wy_ref[h])) for h in every]
    reach = [split(queries[h] * grown_ref[h] - both[h][:, :size]) for h in every]
    out = [both[h][:, size:] + dot3(reach[h], split(padd_ref[h])) for h in every]
    later = [dot3(reach[h], split(pmap_ref[h])) for h in every]
    for h in every:
        out_ref[h] = out[h]
        reach_ref[h] = jnp.concatenate(split(later[h]), 1)


def output_kernel(upper_ref, got_ref, local_ref, reach_ref, gain_ref, normed_ref):
    heads, size, _ = got_ref.shape

    def finish(outs):
        scales = [lax.rsqrt(jnp.mean(out * out, -1, keepdims=True) + 1e-06) for out in outs]
        for h in range(heads):
            normed = outs[h] * scales[h] * gain_ref[...]
            normed_ref[:, h * size : (h + 1) * size] = normed.astype(BF16)

    @pl.when(upper_ref[0] == 0)
    def _():
        finish([local_ref[h] for h in range(heads)])

    @pl.when(upper_ref[0] > 0)
    def _():
        got = [jnp.concatenate([got_ref[h]] * 2, 0) for h in range(heads)]
        finish([local_ref[h] + contract(reach_ref[h], got[h], NN) for h in range(heads)])


def mix_own_kernel(place_ref, wo_hbm, part_ref, out_ref, weight_ref, sem):
    width = weight_ref.shape[1]
    copy = pltpu.make_async_copy(wo_hbm.at[:, block_of(place_ref[0], 0, width)], weight_ref, sem)
    copy.start()
    copy.wait()
    out_ref[...] = contract(part_ref[...], weight_ref[...], NN)


def mix_kernel(n_pieces, base_ref, *refs):
    total = base_ref[...]
    for part, weight in zip(refs[:n_pieces], refs[n_pieces : 2 * n_pieces]):
        total = total + contract(part[...], weight[...], NN)
    refs[-1][...] = total.astype(refs[-1].dtype)


def call(kernel, outs, args, scalars=0, hbm=0, scratch=()):
    vmem = pl.BlockSpec(memory_space=pltpu.VMEM)
    far = pl.BlockSpec(memory_space=pltpu.HBM)
    specs = [pl.BlockSpec(memory_space=pltpu.SMEM)] * scalars + [far] * hbm
    specs += [vmem] * (len(args) - scalars - hbm)
    args = [
        pltpu.with_memory_space_constraint(a, pltpu.HBM) if scalars <= i < scalars + hbm else a
        for i, a in enumerate(args)
    ]
    return pl.pallas_call(
        kernel,
        out_shape=outs,
        in_specs=specs,
        out_specs=[vmem] * len(outs),
        scratch_shapes=scratch,
        compiler_params=pltpu.CompilerParams(vmem_limit_bytes=16 * 1024 * 1024),
    )(*args)


def like(*shape, dtype=F32):
    return jax.ShapeDtypeStruct(shape, dtype)


def shards(n_seq, n_head, tokens, w_query, w_key, w_value, gate_codes, beta_codes, norm_gain, w_out):
    rows, depth = tokens.shape
    heads = gate_codes.shape[1]
    size = norm_gain.shape[0]
    width = w_out.shape[1] // n_head
    place = lax.axis_index("head")
    turn = lax.axis_index("seq")

    def swap(x, axis, count, d):
        return lax.ppermute(x, axis, [(i, i ^ d) for i in range(count)])

    def tie(*x):
        return lax.optimization_barrier(x)

    def spread(x, during):
        d = n_head // 2
        have = {d: swap(x, "head", n_head, d)}
        have[d], extra = tie(have[d], during)
        while d > 1:
            d //= 2
            have.update({e ^ d: swap(have[e], "head", n_head, d) for e in list(have)})
            have[d] = swap(x, "head", n_head, d)
        return [have[d] for d in range(1, n_head)], extra

    here = place.astype(jnp.int32).reshape(1)
    slice_out = like(heads * size, width, dtype=BF16)
    acc, rest, decay, strict, cols, grown, gain, *slices = call(
        functools.partial(prepare_kernel, n_head),
        [
            like(2, rows, heads * size),
            like(n_head - 1, 2, depth, heads * size, dtype=BF16),
            like(heads, rows, rows),
            like(heads, rows, rows),
            like(heads, 3, rows, size),
            like(heads, rows, size),
            like(1, size),
        ]
        + [slice_out] * (n_head - 1),
        [here, tokens, w_key, w_value, w_out, gate_codes.T, beta_codes.T, norm_gain.reshape(1, size)],
        1,
        7,
        [
            pltpu.VMEM((rows, depth), BF16),
            pltpu.VMEM((2, depth, heads * size), BF16),
            pltpu.VMEM((heads, rows), jnp.int32),
            pltpu.VMEM((heads, rows), jnp.int32),
            pltpu.SemaphoreType.DMA((3 + 3 * n_head,)),
        ],
    )
    pieces, (acc, rest) = spread(tokens, (acc, rest))
    (acc,) = call(
        functools.partial(more_kernel, n_head - 2),
        [like(2, rows, heads * size)],
        [acc, rest, *pieces[:-1]],
    )
    state = like(heads, size, size)
    state_sent = like(heads, size, size, dtype=BF16)
    pair_sent = like(heads, size, 2 * size, dtype=BF16)
    send, keys, solved = call(
        functools.partial(summary_kernel, size),
        [pair_sent, like(heads, rows, size), like(heads, rows, 2 * size)],
        [acc, rest, pieces[-1], strict, cols, grown],
    )
    send, *slices = tie(send, *slices)
    out_weights = [swap(slices[d - 1], "head", n_head, d) for d in range(1, n_head)]
    prefix = []
    d = 1
    while 2 * d < n_seq:
        radix = 4 if 4 * d < n_seq else 2
        last = 2 * radix * d >= n_seq
        if radix == 4:
            got = [swap(send, "seq", n_seq, i * d) for i in (3, 2, 1)][::-1]
        else:
            got = [swap(send, "seq", n_seq, d)]
        place_in = (turn // d) % radix
        place_in = place_in.astype(jnp.int32).reshape(1)
        merged = [place_in, *got, send, *prefix]
        d *= radix
        if last:
            upper = ((turn // d) % 2).astype(jnp.int32).reshape(1)
            (send,) = call(
                functools.partial(total_kernel, radix),
                [state_sent],
                [place_in, upper, *merged[1 : radix + 1]],
                2,
            )
        else:
            *prefix, send = call(
                functools.partial(merge_kernel, radix), [state, state, pair_sent], merged, 1
            )
    got = swap(send, "seq", n_seq, d)
    local, reach = call(
        functools.partial(local_kernel, n_head, radix),
        [like(heads, rows, size), like(heads, rows, 2 * size, dtype=BF16)],
        [here, merged[0], w_query, tokens, *pieces, decay, grown, keys, solved, *merged[1:]],
        2,
        2,
        [
            pltpu.VMEM((n_head, depth, heads * size), BF16),
            pltpu.VMEM((rows, depth), BF16),
            pltpu.VMEM((heads, size, size), F32),
            pltpu.VMEM((heads, size, size), F32),
            pltpu.SemaphoreType.DMA((n_head + 1,)),
        ],
    )
    got, local, reach = tie(got, local, reach)
    (normed,) = call(
        output_kernel,
        [like(rows, heads * size, dtype=BF16)],
        [upper, got, local, reach, gain],
        1,
    )
    (mixed,) = call(
        mix_own_kernel,
        [like(rows, width)],
        [here, w_out, normed],
        1,
        1,
        [pltpu.VMEM((heads * size, width), BF16), pltpu.SemaphoreType.DMA(())],
    )
    parts, mixed = spread(normed, mixed)
    (mixed,) = call(
        functools.partial(mix_kernel, n_head - 2),
        [like(rows, width)],
        [mixed, *parts[:-1], *out_weights[:-1]],
    )
    return call(
        functools.partial(mix_kernel, 1),
        [like(rows, width, dtype=BF16)],
        [mixed, parts[-1], out_weights[-1]],
    )[0]


def solution(mesh):
    n_seq, n_head = mesh.shape["seq"], mesh.shape["head"]
    return jax.shard_map(
        functools.partial(shards, n_seq, n_head),
        mesh=mesh,
        in_specs=(
            P("seq", "head"),
            P(None, "head"),
            P(None, "head"),
            P(None, "head"),
            P("seq", "head"),
            P("seq", "head"),
            P(),
            P("head", None),
        ),
        out_specs=P("seq", "head"),
        check_vma=False,
    )
```

```python
import functools
import jax
import jax.numpy as jnp
from jax import lax
from jax.experimental import pallas as pl
from jax.experimental.pallas import tpu as pltpu
from jax.sharding import PartitionSpec as P

BASE = 16
F32 = jnp.float32
BF16 = jnp.bfloat16


def split(x):
    high = x.astype(BF16)
    return high, (x - high.astype(F32)).astype(BF16)


def contract(a, b, dims):
    return lax.dot_general(a, b, (dims, ((), ())), preferred_element_type=F32)


NN = ((1,), (0,))
NT = ((1,), (1,))


def dot3(a, b, dims=NN):
    left = jnp.concatenate([a[0], a[1], a[0]], dims[0][0])
    right = jnp.concatenate([b[0], b[0], b[1]], dims[1][0])
    return contract(left, right, dims)


def gate_tables(codes, beta, decay_ref, strict_ref, cols_ref, grown_ref):
    heads, rows = codes.shape
    tok = lax.broadcasted_iota(jnp.int32, (rows, rows), 0)
    other = lax.broadcasted_iota(jnp.int32, (rows, rows), 1)
    ones = jnp.where(tok <= other, 1.0, 0.0).astype(BF16)
    sums = [
        contract(p.astype(F32).astype(BF16), ones, NN)
        for p in (codes >> 14, (codes >> 7) & 127, codes & 127)
    ]
    logs = -(sums[0] * 16384.0 + sums[1] * 128.0 + sums[2]) / 2097152.0
    beta = beta.astype(F32) / 256.0
    logs_t = jnp.transpose(logs)
    beta_t = jnp.transpose(beta)
    for h in range(heads):
        row = logs[h : h + 1, :]
        col = jnp.broadcast_to(logs_t[:, h : h + 1], (rows, rows))
        gap = col - row
        decay_ref[h] = jnp.where(tok >= other, jnp.exp(jnp.where(tok >= other, gap, 0.0)), 0.0)
        grown = jnp.exp(col)
        beta_col = jnp.broadcast_to(beta_t[:, h : h + 1], (rows, rows))
        strict_ref[h] = jnp.where(tok > other, decay_ref[h] * beta_col, 0.0)
        grown_ref[h] = grown
        cols_ref[h, 0] = beta_col * grown
        cols_ref[h, 1] = beta_col
        cols_ref[h, 2] = jnp.exp(row[:, rows - 1 :] - col)


def copy_all(moves, sems):
    copies = [pltpu.make_async_copy(a, b, sems.at[i]) for i, (a, b) in enumerate(moves)]
    for copy in copies:
        copy.start()
    return copies


def block_of(place, d, depth):
    return pl.ds(pl.multiple_of((place ^ d) * depth, depth), depth)


def out_slices(place, wo_hbm, out_refs, first):
    width = out_refs[0].shape[1]
    return [
        (wo_hbm.at[:, block_of(place, first + i, width)], ref) for i, ref in enumerate(out_refs)
    ]


def prepare_kernel(n_head, place_ref, tok_hbm, wk_hbm, wv_hbm, wo_hbm, gate_hbm, beta_hbm, gain_hbm, *refs):
    acc_ref, rest_ref, decay_ref, strict_ref, cols_ref, grown_ref, gain_ref = refs[:7]
    out_refs = refs[7:-5]
    tok_ref, own_ref, gate_ref, beta_ref, sems = refs[-5:]
    place = place_ref[0]
    depth = tok_ref.shape[1]
    weights = (wk_hbm, wv_hbm)
    moves = [(gate_hbm, gate_ref), (beta_hbm, beta_ref), (gain_hbm, gain_ref), (tok_hbm, tok_ref)]
    moves += [(w.at[block_of(place, 0, depth), :], own_ref.at[i]) for i, w in enumerate(weights)]
    moves += [
        (w.at[block_of(place, d, depth), :], rest_ref.at[d - 1, i])
        for d in range(1, n_head)
        for i, w in enumerate(weights)
    ]
    moves += out_slices(place, wo_hbm, out_refs, n_head - len(out_refs))
    copies = copy_all(moves, sems)
    copies[0].wait()
    copies[1].wait()
    gate_tables(gate_ref[...], beta_ref[...], decay_ref, strict_ref, cols_ref, grown_ref)
    for copy in copies[2:6]:
        copy.wait()
    for i in range(len(weights)):
        acc_ref[i] = contract(tok_ref[...], own_ref[i], NN)
    for copy in copies[6:]:
        copy.wait()


def more_kernel(n_pieces, acc_ref, rest_ref, *refs):
    out_ref = refs[-1]
    for i in range(acc_ref.shape[0]):
        total = acc_ref[i]
        for d in range(n_pieces):
            total = total + contract(refs[d][...], rest_ref[d, i], NN)
        out_ref[i] = total


def solve_lower(lowers, rights):
    rows = lowers[0].shape[0]
    blocks = rows // BASE
    tok = lax.broadcasted_iota(jnp.int32, (rows, rows), 0)
    other = lax.broadcasted_iota(jnp.int32, (rows, rows), 1)
    lane = lax.broadcasted_iota(jnp.int32, (BASE, rows), 1)
    sub = lax.broadcasted_iota(jnp.int32, (BASE, rows), 0)
    diagonal = []
    for lower in lowers:
        compact = jnp.zeros((BASE, rows), F32)
        for b in range(blocks):
            compact = compact + jnp.where(
                lane // BASE == b, lower[b * BASE : (b + 1) * BASE, :], 0.0
            )
        solved = jnp.where(sub == lane % BASE, 1.0, 0.0)
        for j in range(BASE - 1):
            column = jnp.take_along_axis(compact, (lane // BASE) * BASE + j, axis=1)
            solved = solved - column * solved[j : j + 1, :]
        inside = tok // BASE == other // BASE
        diagonal.append(split(jnp.where(inside, jnp.concatenate([solved] * blocks, 0), 0.0)))
    if blocks == 1:
        return [dot3(d, r) for d, r in zip(diagonal, rights)]
    wide = rights[0][0].shape[1]
    outside = tok // BASE != other // BASE
    links = [split(jnp.where(outside, lower, 0.0)) for lower in lowers]
    both = [
        dot3(d, tuple(jnp.concatenate(x, 1) for x in zip(r, link)))
        for d, r, link in zip(diagonal, rights, links)
    ]
    sign, covered = -1.0, 1
    while covered < blocks:
        top = covered * BASE
        halves = [split(x) for x in both]
        last = 2 * covered >= blocks
        keep = wide if last else wide + rows
        moved = [
            dot3(tuple(x[top:, wide:] for x in half), tuple(x[:, :keep] for x in half))
            for half in halves
        ]
        results = [
            jnp.concatenate([x[:top, :wide], x[top:, :wide] + sign * m[:, :wide]], 0)
            for x, m in zip(both, moved)
        ]
        if last:
            return results
        empty = jnp.zeros((top, rows), F32)
        both = [
            jnp.concatenate([x, jnp.concatenate([empty, m[:, wide:]], 0)], 1)
            for x, m in zip(results, moved)
        ]
        sign, covered = 1.0, 2 * covered


def summary_kernel(size, acc_ref, rest_ref, piece_ref, strict_ref, cols_ref, grown_ref, send_ref, keys_ref, wy_ref):
    heads, rows, _ = strict_ref.shape
    last = rest_ref.shape[0] - 1
    keys = acc_ref[0] + contract(piece_ref[...], rest_ref[last, 0], NN)
    values = acc_ref[1] + contract(piece_ref[...], rest_ref[last, 1], NN)
    every = range(heads)
    each = [keys[:, h * size : (h + 1) * size] for h in every]
    scales = [lax.rsqrt(jnp.sum(key * key, -1, keepdims=True) + 1e-06) for key in each]
    each = [key * scale for key, scale in zip(each, scales)]
    halves = [split(key) for key in each]
    lowers = [dot3(halves[h], halves[h], NT) * strict_ref[h] for h in every]
    tails = [split(jnp.transpose(each[h] * cols_ref[h, 2])) for h in every]
    rights = [
        jnp.concatenate(
            [each[h] * cols_ref[h, 0], values[:, h * size : (h + 1) * size] * cols_ref[h, 1]], 1
        )
        for h in every
    ]
    solved = solve_lower(lowers, [split(right) for right in rights])
    eye = lax.broadcasted_iota(jnp.int32, (size, size), 0) == lax.broadcasted_iota(
        jnp.int32, (size, size), 1
    )
    both = [dot3(tails[h], split(solved[h])) for h in every]
    for h in every:
        step = jnp.where(eye, grown_ref[h, rows - 1 :, :], 0.0) - both[h][:, :size]
        send_ref[h, :, :size] = step.astype(BF16)
        send_ref[h, :, size:] = both[h][:, size:].astype(BF16)
        keys_ref[h] = each[h]
        wy_ref[h] = solved[h]


def apply(step, early):
    if step.dtype == BF16 and early.dtype == BF16:
        return contract(step, early, NN)
    if step.dtype == BF16:
        high, low = split(early)
        return contract(
            jnp.concatenate([step, step], 1), jnp.concatenate([high, low], 0), NN
        )
    return apply(step.astype(BF16), early)


def follow(early, late):
    size = early[0].shape[0]
    moved = [apply(late[h][:, :size], early[h]) for h in range(len(early))]
    return [moved[h] + late[h][:, size:].astype(F32) for h in range(len(early))]


def join(early, late):
    every = range(len(early))
    size = early[0].shape[0]
    both = [apply(late[h][:, :size], early[h]) for h in every]
    add = [both[h][:, size:] + late[h][:, size:].astype(F32) for h in every]
    return [jnp.concatenate([both[h][:, :size], add[h]], 1) for h in every]


def parts_of(place, own_ref, got_refs):
    refs = [own_ref, *got_refs]
    return [[refs[i ^ place][h] for h in range(own_ref.shape[0])] for i in range(len(refs))]


def total_of(parts):
    if len(parts) == 2:
        return join(*parts)
    return join(join(parts[0], parts[1]), join(parts[2], parts[3]))


def before(place, parts):
    if place:
        pair = parts[0]
        for part in parts[1:place]:
            pair = join(pair, part)
        return pair
    size = parts[0][0].shape[0]
    row = lax.broadcasted_iota(jnp.int32, (size, 2 * size), 0)
    column = lax.broadcasted_iota(jnp.int32, (size, 2 * size), 1)
    return [jnp.where(row == column, 1.0, 0.0).astype(BF16)] * len(parts[0])


def at_place(radix, place_ref, run):
    for place in range(radix):
        pl.when(place_ref[0] == place)(functools.partial(run, place))


def enter(pair, new_map_ref, new_add_ref, pmap_ref=None, padd_ref=None):
    size = new_map_ref.shape[1]
    for h in range(len(pair)):
        if pmap_ref is None:
            new_map_ref[h] = pair[h][:, :size].astype(F32)
            new_add_ref[h] = pair[h][:, size:].astype(F32)
        else:
            both = apply(pmap_ref[h], pair[h])
            new_map_ref[h] = both[:, :size]
            new_add_ref[h] = both[:, size:] + padd_ref[h]


def merge_kernel(radix, place_ref, *refs):
    got_refs, own_ref, prefix_refs = refs[: radix - 1], refs[radix - 1], refs[radix:-3]
    new_map_ref, new_add_ref, send_ref = refs[-3:]

    def run(place):
        parts = parts_of(place, own_ref, got_refs)
        total = total_of(parts)
        enter(before(place, parts), new_map_ref, new_add_ref, *prefix_refs)
        for h in range(len(total)):
            send_ref[h] = total[h].astype(BF16)

    at_place(radix, place_ref, run)


def total_kernel(radix, place_ref, upper_ref, *refs):
    got_refs, own_ref, send_ref = refs[: radix - 1], refs[radix - 1], refs[-1]
    heads, size, _ = own_ref.shape

    def run(place):
        parts = parts_of(place, own_ref, got_refs)
        add = follow([part[:, size:] for part in parts[0]], parts[1])
        if radix > 2:
            add = follow(add, join(parts[2], parts[3]))
        for h in range(heads):
            send_ref[h] = add[h].astype(BF16)

    @pl.when(upper_ref[0] == 0)
    def _():
        at_place(radix, place_ref, run)

    @pl.when(upper_ref[0] > 0)
    def _():
        send_ref[...] = jnp.zeros_like(send_ref)


def local_kernel(n_head, radix, place_ref, turn_ref, wq_hbm, tok_hbm, *refs):
    pieces, refs = refs[: n_head - 1], refs[n_head - 1 :]
    decay_ref, grown_ref, keys_ref, wy_ref, *refs = refs
    got_refs, own_ref, prefix_refs = refs[: radix - 1], refs[radix - 1], refs[radix:-7]
    out_ref, reach_ref, wq_ref, tok_ref, pmap_ref, padd_ref, sems = refs[-7:]
    heads, size, _ = padd_ref.shape
    every = range(heads)
    depth = tok_ref.shape[1]
    moves = [(tok_hbm, tok_ref)]
    moves += [
        (wq_hbm.at[block_of(place_ref[0], d, depth), :], wq_ref.at[d]) for d in range(n_head)
    ]
    copies = copy_all(moves, sems)

    def run(place):
        parts = parts_of(place, own_ref, got_refs)
        enter(before(place, parts), pmap_ref, padd_ref, *prefix_refs)

    at_place(radix, turn_ref, run)
    for copy in copies:
        copy.wait()
    queries = contract(tok_ref[...], wq_ref[0], NN)
    for d in range(1, n_head):
        queries = queries + contract(pieces[d - 1][...], wq_ref[d], NN)
    queries = [queries[:, h * size : (h + 1) * size] for h in every]
    dots = [dot3(split(queries[h]), split(keys_ref[h]), NT) * decay_ref[h] for h in every]
    both = [dot3(split(dots[h]), split(wy_ref[h])) for h in every]
    reach = [split(queries[h] * grown_ref[h] - both[h][:, :size]) for h in every]
    out = [both[h][:, size:] + dot3(reach[h], split(padd_ref[h])) for h in every]
    later = [dot3(reach[h], split(pmap_ref[h])) for h in every]
    for h in every:
        out_ref[h] = out[h]
        reach_ref[h] = jnp.concatenate(split(later[h]), 1)


def output_kernel(upper_ref, got_ref, local_ref, reach_ref, gain_ref, normed_ref):
    heads, size, _ = got_ref.shape

    def finish(outs):
        scales = [lax.rsqrt(jnp.mean(out * out, -1, keepdims=True) + 1e-06) for out in outs]
        for h in range(heads):
            normed = outs[h] * scales[h] * gain_ref[...]
            normed_ref[:, h * size : (h + 1) * size] = normed.astype(BF16)

    @pl.when(upper_ref[0] == 0)
    def _():
        finish([local_ref[h] for h in range(heads)])

    @pl.when(upper_ref[0] > 0)
    def _():
        got = [jnp.concatenate([got_ref[h]] * 2, 0) for h in range(heads)]
        finish([local_ref[h] + contract(reach_ref[h], got[h], NN) for h in range(heads)])


def mix_own_kernel(place_ref, wo_hbm, part_ref, out_ref, weight_ref, sem):
    width = weight_ref.shape[1]
    copy = pltpu.make_async_copy(wo_hbm.at[:, block_of(place_ref[0], 0, width)], weight_ref, sem)
    copy.start()
    copy.wait()
    out_ref[...] = contract(part_ref[...], weight_ref[...], NN)


def mix_kernel(n_pieces, base_ref, *refs):
    total = base_ref[...]
    for part, weight in zip(refs[:n_pieces], refs[n_pieces : 2 * n_pieces]):
        total = total + contract(part[...], weight[...], NN)
    refs[-1][...] = total.astype(refs[-1].dtype)


def call(kernel, outs, args, scalars=0, hbm=0, scratch=()):
    vmem = pl.BlockSpec(memory_space=pltpu.VMEM)
    far = pl.BlockSpec(memory_space=pltpu.HBM)
    specs = [pl.BlockSpec(memory_space=pltpu.SMEM)] * scalars + [far] * hbm
    specs += [vmem] * (len(args) - scalars - hbm)
    args = [
        pltpu.with_memory_space_constraint(a, pltpu.HBM) if scalars <= i < scalars + hbm else a
        for i, a in enumerate(args)
    ]
    return pl.pallas_call(
        kernel,
        out_shape=outs,
        in_specs=specs,
        out_specs=[vmem] * len(outs),
        scratch_shapes=scratch,
        compiler_params=pltpu.CompilerParams(vmem_limit_bytes=16 * 1024 * 1024),
    )(*args)


def like(*shape, dtype=F32):
    return jax.ShapeDtypeStruct(shape, dtype)


def shards(n_seq, n_head, tokens, w_query, w_key, w_value, gate_codes, beta_codes, norm_gain, w_out):
    rows, depth = tokens.shape
    heads = gate_codes.shape[1]
    size = norm_gain.shape[0]
    width = w_out.shape[1] // n_head
    place = lax.axis_index("head")
    turn = lax.axis_index("seq")

    def swap(x, axis, count, d):
        return lax.ppermute(x, axis, [(i, i ^ d) for i in range(count)])

    def tie(*x):
        return lax.optimization_barrier(x)

    def spread(x, during):
        d = n_head // 2
        have = {d: swap(x, "head", n_head, d)}
        have[d], extra = tie(have[d], during)
        while d > 1:
            d //= 2
            have.update({e ^ d: swap(have[e], "head", n_head, d) for e in list(have)})
            have[d] = swap(x, "head", n_head, d)
        return [have[d] for d in range(1, n_head)], extra

    here = place.astype(jnp.int32).reshape(1)
    slice_out = like(heads * size, width, dtype=BF16)
    acc, rest, decay, strict, cols, grown, gain, *slices = call(
        functools.partial(prepare_kernel, n_head),
        [
            like(2, rows, heads * size),
            like(n_head - 1, 2, depth, heads * size, dtype=BF16),
            like(heads, rows, rows),
            like(heads, rows, rows),
            like(heads, 3, rows, size),
            like(heads, rows, size),
            like(1, size),
        ]
        + [slice_out] * (n_head - 1),
        [here, tokens, w_key, w_value, w_out, gate_codes.T, beta_codes.T, norm_gain.reshape(1, size)],
        1,
        7,
        [
            pltpu.VMEM((rows, depth), BF16),
            pltpu.VMEM((2, depth, heads * size), BF16),
            pltpu.VMEM((heads, rows), jnp.int32),
            pltpu.VMEM((heads, rows), jnp.int32),
            pltpu.SemaphoreType.DMA((3 + 3 * n_head,)),
        ],
    )
    pieces, (acc, rest) = spread(tokens, (acc, rest))
    (acc,) = call(
        functools.partial(more_kernel, n_head - 2),
        [like(2, rows, heads * size)],
        [acc, rest, *pieces[:-1]],
    )
    state = like(heads, size, size)
    state_sent = like(heads, size, size, dtype=BF16)
    pair_sent = like(heads, size, 2 * size, dtype=BF16)
    send, keys, solved = call(
        functools.partial(summary_kernel, size),
        [pair_sent, like(heads, rows, size), like(heads, rows, 2 * size)],
        [acc, rest, pieces[-1], strict, cols, grown],
    )
    send, *slices = tie(send, *slices)
    out_weights = [swap(slices[d - 1], "head", n_head, d) for d in range(1, n_head)]
    prefix = []
    d = 1
    while 2 * d < n_seq:
        radix = 4 if 4 * d < n_seq else 2
        last = 2 * radix * d >= n_seq
        if radix == 4:
            got = [swap(send, "seq", n_seq, i * d) for i in (3, 2, 1)][::-1]
        else:
            got = [swap(send, "seq", n_seq, d)]
        place_in = (turn // d) % radix
        place_in = place_in.astype(jnp.int32).reshape(1)
        merged = [place_in, *got, send, *prefix]
        d *= radix
        if last:
            upper = ((turn // d) % 2).astype(jnp.int32).reshape(1)
            (send,) = call(
                functools.partial(total_kernel, radix),
                [state_sent],
                [place_in, upper, *merged[1 : radix + 1]],
                2,
            )
        else:
            *prefix, send = call(
                functools.partial(merge_kernel, radix), [state, state, pair_sent], merged, 1
            )
    got = swap(send, "seq", n_seq, d)
    local, reach = call(
        functools.partial(local_kernel, n_head, radix),
        [like(heads, rows, size), like(heads, rows, 2 * size, dtype=BF16)],
        [here, merged[0], w_query, tokens, *pieces, decay, grown, keys, solved, *merged[1:]],
        2,
        2,
        [
            pltpu.VMEM((n_head, depth, heads * size), BF16),
            pltpu.VMEM((rows, depth), BF16),
            pltpu.VMEM((heads, size, size), F32),
            pltpu.VMEM((heads, size, size), F32),
            pltpu.SemaphoreType.DMA((n_head + 1,)),
        ],
    )
    got, local, reach = tie(got, local, reach)
    (normed,) = call(
        output_kernel,
        [like(rows, heads * size, dtype=BF16)],
        [upper, got, local, reach, gain],
        1,
    )
    (mixed,) = call(
        mix_own_kernel,
        [like(rows, width)],
        [here, w_out, normed],
        1,
        1,
        [pltpu.VMEM((heads * size, width), BF16), pltpu.SemaphoreType.DMA(())],
    )
    parts, mixed = spread(normed, mixed)
    (mixed,) = call(
        functools.partial(mix_kernel, n_head - 2),
        [like(rows, width)],
        [mixed, *parts[:-1], *out_weights[:-1]],
    )
    return call(
        functools.partial(mix_kernel, 1),
        [like(rows, width, dtype=BF16)],
        [mixed, parts[-1], out_weights[-1]],
    )[0]


def solution(mesh):
    n_seq, n_head = mesh.shape["seq"], mesh.shape["head"]
    return jax.shard_map(
        functools.partial(shards, n_seq, n_head),
        mesh=mesh,
        in_specs=(
            P("seq", "head"),
            P(None, "head"),
            P(None, "head"),
            P(None, "head"),
            P("seq", "head"),
            P("seq", "head"),
            P(),
            P("head", None),
        ),
        out_specs=P("seq", "head"),
        check_vma=False,
    )
```

```python
import functools
import jax
import jax.numpy as jnp
from jax import lax
from jax.experimental import pallas as pl
from jax.experimental.pallas import tpu as pltpu
from jax.sharding import PartitionSpec as P

BASE = 16
F32 = jnp.float32
BF16 = jnp.bfloat16


def split(x):
    high = x.astype(BF16)
    return high, (x - high.astype(F32)).astype(BF16)


def contract(a, b, dims):
    return lax.dot_general(a, b, (dims, ((), ())), preferred_element_type=F32)


NN = ((1,), (0,))
NT = ((1,), (1,))


def dot3(a, b, dims=NN):
    left = jnp.concatenate([a[0], a[1], a[0]], dims[0][0])
    right = jnp.concatenate([b[0], b[0], b[1]], dims[1][0])
    return contract(left, right, dims)


def gate_tables(codes, beta, decay_ref, strict_ref, cols_ref, grown_ref):
    heads, rows = codes.shape
    tok = lax.broadcasted_iota(jnp.int32, (rows, rows), 0)
    other = lax.broadcasted_iota(jnp.int32, (rows, rows), 1)
    ones = jnp.where(tok <= other, 1.0, 0.0).astype(BF16)
    sums = [
        contract(p.astype(F32).astype(BF16), ones, NN)
        for p in (codes >> 14, (codes >> 7) & 127, codes & 127)
    ]
    logs = -(sums[0] * 16384.0 + sums[1] * 128.0 + sums[2]) / 2097152.0
    beta = beta.astype(F32) / 256.0
    logs_t = jnp.transpose(logs)
    beta_t = jnp.transpose(beta)
    for h in range(heads):
        row = logs[h : h + 1, :]
        col = jnp.broadcast_to(logs_t[:, h : h + 1], (rows, rows))
        gap = col - row
        decay_ref[h] = jnp.where(tok >= other, jnp.exp(jnp.where(tok >= other, gap, 0.0)), 0.0)
        grown = jnp.exp(col)
        beta_col = jnp.broadcast_to(beta_t[:, h : h + 1], (rows, rows))
        strict_ref[h] = jnp.where(tok > other, decay_ref[h] * beta_col, 0.0)
        grown_ref[h] = grown
        cols_ref[h, 0] = beta_col * grown
        cols_ref[h, 1] = beta_col
        cols_ref[h, 2] = jnp.exp(row[:, rows - 1 :] - col)


def copy_all(moves, sems):
    copies = [pltpu.make_async_copy(a, b, sems.at[i]) for i, (a, b) in enumerate(moves)]
    for copy in copies:
        copy.start()
    return copies


def block_of(place, d, depth):
    return pl.ds(pl.multiple_of((place ^ d) * depth, depth), depth)


def out_slices(place, wo_hbm, out_refs, first):
    width = out_refs[0].shape[1]
    return [
        (wo_hbm.at[:, block_of(place, first + i, width)], ref) for i, ref in enumerate(out_refs)
    ]


def prepare_kernel(n_head, place_ref, tok_hbm, wk_hbm, wv_hbm, wo_hbm, gate_hbm, beta_hbm, gain_hbm, *refs):
    acc_ref, rest_ref, decay_ref, strict_ref, cols_ref, grown_ref, gain_ref = refs[:7]
    out_refs = refs[7:-5]
    tok_ref, own_ref, gate_ref, beta_ref, sems = refs[-5:]
    place = place_ref[0]
    depth = tok_ref.shape[1]
    weights = (wk_hbm, wv_hbm)
    moves = [(gate_hbm, gate_ref), (beta_hbm, beta_ref), (gain_hbm, gain_ref), (tok_hbm, tok_ref)]
    moves += [(w.at[block_of(place, 0, depth), :], own_ref.at[i]) for i, w in enumerate(weights)]
    moves += [
        (w.at[block_of(place, d, depth), :], rest_ref.at[d - 1, i])
        for d in range(1, n_head)
        for i, w in enumerate(weights)
    ]
    moves += out_slices(place, wo_hbm, out_refs, n_head - len(out_refs))
    copies = copy_all(moves, sems)
    copies[0].wait()
    copies[1].wait()
    gate_tables(gate_ref[...], beta_ref[...], decay_ref, strict_ref, cols_ref, grown_ref)
    for copy in copies[2:6]:
        copy.wait()
    for i in range(len(weights)):
        acc_ref[i] = contract(tok_ref[...], own_ref[i], NN)
    for copy in copies[6:]:
        copy.wait()


def more_kernel(n_pieces, acc_ref, rest_ref, *refs):
    out_ref = refs[-1]
    for i in range(acc_ref.shape[0]):
        total = acc_ref[i]
        for d in range(n_pieces):
            total = total + contract(refs[d][...], rest_ref[d, i], NN)
        out_ref[i] = total


def solve_lower(lowers, rights):
    rows = lowers[0].shape[0]
    blocks = rows // BASE
    tok = lax.broadcasted_iota(jnp.int32, (rows, rows), 0)
    other = lax.broadcasted_iota(jnp.int32, (rows, rows), 1)
    lane = lax.broadcasted_iota(jnp.int32, (BASE, rows), 1)
    sub = lax.broadcasted_iota(jnp.int32, (BASE, rows), 0)
    diagonal = []
    for lower in lowers:
        compact = jnp.zeros((BASE, rows), F32)
        for b in range(blocks):
            compact = compact + jnp.where(
                lane // BASE == b, lower[b * BASE : (b + 1) * BASE, :], 0.0
            )
        solved = jnp.where(sub == lane % BASE, 1.0, 0.0)
        for j in range(BASE - 1):
            column = jnp.take_along_axis(compact, (lane // BASE) * BASE + j, axis=1)
            solved = solved - column * solved[j : j + 1, :]
        inside = tok // BASE == other // BASE
        diagonal.append(split(jnp.where(inside, jnp.concatenate([solved] * blocks, 0), 0.0)))
    if blocks == 1:
        return [dot3(d, r) for d, r in zip(diagonal, rights)]
    wide = rights[0][0].shape[1]
    outside = tok // BASE != other // BASE
    links = [split(jnp.where(outside, lower, 0.0)) for lower in lowers]
    both = [
        dot3(d, tuple(jnp.concatenate(x, 1) for x in zip(r, link)))
        for d, r, link in zip(diagonal, rights, links)
    ]
    sign, covered = -1.0, 1
    while covered < blocks:
        top = covered * BASE
        halves = [split(x) for x in both]
        last = 2 * covered >= blocks
        keep = wide if last else wide + rows
        moved = [
            dot3(tuple(x[top:, wide:] for x in half), tuple(x[:, :keep] for x in half))
            for half in halves
        ]
        results = [
            jnp.concatenate([x[:top, :wide], x[top:, :wide] + sign * m[:, :wide]], 0)
            for x, m in zip(both, moved)
        ]
        if last:
            return results
        empty = jnp.zeros((top, rows), F32)
        both = [
            jnp.concatenate([x, jnp.concatenate([empty, m[:, wide:]], 0)], 1)
            for x, m in zip(results, moved)
        ]
        sign, covered = 1.0, 2 * covered


def summary_kernel(size, acc_ref, rest_ref, piece_ref, strict_ref, cols_ref, grown_ref, send_ref, keys_ref, wy_ref):
    heads, rows, _ = strict_ref.shape
    last = rest_ref.shape[0] - 1
    keys = acc_ref[0] + contract(piece_ref[...], rest_ref[last, 0], NN)
    values = acc_ref[1] + contract(piece_ref[...], rest_ref[last, 1], NN)
    every = range(heads)
    each = [keys[:, h * size : (h + 1) * size] for h in every]
    scales = [lax.rsqrt(jnp.sum(key * key, -1, keepdims=True) + 1e-06) for key in each]
    each = [key * scale for key, scale in zip(each, scales)]
    halves = [split(key) for key in each]
    lowers = [dot3(halves[h], halves[h], NT) * strict_ref[h] for h in every]
    tails = [split(jnp.transpose(each[h] * cols_ref[h, 2])) for h in every]
    rights = [
        jnp.concatenate(
            [each[h] * cols_ref[h, 0], values[:, h * size : (h + 1) * size] * cols_ref[h, 1]], 1
        )
        for h in every
    ]
    solved = solve_lower(lowers, [split(right) for right in rights])
    eye = lax.broadcasted_iota(jnp.int32, (size, size), 0) == lax.broadcasted_iota(
        jnp.int32, (size, size), 1
    )
    both = [dot3(tails[h], split(solved[h])) for h in every]
    for h in every:
        step = jnp.where(eye, grown_ref[h, rows - 1 :, :], 0.0) - both[h][:, :size]
        send_ref[h, :, :size] = step.astype(BF16)
        send_ref[h, :, size:] = both[h][:, size:].astype(BF16)
        keys_ref[h] = each[h]
        wy_ref[h] = solved[h]


def apply(step, early):
    if step.dtype == BF16 and early.dtype == BF16:
        return contract(step, early, NN)
    if step.dtype == BF16:
        high, low = split(early)
        return contract(
            jnp.concatenate([step, step], 1), jnp.concatenate([high, low], 0), NN
        )
    return apply(step.astype(BF16), early)


def follow(early, late):
    size = early[0].shape[0]
    moved = [apply(late[h][:, :size], early[h]) for h in range(len(early))]
    return [moved[h] + late[h][:, size:].astype(F32) for h in range(len(early))]


def join(early, late):
    every = range(len(early))
    size = early[0].shape[0]
    both = [apply(late[h][:, :size], early[h]) for h in every]
    add = [both[h][:, size:] + late[h][:, size:].astype(F32) for h in every]
    return [jnp.concatenate([both[h][:, :size], add[h]], 1) for h in every]


def parts_of(place, own_ref, got_refs):
    refs = [own_ref, *got_refs]
    return [[refs[i ^ place][h] for h in range(own_ref.shape[0])] for i in range(len(refs))]


def total_of(parts):
    if len(parts) == 2:
        return join(*parts)
    return join(join(parts[0], parts[1]), join(parts[2], parts[3]))


def before(place, parts):
    if place:
        pair = parts[0]
        for part in parts[1:place]:
            pair = join(pair, part)
        return pair
    size = parts[0][0].shape[0]
    row = lax.broadcasted_iota(jnp.int32, (size, 2 * size), 0)
    column = lax.broadcasted_iota(jnp.int32, (size, 2 * size), 1)
    return [jnp.where(row == column, 1.0, 0.0).astype(BF16)] * len(parts[0])


def at_place(radix, place_ref, run):
    for place in range(radix):
        pl.when(place_ref[0] == place)(functools.partial(run, place))


def enter(pair, new_map_ref, new_add_ref, pmap_ref=None, padd_ref=None):
    size = new_map_ref.shape[1]
    for h in range(len(pair)):
        if pmap_ref is None:
            new_map_ref[h] = pair[h][:, :size].astype(F32)
            new_add_ref[h] = pair[h][:, size:].astype(F32)
        else:
            both = apply(pmap_ref[h], pair[h])
            new_map_ref[h] = both[:, :size]
            new_add_ref[h] = both[:, size:] + padd_ref[h]


def merge_kernel(radix, place_ref, *refs):
    got_refs, own_ref, prefix_refs = refs[: radix - 1], refs[radix - 1], refs[radix:-3]
    new_map_ref, new_add_ref, send_ref = refs[-3:]

    def run(place):
        parts = parts_of(place, own_ref, got_refs)
        total = total_of(parts)
        enter(before(place, parts), new_map_ref, new_add_ref, *prefix_refs)
        for h in range(len(total)):
            send_ref[h] = total[h].astype(BF16)

    at_place(radix, place_ref, run)


def total_kernel(radix, place_ref, upper_ref, *refs):
    got_refs, own_ref, send_ref = refs[: radix - 1], refs[radix - 1], refs[-1]
    heads, size, _ = own_ref.shape

    def run(place):
        parts = parts_of(place, own_ref, got_refs)
        add = follow([part[:, size:] for part in parts[0]], parts[1])
        if radix > 2:
            add = follow(add, join(parts[2], parts[3]))
        for h in range(heads):
            send_ref[h] = add[h].astype(BF16)

    @pl.when(upper_ref[0] == 0)
    def _():
        at_place(radix, place_ref, run)

    @pl.when(upper_ref[0] > 0)
    def _():
        send_ref[...] = jnp.zeros_like(send_ref)


def normalize(outs, gain_ref, normed_ref):
    scales = [lax.rsqrt(jnp.mean(out * out, -1, keepdims=True) + 1e-06) for out in outs]
    for h, (out, scale) in enumerate(zip(outs, scales)):
        size = out.shape[1]
        normed = out * scale * gain_ref[...]
        normed_ref[:, h * size : (h + 1) * size] = normed.astype(BF16)


def local_kernel(n_head, radix, place_ref, turn_ref, wq_hbm, tok_hbm, *refs):
    pieces, refs = refs[: n_head - 1], refs[n_head - 1 :]
    decay_ref, grown_ref, keys_ref, wy_ref, gain_ref, *refs = refs
    got_refs, own_ref, prefix_refs = refs[: radix - 1], refs[radix - 1], refs[radix:-8]
    out_ref, reach_ref, ready_ref, wq_ref, tok_ref, pmap_ref, padd_ref, sems = refs[-8:]
    heads, size, _ = padd_ref.shape
    every = range(heads)
    depth = tok_ref.shape[1]
    moves = [(tok_hbm, tok_ref)]
    moves += [
        (wq_hbm.at[block_of(place_ref[0], d, depth), :], wq_ref.at[d]) for d in range(n_head)
    ]
    copies = copy_all(moves, sems)

    def run(place):
        parts = parts_of(place, own_ref, got_refs)
        enter(before(place, parts), pmap_ref, padd_ref, *prefix_refs)

    at_place(radix, turn_ref, run)
    for copy in copies:
        copy.wait()
    queries = contract(tok_ref[...], wq_ref[0], NN)
    for d in range(1, n_head):
        queries = queries + contract(pieces[d - 1][...], wq_ref[d], NN)
    queries = [queries[:, h * size : (h + 1) * size] for h in every]
    dots = [dot3(split(queries[h]), split(keys_ref[h]), NT) * decay_ref[h] for h in every]
    both = [dot3(split(dots[h]), split(wy_ref[h])) for h in every]
    reach = [split(queries[h] * grown_ref[h] - both[h][:, :size]) for h in every]
    out = [both[h][:, size:] + dot3(reach[h], split(padd_ref[h])) for h in every]
    later = [dot3(reach[h], split(pmap_ref[h])) for h in every]
    for h in every:
        out_ref[h] = out[h]
        reach_ref[h] = jnp.concatenate(split(later[h]), 1)
    normalize(out, gain_ref, ready_ref)


def output_kernel(upper_ref, got_ref, local_ref, reach_ref, ready_ref, gain_ref, normed_ref):
    heads = got_ref.shape[0]

    @pl.when(upper_ref[0] == 0)
    def _():
        normed_ref[...] = ready_ref[...]

    @pl.when(upper_ref[0] > 0)
    def _():
        got = [jnp.concatenate([got_ref[h]] * 2, 0) for h in range(heads)]
        outs = [local_ref[h] + contract(reach_ref[h], got[h], NN) for h in range(heads)]
        normalize(outs, gain_ref, normed_ref)


def mix_own_kernel(place_ref, wo_hbm, part_ref, out_ref, weight_ref, sem):
    width = weight_ref.shape[1]
    copy = pltpu.make_async_copy(wo_hbm.at[:, block_of(place_ref[0], 0, width)], weight_ref, sem)
    copy.start()
    copy.wait()
    out_ref[...] = contract(part_ref[...], weight_ref[...], NN)


def mix_kernel(n_pieces, base_ref, *refs):
    total = base_ref[...]
    for part, weight in zip(refs[:n_pieces], refs[n_pieces : 2 * n_pieces]):
        total = total + contract(part[...], weight[...], NN)
    refs[-1][...] = total.astype(refs[-1].dtype)


def call(kernel, outs, args, scalars=0, hbm=0, scratch=()):
    vmem = pl.BlockSpec(memory_space=pltpu.VMEM)
    far = pl.BlockSpec(memory_space=pltpu.HBM)
    specs = [pl.BlockSpec(memory_space=pltpu.SMEM)] * scalars + [far] * hbm
    specs += [vmem] * (len(args) - scalars - hbm)
    args = [
        pltpu.with_memory_space_constraint(a, pltpu.HBM) if scalars <= i < scalars + hbm else a
        for i, a in enumerate(args)
    ]
    return pl.pallas_call(
        kernel,
        out_shape=outs,
        in_specs=specs,
        out_specs=[vmem] * len(outs),
        scratch_shapes=scratch,
        compiler_params=pltpu.CompilerParams(vmem_limit_bytes=16 * 1024 * 1024),
    )(*args)


def like(*shape, dtype=F32):
    return jax.ShapeDtypeStruct(shape, dtype)


def shards(n_seq, n_head, tokens, w_query, w_key, w_value, gate_codes, beta_codes, norm_gain, w_out):
    rows, depth = tokens.shape
    heads = gate_codes.shape[1]
    size = norm_gain.shape[0]
    width = w_out.shape[1] // n_head
    place = lax.axis_index("head")
    turn = lax.axis_index("seq")

    def swap(x, axis, count, d):
        return lax.ppermute(x, axis, [(i, i ^ d) for i in range(count)])

    def tie(*x):
        return lax.optimization_barrier(x)

    def spread(x, during):
        d = n_head // 2
        have = {d: swap(x, "head", n_head, d)}
        have[d], extra = tie(have[d], during)
        while d > 1:
            d //= 2
            have.update({e ^ d: swap(have[e], "head", n_head, d) for e in list(have)})
            have[d] = swap(x, "head", n_head, d)
        return [have[d] for d in range(1, n_head)], extra

    here = place.astype(jnp.int32).reshape(1)
    slice_out = like(heads * size, width, dtype=BF16)
    acc, rest, decay, strict, cols, grown, gain, *slices = call(
        functools.partial(prepare_kernel, n_head),
        [
            like(2, rows, heads * size),
            like(n_head - 1, 2, depth, heads * size, dtype=BF16),
            like(heads, rows, rows),
            like(heads, rows, rows),
            like(heads, 3, rows, size),
            like(heads, rows, size),
            like(1, size),
        ]
        + [slice_out] * (n_head - 1),
        [here, tokens, w_key, w_value, w_out, gate_codes.T, beta_codes.T, norm_gain.reshape(1, size)],
        1,
        7,
        [
            pltpu.VMEM((rows, depth), BF16),
            pltpu.VMEM((2, depth, heads * size), BF16),
            pltpu.VMEM((heads, rows), jnp.int32),
            pltpu.VMEM((heads, rows), jnp.int32),
            pltpu.SemaphoreType.DMA((3 + 3 * n_head,)),
        ],
    )
    pieces, (acc, rest) = spread(tokens, (acc, rest))
    (acc,) = call(
        functools.partial(more_kernel, n_head - 2),
        [like(2, rows, heads * size)],
        [acc, rest, *pieces[:-1]],
    )
    state = like(heads, size, size)
    state_sent = like(heads, size, size, dtype=BF16)
    pair_sent = like(heads, size, 2 * size, dtype=BF16)
    send, keys, solved = call(
        functools.partial(summary_kernel, size),
        [pair_sent, like(heads, rows, size), like(heads, rows, 2 * size)],
        [acc, rest, pieces[-1], strict, cols, grown],
    )
    send, *slices = tie(send, *slices)
    out_weights = [swap(slices[d - 1], "head", n_head, d) for d in range(1, n_head)]
    prefix = []
    d = 1
    while 2 * d < n_seq:
        radix = 4 if 4 * d < n_seq else 2
        last = 2 * radix * d >= n_seq
        if radix == 4:
            got = [swap(send, "seq", n_seq, i * d) for i in (3, 2, 1)][::-1]
        else:
            got = [swap(send, "seq", n_seq, d)]
        place_in = (turn // d) % radix
        place_in = place_in.astype(jnp.int32).reshape(1)
        merged = [place_in, *got, send, *prefix]
        d *= radix
        if last:
            upper = ((turn // d) % 2).astype(jnp.int32).reshape(1)
            (send,) = call(
                functools.partial(total_kernel, radix),
                [state_sent],
                [place_in, upper, *merged[1 : radix + 1]],
                2,
            )
        else:
            *prefix, send = call(
                functools.partial(merge_kernel, radix), [state, state, pair_sent], merged, 1
            )
    got = swap(send, "seq", n_seq, d)
    local, reach, ready = call(
        functools.partial(local_kernel, n_head, radix),
        [
            like(heads, rows, size),
            like(heads, rows, 2 * size, dtype=BF16),
            like(rows, heads * size, dtype=BF16),
        ],
        [here, merged[0], w_query, tokens, *pieces, decay, grown, keys, solved, gain, *merged[1:]],
        2,
        2,
        [
            pltpu.VMEM((n_head, depth, heads * size), BF16),
            pltpu.VMEM((rows, depth), BF16),
            pltpu.VMEM((heads, size, size), F32),
            pltpu.VMEM((heads, size, size), F32),
            pltpu.SemaphoreType.DMA((n_head + 1,)),
        ],
    )
    got, local, reach, ready = tie(got, local, reach, ready)
    (normed,) = call(
        output_kernel,
        [like(rows, heads * size, dtype=BF16)],
        [upper, got, local, reach, ready, gain],
        1,
    )
    (mixed,) = call(
        mix_own_kernel,
        [like(rows, width)],
        [here, w_out, normed],
        1,
        1,
        [pltpu.VMEM((heads * size, width), BF16), pltpu.SemaphoreType.DMA(())],
    )
    parts, mixed = spread(normed, mixed)
    (mixed,) = call(
        functools.partial(mix_kernel, n_head - 2),
        [like(rows, width)],
        [mixed, *parts[:-1], *out_weights[:-1]],
    )
    return call(
        functools.partial(mix_kernel, 1),
        [like(rows, width, dtype=BF16)],
        [mixed, parts[-1], out_weights[-1]],
    )[0]


def solution(mesh):
    n_seq, n_head = mesh.shape["seq"], mesh.shape["head"]
    return jax.shard_map(
        functools.partial(shards, n_seq, n_head),
        mesh=mesh,
        in_specs=(
            P("seq", "head"),
            P(None, "head"),
            P(None, "head"),
            P(None, "head"),
            P("seq", "head"),
            P("seq", "head"),
            P(),
            P("head", None),
        ),
        out_specs=P("seq", "head"),
        check_vma=False,
    )
```

```python
import functools
import jax
import jax.numpy as jnp
from jax import lax
from jax.experimental import pallas as pl
from jax.experimental.pallas import tpu as pltpu
from jax.sharding import PartitionSpec as P

BASE = 16
F32 = jnp.float32
BF16 = jnp.bfloat16


def split(x):
    high = x.astype(BF16)
    return high, (x - high.astype(F32)).astype(BF16)


def contract(a, b, dims):
    return lax.dot_general(a, b, (dims, ((), ())), preferred_element_type=F32)


NN = ((1,), (0,))
NT = ((1,), (1,))


def dot3(a, b, dims=NN):
    left = jnp.concatenate([a[0], a[1], a[0]], dims[0][0])
    right = jnp.concatenate([b[0], b[0], b[1]], dims[1][0])
    return contract(left, right, dims)


def gate_tables(codes, beta, decay_ref, strict_ref, cols_ref, grown_ref):
    heads, rows = codes.shape
    tok = lax.broadcasted_iota(jnp.int32, (rows, rows), 0)
    other = lax.broadcasted_iota(jnp.int32, (rows, rows), 1)
    ones = jnp.where(tok <= other, 1.0, 0.0).astype(BF16)
    sums = [
        contract(p.astype(F32).astype(BF16), ones, NN)
        for p in (codes >> 14, (codes >> 7) & 127, codes & 127)
    ]
    logs = -(sums[0] * 16384.0 + sums[1] * 128.0 + sums[2]) / 2097152.0
    beta = beta.astype(F32) / 256.0
    logs_t = jnp.transpose(logs)
    beta_t = jnp.transpose(beta)
    for h in range(heads):
        row = logs[h : h + 1, :]
        col = jnp.broadcast_to(logs_t[:, h : h + 1], (rows, rows))
        gap = col - row
        decay_ref[h] = jnp.where(tok >= other, jnp.exp(jnp.where(tok >= other, gap, 0.0)), 0.0)
        grown = jnp.exp(col)
        beta_col = jnp.broadcast_to(beta_t[:, h : h + 1], (rows, rows))
        strict_ref[h] = jnp.where(tok > other, decay_ref[h] * beta_col, 0.0)
        grown_ref[h] = grown
        cols_ref[h, 0] = beta_col * grown
        cols_ref[h, 1] = beta_col
        cols_ref[h, 2] = jnp.exp(row[:, rows - 1 :] - col)


def copy_all(moves, sems):
    copies = [pltpu.make_async_copy(a, b, sems.at[i]) for i, (a, b) in enumerate(moves)]
    for copy in copies:
        copy.start()
    return copies


def block_of(place, d, depth):
    return pl.ds(pl.multiple_of((place ^ d) * depth, depth), depth)


def out_slices(place, wo_hbm, out_refs, first):
    width = out_refs[0].shape[1]
    return [
        (wo_hbm.at[:, block_of(place, first + i, width)], ref) for i, ref in enumerate(out_refs)
    ]


def prepare_kernel(n_head, place_ref, tok_hbm, wk_hbm, wv_hbm, wo_hbm, gate_hbm, beta_hbm, gain_hbm, *refs):
    acc_ref, rest_ref, decay_ref, strict_ref, cols_ref, grown_ref, gain_ref = refs[:7]
    out_refs = refs[7:-5]
    tok_ref, own_ref, gate_ref, beta_ref, sems = refs[-5:]
    place = place_ref[0]
    depth = tok_ref.shape[1]
    weights = (wk_hbm, wv_hbm)
    moves = [(gate_hbm, gate_ref), (beta_hbm, beta_ref), (gain_hbm, gain_ref), (tok_hbm, tok_ref)]
    moves += [(w.at[block_of(place, 0, depth), :], own_ref.at[i]) for i, w in enumerate(weights)]
    moves += [
        (w.at[block_of(place, d, depth), :], rest_ref.at[d - 1, i])
        for d in range(1, n_head)
        for i, w in enumerate(weights)
    ]
    moves += out_slices(place, wo_hbm, out_refs, n_head - len(out_refs))
    copies = copy_all(moves, sems)
    copies[0].wait()
    copies[1].wait()
    gate_tables(gate_ref[...], beta_ref[...], decay_ref, strict_ref, cols_ref, grown_ref)
    for copy in copies[2:6]:
        copy.wait()
    for i in range(len(weights)):
        acc_ref[i] = contract(tok_ref[...], own_ref[i], NN)
    for copy in copies[6:]:
        copy.wait()


def more_kernel(n_pieces, acc_ref, rest_ref, *refs):
    out_ref = refs[-1]
    for i in range(acc_ref.shape[0]):
        total = acc_ref[i]
        for d in range(n_pieces):
            total = total + contract(refs[d][...], rest_ref[d, i], NN)
        out_ref[i] = total


def solve_lower(lowers, rights):
    rows = lowers[0].shape[0]
    blocks = rows // BASE
    tok = lax.broadcasted_iota(jnp.int32, (rows, rows), 0)
    other = lax.broadcasted_iota(jnp.int32, (rows, rows), 1)
    lane = lax.broadcasted_iota(jnp.int32, (BASE, rows), 1)
    sub = lax.broadcasted_iota(jnp.int32, (BASE, rows), 0)
    diagonal = []
    for lower in lowers:
        compact = jnp.zeros((BASE, rows), F32)
        for b in range(blocks):
            compact = compact + jnp.where(
                lane // BASE == b, lower[b * BASE : (b + 1) * BASE, :], 0.0
            )
        solved = jnp.where(sub == lane % BASE, 1.0, 0.0)
        for j in range(BASE - 1):
            column = jnp.take_along_axis(compact, (lane // BASE) * BASE + j, axis=1)
            solved = solved - column * solved[j : j + 1, :]
        inside = tok // BASE == other // BASE
        diagonal.append(split(jnp.where(inside, jnp.concatenate([solved] * blocks, 0), 0.0)))
    if blocks == 1:
        return [dot3(d, r) for d, r in zip(diagonal, rights)]
    wide = rights[0][0].shape[1]
    outside = tok // BASE != other // BASE
    links = [split(jnp.where(outside, lower, 0.0)) for lower in lowers]
    both = [
        dot3(d, tuple(jnp.concatenate(x, 1) for x in zip(r, link)))
        for d, r, link in zip(diagonal, rights, links)
    ]
    sign, covered = -1.0, 1
    while covered < blocks:
        top = covered * BASE
        halves = [split(x) for x in both]
        last = 2 * covered >= blocks
        keep = wide if last else wide + rows
        moved = [
            dot3(tuple(x[top:, wide:] for x in half), tuple(x[:, :keep] for x in half))
            for half in halves
        ]
        results = [
            jnp.concatenate([x[:top, :wide], x[top:, :wide] + sign * m[:, :wide]], 0)
            for x, m in zip(both, moved)
        ]
        if last:
            return results
        empty = jnp.zeros((top, rows), F32)
        both = [
            jnp.concatenate([x, jnp.concatenate([empty, m[:, wide:]], 0)], 1)
            for x, m in zip(results, moved)
        ]
        sign, covered = 1.0, 2 * covered


def summary_kernel(size, acc_ref, rest_ref, piece_ref, strict_ref, cols_ref, grown_ref, send_ref, keys_ref, wy_ref):
    heads, rows, _ = strict_ref.shape
    last = rest_ref.shape[0] - 1
    keys = acc_ref[0] + contract(piece_ref[...], rest_ref[last, 0], NN)
    values = acc_ref[1] + contract(piece_ref[...], rest_ref[last, 1], NN)
    every = range(heads)
    each = [keys[:, h * size : (h + 1) * size] for h in every]
    scales = [lax.rsqrt(jnp.sum(key * key, -1, keepdims=True) + 1e-06) for key in each]
    each = [key * scale for key, scale in zip(each, scales)]
    halves = [split(key) for key in each]
    lowers = [dot3(halves[h], halves[h], NT) * strict_ref[h] for h in every]
    tails = [split(jnp.transpose(each[h] * cols_ref[h, 2])) for h in every]
    rights = [
        jnp.concatenate(
            [each[h] * cols_ref[h, 0], values[:, h * size : (h + 1) * size] * cols_ref[h, 1]], 1
        )
        for h in every
    ]
    solved = solve_lower(lowers, [split(right) for right in rights])
    eye = lax.broadcasted_iota(jnp.int32, (size, size), 0) == lax.broadcasted_iota(
        jnp.int32, (size, size), 1
    )
    both = [dot3(tails[h], split(solved[h])) for h in every]
    for h in every:
        step = jnp.where(eye, grown_ref[h, rows - 1 :, :], 0.0) - both[h][:, :size]
        send_ref[h, :, :size] = step.astype(BF16)
        send_ref[h, :, size:] = both[h][:, size:].astype(BF16)
        keys_ref[h] = each[h]
        wy_ref[h] = solved[h]


def apply(step, early):
    if step.dtype == BF16 and early.dtype == BF16:
        return contract(step, early, NN)
    if step.dtype == BF16:
        high, low = split(early)
        return contract(
            jnp.concatenate([step, step], 1), jnp.concatenate([high, low], 0), NN
        )
    return apply(step.astype(BF16), early)


def follow(early, late):
    size = early[0].shape[0]
    moved = [apply(late[h][:, :size], early[h]) for h in range(len(early))]
    return [moved[h] + late[h][:, size:].astype(F32) for h in range(len(early))]


def join(early, late):
    every = range(len(early))
    size = early[0].shape[0]
    both = [apply(late[h][:, :size], early[h]) for h in every]
    add = [both[h][:, size:] + late[h][:, size:].astype(F32) for h in every]
    return [jnp.concatenate([both[h][:, :size], add[h]], 1) for h in every]


def parts_of(place, own_ref, got_refs):
    refs = [own_ref, *got_refs]
    return [[refs[i ^ place][h] for h in range(own_ref.shape[0])] for i in range(len(refs))]


def total_of(parts):
    if len(parts) == 2:
        return join(*parts)
    return join(join(parts[0], parts[1]), join(parts[2], parts[3]))


def before(place, parts):
    if place:
        pair = parts[0]
        for part in parts[1:place]:
            pair = join(pair, part)
        return pair
    size = parts[0][0].shape[0]
    row = lax.broadcasted_iota(jnp.int32, (size, 2 * size), 0)
    column = lax.broadcasted_iota(jnp.int32, (size, 2 * size), 1)
    return [jnp.where(row == column, 1.0, 0.0).astype(BF16)] * len(parts[0])


def at_place(radix, place_ref, run):
    for place in range(radix):
        pl.when(place_ref[0] == place)(functools.partial(run, place))


def enter(pair, new_map_ref, new_add_ref, pmap_ref=None, padd_ref=None):
    size = new_map_ref.shape[1]
    for h in range(len(pair)):
        if pmap_ref is None:
            new_map_ref[h] = pair[h][:, :size].astype(F32)
            new_add_ref[h] = pair[h][:, size:].astype(F32)
        else:
            both = apply(pmap_ref[h], pair[h])
            new_map_ref[h] = both[:, :size]
            new_add_ref[h] = both[:, size:] + padd_ref[h]


def merge_kernel(radix, place_ref, *refs):
    got_refs, own_ref, prefix_refs = refs[: radix - 1], refs[radix - 1], refs[radix:-3]
    new_map_ref, new_add_ref, send_ref = refs[-3:]

    def run(place):
        parts = parts_of(place, own_ref, got_refs)
        total = total_of(parts)
        enter(before(place, parts), new_map_ref, new_add_ref, *prefix_refs)
        for h in range(len(total)):
            send_ref[h] = total[h].astype(BF16)

    at_place(radix, place_ref, run)


def total_kernel(radix, place_ref, upper_ref, *refs):
    got_refs, own_ref, send_ref = refs[: radix - 1], refs[radix - 1], refs[-1]
    heads, size, _ = own_ref.shape

    def run(place):
        parts = parts_of(place, own_ref, got_refs)
        add = follow([part[:, size:] for part in parts[0]], parts[1])
        if radix > 2:
            add = follow([x.astype(BF16) for x in add], join(parts[2], parts[3]))
        for h in range(heads):
            send_ref[h] = add[h].astype(BF16)

    @pl.when(upper_ref[0] == 0)
    def _():
        at_place(radix, place_ref, run)

    @pl.when(upper_ref[0] > 0)
    def _():
        send_ref[...] = jnp.zeros_like(send_ref)


def normalize(outs, gain_ref, normed_ref):
    scales = [lax.rsqrt(jnp.mean(out * out, -1, keepdims=True) + 1e-06) for out in outs]
    for h, (out, scale) in enumerate(zip(outs, scales)):
        size = out.shape[1]
        normed = out * scale * gain_ref[...]
        normed_ref[:, h * size : (h + 1) * size] = normed.astype(BF16)


def local_kernel(n_head, radix, place_ref, turn_ref, wq_hbm, tok_hbm, *refs):
    pieces, refs = refs[: n_head - 1], refs[n_head - 1 :]
    decay_ref, grown_ref, keys_ref, wy_ref, gain_ref, *refs = refs
    got_refs, own_ref, prefix_refs = refs[: radix - 1], refs[radix - 1], refs[radix:-8]
    out_ref, reach_ref, ready_ref, wq_ref, tok_ref, pmap_ref, padd_ref, sems = refs[-8:]
    heads, size, _ = padd_ref.shape
    every = range(heads)
    depth = tok_ref.shape[1]
    moves = [(tok_hbm, tok_ref)]
    moves += [
        (wq_hbm.at[block_of(place_ref[0], d, depth), :], wq_ref.at[d]) for d in range(n_head)
    ]
    copies = copy_all(moves, sems)

    def run(place):
        parts = parts_of(place, own_ref, got_refs)
        enter(before(place, parts), pmap_ref, padd_ref, *prefix_refs)

    at_place(radix, turn_ref, run)
    for copy in copies:
        copy.wait()
    queries = contract(tok_ref[...], wq_ref[0], NN)
    for d in range(1, n_head):
        queries = queries + contract(pieces[d - 1][...], wq_ref[d], NN)
    queries = [queries[:, h * size : (h + 1) * size] for h in every]
    dots = [dot3(split(queries[h]), split(keys_ref[h]), NT) * decay_ref[h] for h in every]
    both = [dot3(split(dots[h]), split(wy_ref[h])) for h in every]
    reach = [split(queries[h] * grown_ref[h] - both[h][:, :size]) for h in every]
    out = [both[h][:, size:] + dot3(reach[h], split(padd_ref[h])) for h in every]
    later = [dot3(reach[h], split(pmap_ref[h])) for h in every]
    for h in every:
        out_ref[h] = out[h]
        reach_ref[h] = jnp.concatenate(split(later[h]), 1)
    normalize(out, gain_ref, ready_ref)


def output_kernel(upper_ref, got_ref, local_ref, reach_ref, ready_ref, gain_ref, normed_ref):
    heads = got_ref.shape[0]

    @pl.when(upper_ref[0] == 0)
    def _():
        normed_ref[...] = ready_ref[...]

    @pl.when(upper_ref[0] > 0)
    def _():
        got = [jnp.concatenate([got_ref[h]] * 2, 0) for h in range(heads)]
        outs = [local_ref[h] + contract(reach_ref[h], got[h], NN) for h in range(heads)]
        normalize(outs, gain_ref, normed_ref)


def mix_own_kernel(place_ref, wo_hbm, part_ref, out_ref, weight_ref, sem):
    width = weight_ref.shape[1]
    copy = pltpu.make_async_copy(wo_hbm.at[:, block_of(place_ref[0], 0, width)], weight_ref, sem)
    copy.start()
    copy.wait()
    out_ref[...] = contract(part_ref[...], weight_ref[...], NN)


def mix_kernel(n_pieces, base_ref, *refs):
    total = base_ref[...]
    for part, weight in zip(refs[:n_pieces], refs[n_pieces : 2 * n_pieces]):
        total = total + contract(part[...], weight[...], NN)
    refs[-1][...] = total.astype(refs[-1].dtype)


def call(kernel, outs, args, scalars=0, hbm=0, scratch=()):
    vmem = pl.BlockSpec(memory_space=pltpu.VMEM)
    far = pl.BlockSpec(memory_space=pltpu.HBM)
    specs = [pl.BlockSpec(memory_space=pltpu.SMEM)] * scalars + [far] * hbm
    specs += [vmem] * (len(args) - scalars - hbm)
    args = [
        pltpu.with_memory_space_constraint(a, pltpu.HBM) if scalars <= i < scalars + hbm else a
        for i, a in enumerate(args)
    ]
    return pl.pallas_call(
        kernel,
        out_shape=outs,
        in_specs=specs,
        out_specs=[vmem] * len(outs),
        scratch_shapes=scratch,
        compiler_params=pltpu.CompilerParams(vmem_limit_bytes=16 * 1024 * 1024),
    )(*args)


def like(*shape, dtype=F32):
    return jax.ShapeDtypeStruct(shape, dtype)


def shards(n_seq, n_head, tokens, w_query, w_key, w_value, gate_codes, beta_codes, norm_gain, w_out):
    rows, depth = tokens.shape
    heads = gate_codes.shape[1]
    size = norm_gain.shape[0]
    width = w_out.shape[1] // n_head
    place = lax.axis_index("head")
    turn = lax.axis_index("seq")

    def swap(x, axis, count, d):
        return lax.ppermute(x, axis, [(i, i ^ d) for i in range(count)])

    def tie(*x):
        return lax.optimization_barrier(x)

    def spread(x, during):
        d = n_head // 2
        have = {d: swap(x, "head", n_head, d)}
        have[d], extra = tie(have[d], during)
        while d > 1:
            d //= 2
            have.update({e ^ d: swap(have[e], "head", n_head, d) for e in list(have)})
            have[d] = swap(x, "head", n_head, d)
        return [have[d] for d in range(1, n_head)], extra

    here = place.astype(jnp.int32).reshape(1)
    slice_out = like(heads * size, width, dtype=BF16)
    acc, rest, decay, strict, cols, grown, gain, *slices = call(
        functools.partial(prepare_kernel, n_head),
        [
            like(2, rows, heads * size),
            like(n_head - 1, 2, depth, heads * size, dtype=BF16),
            like(heads, rows, rows),
            like(heads, rows, rows),
            like(heads, 3, rows, size),
            like(heads, rows, size),
            like(1, size),
        ]
        + [slice_out] * (n_head - 1),
        [here, tokens, w_key, w_value, w_out, gate_codes.T, beta_codes.T, norm_gain.reshape(1, size)],
        1,
        7,
        [
            pltpu.VMEM((rows, depth), BF16),
            pltpu.VMEM((2, depth, heads * size), BF16),
            pltpu.VMEM((heads, rows), jnp.int32),
            pltpu.VMEM((heads, rows), jnp.int32),
            pltpu.SemaphoreType.DMA((3 + 3 * n_head,)),
        ],
    )
    pieces, (acc, rest) = spread(tokens, (acc, rest))
    (acc,) = call(
        functools.partial(more_kernel, n_head - 2),
        [like(2, rows, heads * size)],
        [acc, rest, *pieces[:-1]],
    )
    state = like(heads, size, size)
    state_sent = like(heads, size, size, dtype=BF16)
    pair_sent = like(heads, size, 2 * size, dtype=BF16)
    send, keys, solved = call(
        functools.partial(summary_kernel, size),
        [pair_sent, like(heads, rows, size), like(heads, rows, 2 * size)],
        [acc, rest, pieces[-1], strict, cols, grown],
    )
    send, *slices = tie(send, *slices)
    out_weights = [swap(slices[d - 1], "head", n_head, d) for d in range(1, n_head)]
    prefix = []
    d = 1
    while 2 * d < n_seq:
        radix = 4 if 4 * d < n_seq else 2
        last = 2 * radix * d >= n_seq
        if radix == 4:
            got = [swap(send, "seq", n_seq, i * d) for i in (3, 2, 1)][::-1]
        else:
            got = [swap(send, "seq", n_seq, d)]
        place_in = (turn // d) % radix
        place_in = place_in.astype(jnp.int32).reshape(1)
        merged = [place_in, *got, send, *prefix]
        d *= radix
        if last:
            upper = ((turn // d) % 2).astype(jnp.int32).reshape(1)
            (send,) = call(
                functools.partial(total_kernel, radix),
                [state_sent],
                [place_in, upper, *merged[1 : radix + 1]],
                2,
            )
        else:
            *prefix, send = call(
                functools.partial(merge_kernel, radix), [state, state, pair_sent], merged, 1
            )
    got = swap(send, "seq", n_seq, d)
    local, reach, ready = call(
        functools.partial(local_kernel, n_head, radix),
        [
            like(heads, rows, size),
            like(heads, rows, 2 * size, dtype=BF16),
            like(rows, heads * size, dtype=BF16),
        ],
        [here, merged[0], w_query, tokens, *pieces, decay, grown, keys, solved, gain, *merged[1:]],
        2,
        2,
        [
            pltpu.VMEM((n_head, depth, heads * size), BF16),
            pltpu.VMEM((rows, depth), BF16),
            pltpu.VMEM((heads, size, size), F32),
            pltpu.VMEM((heads, size, size), F32),
            pltpu.SemaphoreType.DMA((n_head + 1,)),
        ],
    )
    got, local, reach, ready = tie(got, local, reach, ready)
    (normed,) = call(
        output_kernel,
        [like(rows, heads * size, dtype=BF16)],
        [upper, got, local, reach, ready, gain],
        1,
    )
    (mixed,) = call(
        mix_own_kernel,
        [like(rows, width)],
        [here, w_out, normed],
        1,
        1,
        [pltpu.VMEM((heads * size, width), BF16), pltpu.SemaphoreType.DMA(())],
    )
    parts, mixed = spread(normed, mixed)
    (mixed,) = call(
        functools.partial(mix_kernel, n_head - 2),
        [like(rows, width)],
        [mixed, *parts[:-1], *out_weights[:-1]],
    )
    return call(
        functools.partial(mix_kernel, 1),
        [like(rows, width, dtype=BF16)],
        [mixed, parts[-1], out_weights[-1]],
    )[0]


def solution(mesh):
    n_seq, n_head = mesh.shape["seq"], mesh.shape["head"]
    return jax.shard_map(
        functools.partial(shards, n_seq, n_head),
        mesh=mesh,
        in_specs=(
            P("seq", "head"),
            P(None, "head"),
            P(None, "head"),
            P(None, "head"),
            P("seq", "head"),
            P("seq", "head"),
            P(),
            P("head", None),
        ),
        out_specs=P("seq", "head"),
        check_vma=False,
    )
```
